32 devices in a mesh: row: 16 (over z, x, core), col: 2 (over y).
Axes of the slice: x: 2, y: 2, z: 4, core: 2. Of those that a mesh axis runs over, the one named last changes fastest.
Arguments:
- x0_rows: bfloat16 [4096, 32768], P('row', 'col'), may hold values from -0.1875 to 0.1875
- x1_rows: bfloat16 [4096, 32768], P('row', 'col'), may hold values from -0.1875 to 0.1875
- x0_cols: bfloat16 [32768, 1536], P('row', 'col'), may hold values from -6 to 6
- x1_cols: bfloat16 [32768, 1536], P('row', 'col'), may hold values from -6 to 6
- mask0_rows: int32 [32, 256], P('row', 'col'), may hold values 0 or 1
- mask1_rows: int32 [32, 256], P('row', 'col'), may hold values 0 or 1
- mask0_cols: int32 [256, 12], P('row', 'col'), may hold values 0 or 1
- mask1_cols: int32 [256, 12], P('row', 'col'), may hold values 0 or 1
- keep_mask: int32 [32, 12], P('row', 'col'), may hold values 0 or 1
Outputs:
- x_square: bfloat16 [4096, 1536], P('row', 'col')
- x_tangent: bfloat16 [4096, 1536], P('row', 'col')
The draws below stay inside these ranges and needn't reach their ends.
All inputs are finite; a program needn't handle non-finite values. No bound on the sum of `mask0_rows` or of `mask1_rows` or of `mask0_cols` or of `mask1_cols` or of `keep_mask` on one device may be relied on, other than what follows from the above.
Results may differ from the reference program's by a relative error of at most 0.001.
Values may be sent and summed in bfloat16 or wider, within the bound.
No kernel may reach another device: no remote copies, remote signals or barrier semaphores. Data moves between devices by JAX's collectives and lax.ppermute only.
A program may use at most 128 MiB of HBM per device.

```python
import jax
import jax.numpy as jnp

ORDER = 32768
BLOCK = 128
ROWS_DEV = 256
GROUP = 8
PANEL = 2048
WROWS = 4096
WCOLS = 1536
BLOCKS = 256
N_ROW = 16
N_COL = 2


def with_ends(entries, key, least, top_value):
    longest = entries.shape.index(max(entries.shape))
    spots = []
    for shift in (0, 1):
        where = [jax.random.randint(jax.random.fold_in(key, axis), (), 0, length) for axis, length in enumerate(entries.shape)]
        where[longest] = (where[longest] + shift) % entries.shape[longest]
        spots.append(tuple(where))
    return entries.at[spots[0]].set(least).at[spots[1]].set(top_value)


def steps_of(rng, dims, shards, smallest, largest):
    def one(position, blocks):
        heights = jax.random.uniform(jax.random.fold_in(jax.random.fold_in(rng, 6), position), (blocks,), jnp.float32, smallest / len(shards), largest / len(shards))
        return jnp.repeat(jnp.exp(heights), dims[position] // blocks).reshape((-1,) + (1,) * (len(dims) - position - 1))

    factor_of = one(*shards[0])
    for cut in shards[1:]:
        factor_of = factor_of * one(*cut)
    return factor_of


def normal_values(own_key, dims, spread, most, cuts=(), kind=jnp.bfloat16):
    level = steps_of(own_key, dims, cuts, -0.22, 0.18) if cuts else 1.0
    entries = jax.random.normal(own_key, dims, jnp.float32) * spread * level
    return jnp.minimum(jnp.maximum(entries, -most), most).astype(kind)


def setup_inputs(seed: int = 0) -> dict:
    arg_keys = jax.random.split(jax.random.key(seed), 10)
    return {
        "x0_rows": normal_values(arg_keys[0], (WROWS, ORDER), (ORDER * N_COL // (4 * N_ROW)) ** -0.5, 0.1875, ((0, 16), (1, 2))),
        "x1_rows": normal_values(arg_keys[1], (WROWS, ORDER), (ORDER * N_COL // (4 * N_ROW)) ** -0.5, 0.1875, ((0, 16), (1, 2))),
        "x0_cols": normal_values(arg_keys[2], (ORDER, WCOLS), 1.0, 6.0, ((0, 16), (1, 2))),
        "x1_cols": normal_values(arg_keys[3], (ORDER, WCOLS), 1.0, 6.0, ((0, 16), (1, 2))),
        "mask0_rows": with_ends((jax.random.randint(arg_keys[4], (WROWS // BLOCK, BLOCKS), 0, 2) < 1).astype(jnp.int32), jax.random.fold_in(arg_keys[4], 1), 0, 1),
        "mask1_rows": with_ends((jax.random.randint(arg_keys[5], (WROWS // BLOCK, BLOCKS), 0, 2) < 1).astype(jnp.int32), jax.random.fold_in(arg_keys[5], 1), 0, 1),
        "mask0_cols": with_ends((jax.random.randint(arg_keys[6], (BLOCKS, WCOLS // BLOCK), 0, 2) < 1).astype(jnp.int32), jax.random.fold_in(arg_keys[6], 1), 0, 1),
        "mask1_cols": with_ends((jax.random.randint(arg_keys[7], (BLOCKS, WCOLS // BLOCK), 0, 2) < 1).astype(jnp.int32), jax.random.fold_in(arg_keys[7], 1), 0, 1),
        "keep_mask": with_ends((jax.random.randint(arg_keys[8], (WROWS // BLOCK, WCOLS // BLOCK), 0, 4) < 3).astype(jnp.int32), jax.random.fold_in(arg_keys[8], 1), 0, 1),
    }


def masked(values, mask):
    rows_b, cols_b = mask.shape
    tiles = values.reshape(rows_b, BLOCK, cols_b, BLOCK)
    return (tiles * mask.astype(values.dtype)[:, None, :, None]).reshape(values.shape)


def pick_rows(left, which):
    shaped = left.reshape(N_COL, GROUP, ROWS_DEV, N_COL, GROUP, PANEL)
    return shaped[:, which, :, :, which, :].reshape(N_COL * ROWS_DEV, N_COL * PANEL)


def pick_cols(right, which):
    shaped = right.reshape(N_COL, GROUP, PANEL, WCOLS)
    return shaped[:, which].reshape(N_COL * PANEL, WCOLS)


def reference(x0_rows, x1_rows, x0_cols, x1_cols, mask0_rows, mask1_rows, mask0_cols, mask1_cols, keep_mask):
    left0 = masked(x0_rows, mask0_rows)
    left1 = masked(x1_rows, mask1_rows)
    right0 = masked(x0_cols, mask0_cols)
    right1 = masked(x1_cols, mask1_cols)
    squares = []
    tangents = []
    for which in range(GROUP):
        l_zero = pick_rows(left0, which)
        l_one = pick_rows(left1, which)
        r_zero = pick_cols(right0, which)
        r_one = pick_cols(right1, which)
        square = jnp.dot(l_zero, r_zero, preferred_element_type=jnp.float32)
        tangent = jnp.dot(l_zero, r_one, preferred_element_type=jnp.float32) + jnp.dot(l_one, r_zero, preferred_element_type=jnp.float32)
        squares.append(square.reshape(N_COL, ROWS_DEV, WCOLS))
        tangents.append(tangent.reshape(N_COL, ROWS_DEV, WCOLS))
    square_all = jnp.stack(squares, 1).reshape(WROWS, WCOLS)
    tangent_all = jnp.stack(tangents, 1).reshape(WROWS, WCOLS)
    x_square = masked(square_all, keep_mask).astype(jnp.bfloat16)
    x_tangent = masked(tangent_all, keep_mask).astype(jnp.bfloat16)
    return (x_square, x_tangent)
```

```python
import functools
import math

import jax
import jax.numpy as jnp
from jax import lax
from jax.experimental import pallas as pl
from jax.experimental.pallas import tpu as pltpu
from jax.sharding import PartitionSpec as P

BLOCK = 128
LEVELS = 32000.0
STEPS = 32.0
LN2 = math.log(2.0)
VMEM_BYTES = 48 * 1024 * 1024

VM = functools.partial(pl.BlockSpec, memory_space=pltpu.VMEM)
SM = functools.partial(pl.BlockSpec, memory_space=pltpu.SMEM)
HB = functools.partial(pl.BlockSpec, memory_space=pl.ANY)


def params():
    return pltpu.CompilerParams(vmem_limit_bytes=VMEM_BYTES)


def cost(flops, moved):
    return pl.CostEstimate(flops=int(flops), bytes_accessed=int(moved), transcendentals=0)


def scaled(values, entry):
    return (values.astype(jnp.float32) * entry.astype(jnp.float32)).astype(values.dtype)


def chunk_kernel(row_block, blocks, place, mask0, mask1, x0, x1, a_out, b_out):
    first = place[0] * blocks
    for j in range(blocks):
        cut = slice(j * BLOCK, (j + 1) * BLOCK)
        a_out[:, cut] = scaled(x0[:, cut], mask0[row_block, first + j])
        b_out[:, cut] = scaled(x1[:, cut], mask1[row_block, first + j])


def masked_chunk(place, mask0, mask1, x0, x1, step, rows, panel):
    blocks = panel // BLOCK
    out = jax.ShapeDtypeStruct((rows, panel), x0.dtype)
    return pl.pallas_call(
        functools.partial(chunk_kernel, step * rows // BLOCK, blocks),
        grid_spec=pltpu.PrefetchScalarGridSpec(
            num_scalar_prefetch=1,
            grid=(1,),
            in_specs=[
                SM(),
                SM(),
                pl.BlockSpec((rows, panel), lambda g, place: (step, place[0])),
                pl.BlockSpec((rows, panel), lambda g, place: (step, place[0])),
            ],
            out_specs=[
                pl.BlockSpec((rows, panel), lambda g, place: (0, 0)),
                pl.BlockSpec((rows, panel), lambda g, place: (0, 0)),
            ],
        ),
        out_shape=[out, out],
        compiler_params=params(),
        cost_estimate=cost(0, 8 * rows * panel),
        name="left_chunk",
    )(place, mask0, mask1, x0, x1)


def slab_kernel(blocks, place, mask0, mask1, x0, x1, out):
    first = place[0] * blocks
    row_block = pl.program_id(0)
    for j in range(blocks):
        cut = slice(j * BLOCK, (j + 1) * BLOCK)
        out[0, :, cut] = scaled(x0[:, cut], mask0[row_block, first + j])
        out[1, :, cut] = scaled(x1[:, cut], mask1[row_block, first + j])


def masked_slab(place, mask0, mask1, x0, x1, panel):
    rows = x0.shape[0]
    return pl.pallas_call(
        functools.partial(slab_kernel, panel // BLOCK),
        grid_spec=pltpu.PrefetchScalarGridSpec(
            num_scalar_prefetch=1,
            grid=(rows // BLOCK,),
            in_specs=[
                SM(),
                SM(),
                pl.BlockSpec((BLOCK, panel), lambda g, place: (g, place[0])),
                pl.BlockSpec((BLOCK, panel), lambda g, place: (g, place[0])),
            ],
            out_specs=pl.BlockSpec((2, BLOCK, panel), lambda g, place: (0, g, 0)),
        ),
        out_shape=jax.ShapeDtypeStruct((2, rows, panel), x0.dtype),
        compiler_params=params(),
        cost_estimate=cost(0, 8 * rows * panel),
        name="left_slab",
    )(place, mask0, mask1, x0, x1)


def right_kernel(mask0, mask1, x0, x1, out0, out1):
    step = pl.program_id(0)
    many = x0.shape[0] // BLOCK
    for i in range(many):
        for j in range(x0.shape[1] // BLOCK):
            at = (slice(i * BLOCK, (i + 1) * BLOCK), slice(j * BLOCK, (j + 1) * BLOCK))
            out0[at] = scaled(x0[at], mask0[step * many + i, j])
            out1[at] = scaled(x1[at], mask1[step * many + i, j])


def masked_right(mask0, mask1, x0, x1):
    depth, columns = x0.shape
    tall = 2 * BLOCK
    out = jax.ShapeDtypeStruct(x0.shape, x0.dtype)
    tile = pl.BlockSpec((tall, columns), lambda g: (g, 0))
    return pl.pallas_call(
        right_kernel,
        grid=(depth // tall,),
        in_specs=[SM(), SM(), tile, tile],
        out_specs=[tile, tile],
        out_shape=[out, out],
        compiler_params=params(),
        cost_estimate=cost(0, 8 * depth * columns),
        name="right_panels",
    )(mask0, mask1, x0, x1)


def both_products(held, right0, right1):
    rows = held.shape[0] // 2
    first = jnp.dot(held[...], right0[...], preferred_element_type=jnp.float32)
    second = jnp.dot(held[:rows], right1[...], preferred_element_type=jnp.float32)
    return first[:rows], first[rows:] + second


def local_kernel(diag, own, got, right0, right1, square, tangent, held):
    rows = own.shape[1]

    @pl.when((pl.program_id(0) == 0) & (diag[0] == 1))
    def _():
        held[:rows] = own[0]
        held[rows:] = own[1]

    @pl.when((pl.program_id(0) == 0) & (diag[0] == 0))
    def _():
        held[:rows] = got[0]
        held[rows:] = got[1]

    square[...], tangent[...] = both_products(held, right0, right1)


def local_products(diag, own, got, right0, right1, wide):
    rows, depth = own.shape[1:]
    columns = right0.shape[1]
    out = jax.ShapeDtypeStruct((rows, columns), jnp.float32)
    whole = pl.BlockSpec((2, rows, depth), lambda g: (0, 0, 0))
    return pl.pallas_call(
        local_kernel,
        grid=(columns // wide,),
        in_specs=[
            SM(),
            whole,
            whole,
            pl.BlockSpec((depth, wide), lambda g: (0, g)),
            pl.BlockSpec((depth, wide), lambda g: (0, g)),
        ],
        out_specs=[
            pl.BlockSpec((rows, wide), lambda g: (0, g)),
            pl.BlockSpec((rows, wide), lambda g: (0, g)),
        ],
        out_shape=[out, out],
        scratch_shapes=[pltpu.VMEM((2 * rows, depth), own.dtype)],
        compiler_params=params(),
        cost_estimate=cost(6 * rows * depth * columns, 8 * rows * depth + 4 * depth * columns),
        name="own_products",
    )(diag, own, got, right0, right1)


def partial_kernel(diag, near, far, right0, right1, out, held, steps):
    rows, wide = near.shape[0], right0.shape[1]
    step = pl.program_id(0)
    tiles = wide // BLOCK
    across = pl.num_programs(0) * tiles

    @pl.when((step == 0) & (diag[0] == 1))
    def _():
        held[:rows] = near[...]
        held[rows:] = far[...]

    @pl.when((step == 0) & (diag[0] == 0))
    def _():
        held[:rows] = far[...]
        held[rows:] = near[...]

    for which, values in enumerate(both_products(held, right0, right1)):
        top = jnp.maximum(jnp.max(jnp.abs(values), axis=0, keepdims=True), 1e-30)
        level = jnp.ceil(jnp.log(top) * (STEPS / LN2)) + 1.0
        coded = jnp.round(values * (LEVELS * jnp.exp(level * (-LN2 / STEPS))))
        coded = jnp.clip(coded, -32767.0, 32767.0).astype(jnp.int32).astype(jnp.int16)
        for t in range(tiles):
            at = which * across + step * tiles + t
            cut = slice(t * BLOCK, (t + 1) * BLOCK)
            out[pl.ds(pl.multiple_of(at * rows, rows), rows), :] = coded[:, cut]
            steps[pl.ds(at, 1), :] = level[:, cut]

    @pl.when(step == pl.num_programs(0) - 1)
    def _():
        tail = steps.shape[0]
        out[out.shape[0] - tail :, :] = steps[...].astype(jnp.int32).astype(jnp.int16)


def partial_products(diag, near, far, right0, right1, wide):
    rows, depth = near.shape
    columns = right0.shape[1]
    tiles = 2 * columns // BLOCK
    tail = -(-tiles // 16) * 16
    whole = pl.BlockSpec((rows, depth), lambda g: (0, 0))
    return pl.pallas_call(
        partial_kernel,
        grid=(columns // wide,),
        in_specs=[
            SM(),
            whole,
            whole,
            pl.BlockSpec((depth, wide), lambda g: (0, g)),
            pl.BlockSpec((depth, wide), lambda g: (0, g)),
        ],
        out_specs=pl.BlockSpec((tiles * rows + tail, BLOCK), lambda g: (0, 0)),
        out_shape=jax.ShapeDtypeStruct((tiles * rows + tail, BLOCK), jnp.int16),
        scratch_shapes=[
            pltpu.VMEM((2 * rows, depth), near.dtype),
            pltpu.VMEM((tail, BLOCK), jnp.float32),
        ],
        compiler_params=params(),
        cost_estimate=cost(6 * rows * depth * columns, 4 * rows * depth + 4 * depth * columns),
        name="partial_products",
    )(diag, near, far, right0, right1)


def finish_kernel(row_block, keep, square, tangent, coded, *rest):
    outs = rest[-2:]
    rows, columns = square.shape
    across = columns // BLOCK
    tail = coded.shape[0] - 2 * across * rows
    levels = coded[coded.shape[0] - tail :, :].astype(jnp.int32).astype(jnp.float32)
    steps = jnp.exp(levels * (LN2 / STEPS)) * (1.0 / LEVELS)
    for which, (mine, out) in enumerate(zip((square, tangent), outs)):
        for j in range(across):
            at = which * across + j
            cut = slice(j * BLOCK, (j + 1) * BLOCK)
            other = coded[at * rows : (at + 1) * rows, :].astype(jnp.int32).astype(jnp.float32)
            total = mine[:, cut] + other * steps[at : at + 1, :]
            out[:, cut] = (total * keep[row_block, j].astype(jnp.float32)).astype(out.dtype)


def finished(keep, square, tangent, coded, before, step, rows):
    all_rows, columns = square.shape
    tile = pl.BlockSpec((rows, columns), lambda g: (step, 0))
    out = jax.ShapeDtypeStruct((all_rows, columns), jnp.bfloat16)
    handed = [] if before is None else list(before)
    return pl.pallas_call(
        functools.partial(finish_kernel, step * rows // BLOCK),
        grid=(1,),
        in_specs=[SM(), tile, tile, pl.BlockSpec(coded.shape, lambda g: (0, 0))]
        + [HB() for _ in handed],
        out_specs=[tile, tile],
        out_shape=[out, out],
        input_output_aliases={4: 0, 5: 1} if handed else {},
        compiler_params=params(),
        cost_estimate=cost(0, 16 * rows * columns),
        name="finish",
    )(keep, square, tangent, coded, *handed)


def per_device_pair(
    n_row, x0_rows, x1_rows, x0_cols, x1_cols, mask0_rows, mask1_rows, mask0_cols, mask1_cols, keep
):
    n_col = 2
    group = n_row // n_col
    panel = x0_cols.shape[0]
    all_rows = x0_rows.shape[0]
    row_index = lax.axis_index("row")
    half = row_index // group
    is_diag = half == lax.axis_index("col")
    diag = is_diag.astype(jnp.int32).reshape(1)
    place = (row_index % group).astype(jnp.int32).reshape(1)
    rows = 64
    chunks = all_rows // rows
    wide = 256

    def device(h, q, c):
        return (h * group + q) * n_col + c

    spots = [(h, q, c) for h in range(2) for q in range(group) for c in range(2)]
    over_y = [(device(h, q, c), device(h, q, 1 - c)) for h, q, c in spots]
    over_z = [(device(h, q, c), device(1 - h, q, c)) for h, q, c in spots]
    to_diag = [(device(h, q, c), device(h, q, 1 - c)) for h, q, c in spots if h != c]
    from_diag = [(device(h, q, c), device(h, q, 1 - c)) for h, q, c in spots if h == c]

    def move(values, pairs):
        return lax.ppermute(values, ("row", "col"), pairs)

    parts = [
        masked_chunk(place, mask0_rows, mask1_rows, x0_rows, x1_rows, i, rows, panel)
        for i in range(chunks)
    ]
    passed = [move(b, to_diag) for _, b in parts]
    own = masked_slab(place, mask0_rows, mask1_rows, x0_rows, x1_rows, panel)
    got = move(own, from_diag)
    right0, right1 = masked_right(mask0_cols, mask1_cols, x0_cols, x1_cols)
    near = [
        move(jnp.where(is_diag, r, a), over_z) for r, (a, _) in zip(passed, parts)
    ]
    far = [move(r, over_y) for r in near]
    coded = [
        partial_products(diag, n, f, right0, right1, wide) for n, f in zip(near, far)
    ]
    back = [move(p, over_z) for p in coded]
    square, tangent = local_products(diag, own, got, right0, right1, wide)
    outs = None
    for i in range(chunks):
        outs = finished(keep, square, tangent, back[i], outs, i, rows)
    return tuple(outs)


def passed_along(shard, axis, by):
    devices = lax.axis_size(axis)
    return lax.ppermute(shard, axis, [(i, (i + by) % devices) for i in range(devices)])


def masked(values, mask):
    rows_b, cols_b = mask.shape
    tiles = values.reshape(rows_b, BLOCK, cols_b, BLOCK)
    return (tiles * mask.astype(values.dtype)[:, None, :, None]).reshape(values.shape)


def per_device(
    x0_rows, x1_rows, x0_cols, x1_cols, mask0_rows, mask1_rows, mask0_cols, mask1_cols, keep_mask
):
    n_row = lax.axis_size("row")
    n_col = lax.axis_size("col")
    group = n_row // n_col
    row_index = lax.axis_index("row")
    col_index = lax.axis_index("col")
    panel = x0_cols.shape[0]
    start = row_index % group * panel
    block_start = row_index % group * (panel // BLOCK)
    left_zero = masked(
        lax.dynamic_slice_in_dim(x0_rows, start, panel, 1),
        lax.dynamic_slice_in_dim(mask0_rows, block_start, panel // BLOCK, 1),
    )
    left_one = masked(
        lax.dynamic_slice_in_dim(x1_rows, start, panel, 1),
        lax.dynamic_slice_in_dim(mask1_rows, block_start, panel // BLOCK, 1),
    )
    right_zero = masked(x0_cols, mask0_cols)
    right_one = masked(x1_cols, mask1_cols)
    left = jnp.stack([left_zero, left_one])
    right = jnp.stack([right_zero, right_one])
    left_offset = row_index // group % n_col
    right_offset = col_index % n_col
    levels = n_col.bit_length() - 1
    for level in range(levels):
        moved_left = passed_along(left, "col", -(1 << level))
        moved_right = passed_along(right, "row", -group * (1 << level))
        left = jnp.where(left_offset // (1 << level) % 2 == 1, moved_left, left)
        right = jnp.where(right_offset // (1 << level) % 2 == 1, moved_right, right)

    def accumulate(left_now, right_now, square, tangent):
        square = square + jnp.dot(left_now[0], right_now[0], preferred_element_type=jnp.float32)
        tangent = tangent + jnp.dot(left_now[0], right_now[1], preferred_element_type=jnp.float32)
        tangent = tangent + jnp.dot(left_now[1], right_now[0], preferred_element_type=jnp.float32)
        return (square, tangent)

    def section_body(section, carry):
        left_now, right_now, square, tangent = carry
        square, tangent = accumulate(left_now, right_now, square, tangent)
        left_now = passed_along(left_now, "col", -1)
        right_now = passed_along(right_now, "row", -group)
        return (left_now, right_now, square, tangent)

    zeros = jnp.zeros((left_zero.shape[0], right_zero.shape[1]), jnp.float32)
    left, right, square, tangent = lax.fori_loop(
        0, n_col - 1, section_body, (left, right, zeros, zeros)
    )
    square, tangent = accumulate(left, right, square, tangent)
    x_square = masked(square, keep_mask).astype(jnp.bfloat16)
    x_tangent = masked(tangent, keep_mask).astype(jnp.bfloat16)
    return (x_square, x_tangent)


def solution(mesh):
    if mesh.shape["col"] == 2:
        body = functools.partial(per_device_pair, mesh.shape["row"])
    else:
        body = per_device
    return jax.shard_map(
        body,
        mesh=mesh,
        in_specs=(P("row", "col"),) * 9,
        out_specs=(P("row", "col"), P("row", "col")),
        check_vma=False,
    )
```

```python
import functools
import math

import jax
import jax.numpy as jnp
from jax import lax
from jax.experimental import pallas as pl
from jax.experimental.pallas import tpu as pltpu
from jax.sharding import PartitionSpec as P

BLOCK = 128
LEVELS = 32000.0
STEPS = 32.0
LN2 = math.log(2.0)
VMEM_BYTES = 48 * 1024 * 1024

VM = functools.partial(pl.BlockSpec, memory_space=pltpu.VMEM)
SM = functools.partial(pl.BlockSpec, memory_space=pltpu.SMEM)
HB = functools.partial(pl.BlockSpec, memory_space=pl.ANY)


def params():
    return pltpu.CompilerParams(vmem_limit_bytes=VMEM_BYTES)


def cost(flops, moved):
    return pl.CostEstimate(flops=int(flops) // 64, bytes_accessed=int(moved) // 64, transcendentals=0)


def scaled(values, entry):
    return (values.astype(jnp.float32) * entry.astype(jnp.float32)).astype(values.dtype)


def row_pieces(start, rows):
    edges = sorted({start, start + rows} | {e for e in range(0, start + rows, BLOCK) if e > start})
    return [(lo // BLOCK, slice(lo - start, hi - start)) for lo, hi in zip(edges, edges[1:])]


def chunk_kernel(spans, panel, with_slab, *refs):
    place, diag, mask0, mask1, x0, x1 = refs[:6]
    held, sems = refs[-2:]
    many = 2 * len(spans) + with_slab
    outs = refs[-2 - many : -2]
    slab = outs[-1] if with_slab else None
    blocks = panel // BLOCK
    first = place[0] * blocks
    at = pl.ds(pl.multiple_of(place[0] * panel, BLOCK), panel)
    origin = 0 if with_slab else spans[0][0]
    copies = []
    for n, (lo, hi) in enumerate(spans):
        lo = origin if n == 0 else lo
        for i, x in enumerate((x0, x1)):
            here = pl.ds(lo - origin, hi - lo)
            copies.append(
                pltpu.make_async_copy(x.at[pl.ds(lo, hi - lo), at], held.at[i, here], sems.at[n, i])
            )
    for copy in copies:
        copy.start()
    for n, (lo, hi) in enumerate(spans):
        a_out, swap = outs[2 * n], outs[2 * n + 1]
        copies[2 * n].wait()
        copies[2 * n + 1].wait()
        if with_slab:
            top = origin if n == 0 else lo
            for row_block, piece in row_pieces(top, hi - top):
                rows = slice(piece.start + top, piece.stop + top)
                for j in range(blocks):
                    cut = slice(j * BLOCK, (j + 1) * BLOCK)
                    slab[rows, cut] = scaled(held[1, rows, cut], mask1[row_block, first + j])
        for row_block, piece in row_pieces(lo, hi - lo):
            rows = slice(piece.start + lo - origin, piece.stop + lo - origin)
            for j in range(blocks):
                cut = slice(j * BLOCK, (j + 1) * BLOCK)
                a_out[piece, cut] = scaled(held[0, rows, cut], mask0[row_block, first + j])
            if not with_slab:
                for j in range(blocks):
                    cut = slice(j * BLOCK, (j + 1) * BLOCK)
                    swap[piece, cut] = scaled(held[1, rows, cut], mask1[row_block, first + j])

        @pl.when(diag[0] == 1)
        def _():
            swap[...] = a_out[...]

        if with_slab:

            @pl.when(diag[0] == 0)
            def _():
                swap[...] = slab[lo:hi]


def masked_chunks(place, diag, mask0, mask1, x0, x1, spans, panel, with_slab, after=()):
    outs = []
    for lo, hi in spans:
        outs += [jax.ShapeDtypeStruct((hi - lo, panel), x0.dtype)] * 2
    high = spans[-1][1] - (0 if with_slab else spans[0][0])
    if with_slab:
        outs.append(jax.ShapeDtypeStruct((spans[-1][1], panel), x0.dtype))
    return pl.pallas_call(
        functools.partial(chunk_kernel, spans, panel, with_slab),
        in_specs=[SM(), SM(), SM(), SM(), HB(), HB()] + [HB() for _ in after],
        out_specs=[VM() for _ in outs],
        out_shape=outs,
        scratch_shapes=[
            pltpu.VMEM((2, high, panel), x0.dtype),
            pltpu.SemaphoreType.DMA((len(spans), 2)),
        ],
        compiler_params=params(),
        cost_estimate=cost(0, 8 * high * panel),
        name="left_chunks",
    )(place, diag, mask0, mask1, x0, x1, *after)


def choose_kernel(many, diag, one, other, *refs):
    held, outs, sems = refs[:many], refs[-many - 2 : -1], refs[-1]
    others = [
        pltpu.make_async_copy(x, out, sems.at[1 + i])
        for i, (x, out) in enumerate(zip(held, outs[1:]))
    ]
    for copy in others:
        copy.start()

    @pl.when(diag[0] == 1)
    def _():
        copy = pltpu.make_async_copy(one, outs[0], sems.at[0])
        copy.start()
        copy.wait()

    @pl.when(diag[0] == 0)
    def _():
        copy = pltpu.make_async_copy(other, outs[0], sems.at[0])
        copy.start()
        copy.wait()

    for copy in others:
        copy.wait()


def chosen(diag, one, other, held=(), after=()):
    outs = [jax.ShapeDtypeStruct(x.shape, x.dtype) for x in (one, *held)]
    return pl.pallas_call(
        functools.partial(choose_kernel, len(held)),
        in_specs=[SM(), HB(), HB()] + [HB() for _ in (*held, *after)],
        out_specs=[HB() for _ in outs],
        out_shape=outs,
        scratch_shapes=[pltpu.SemaphoreType.DMA((len(outs),))],
        compiler_params=params(),
        cost_estimate=cost(0, 4 * one.size),
        name="to_send",
    )(diag, one, other, *held, *after)


def right_kernel(mask0, mask1, x0, x1, *rest):
    out0, out1 = rest[-2:]
    step = pl.program_id(0)
    many = x0.shape[0] // BLOCK
    for i in range(many):
        for j in range(x0.shape[1] // BLOCK):
            at = (slice(i * BLOCK, (i + 1) * BLOCK), slice(j * BLOCK, (j + 1) * BLOCK))
            out0[at] = scaled(x0[at], mask0[step * many + i, j])
            out1[at] = scaled(x1[at], mask1[step * many + i, j])


def masked_right(mask0, mask1, x0, x1, after=()):
    depth, columns = x0.shape
    tall = 2 * BLOCK
    out = jax.ShapeDtypeStruct(x0.shape, x0.dtype)
    tile = pl.BlockSpec((tall, columns), lambda g: (g, 0))
    return pl.pallas_call(
        right_kernel,
        grid=(depth // tall,),
        in_specs=[SM(), SM(), tile, tile] + [HB() for _ in after],
        out_specs=[tile, tile],
        out_shape=[out, out],
        compiler_params=params(),
        cost_estimate=cost(0, 8 * depth * columns),
        name="right_panels",
    )(mask0, mask1, x0, x1, *after)


def both_products(held, right0, right1):
    rows = held.shape[0] // 2
    first = jnp.dot(held[...], right0[...], preferred_element_type=jnp.float32)
    second = jnp.dot(held[:rows], right1[...], preferred_element_type=jnp.float32)
    return first[:rows], first[rows:] + second


def fetched(pieces, held, sems):
    copies = []
    top = 0
    for i, piece in enumerate(pieces):
        rows = piece.shape[0]
        copies.append(pltpu.make_async_copy(piece, held.at[pl.ds(top, rows)], sems.at[i]))
        top += rows
    for copy in copies:
        copy.start()
    for copy in copies:
        copy.wait()


def fetch_left(diag, one, other, held, sems):
    first = pl.program_id(0) == 0

    @pl.when(first & (diag[0] == 1))
    def _():
        fetched(one, held, sems)

    @pl.when(first & (diag[0] == 0))
    def _():
        fetched(other, held, sems)


def local_kernel(many, diag, right0, right1, *refs):
    own, got = refs[: many + 1], refs[many + 1 : 2 * many + 2]
    square, tangent, held, sems = refs[-4:]
    fetch_left(diag, own, got, held, sems)
    square[...], tangent[...] = both_products(held, right0, right1)


def local_products(diag, own, got, right0, right1, wide, after=()):
    rows, depth = own[-1].shape
    columns = right0.shape[1]
    many = len(own) - 1
    out = jax.ShapeDtypeStruct((rows, columns), jnp.float32)
    tile = pl.BlockSpec((rows, wide), lambda g: (0, g))
    return pl.pallas_call(
        functools.partial(local_kernel, many),
        grid=(columns // wide,),
        in_specs=[
            SM(),
            pl.BlockSpec((depth, wide), lambda g: (0, g)),
            pl.BlockSpec((depth, wide), lambda g: (0, g)),
        ]
        + [HB() for _ in (*own, *got, *after)],
        out_specs=[tile, tile],
        out_shape=[out, out],
        scratch_shapes=[
            pltpu.VMEM((2 * rows, depth), own[-1].dtype),
            pltpu.SemaphoreType.DMA((many + 1,)),
        ],
        compiler_params=params(),
        cost_estimate=cost(6 * rows * depth * columns, 8 * rows * depth + 4 * depth * columns),
        name="own_products",
    )(diag, right0, right1, *own, *got, *after)


def partial_kernel(diag, right0, right1, near, far, *refs):
    out, held, steps, sems = refs[-4:]
    rows, wide = near.shape[0], right0.shape[1]
    step = pl.program_id(0)
    tiles = wide // BLOCK
    across = pl.num_programs(0) * tiles
    fetch_left(diag, (near, far), (far, near), held, sems)
    for which, values in enumerate(both_products(held, right0, right1)):
        top = jnp.maximum(jnp.max(jnp.abs(values), axis=0, keepdims=True), 1e-30)
        level = jnp.ceil(jnp.log(top) * (STEPS / LN2)) + 1.0
        coded = jnp.round(values * (LEVELS * jnp.exp(level * (-LN2 / STEPS))))
        coded = jnp.clip(coded, -32767.0, 32767.0).astype(jnp.int32).astype(jnp.int16)
        for t in range(tiles):
            at = which * across + step * tiles + t
            cut = slice(t * BLOCK, (t + 1) * BLOCK)
            out[pl.ds(pl.multiple_of(at * rows, rows), rows), :] = coded[:, cut]
            steps[pl.ds(at, 1), :] = level[:, cut]

    @pl.when(step == pl.num_programs(0) - 1)
    def _():
        tail = steps.shape[0]
        out[out.shape[0] - tail :, :] = steps[...].astype(jnp.int32).astype(jnp.int16)


def partial_products(diag, near, far, right0, right1, wide, after=()):
    rows, depth = near.shape
    columns = right0.shape[1]
    tiles = 2 * columns // BLOCK
    tail = -(-tiles // 16) * 16
    return pl.pallas_call(
        partial_kernel,
        grid=(columns // wide,),
        in_specs=[
            SM(),
            pl.BlockSpec((depth, wide), lambda g: (0, g)),
            pl.BlockSpec((depth, wide), lambda g: (0, g)),
            HB(),
            HB(),
        ]
        + [HB() for _ in after],
        out_specs=pl.BlockSpec((tiles * rows + tail, BLOCK), lambda g: (0, 0)),
        out_shape=jax.ShapeDtypeStruct((tiles * rows + tail, BLOCK), jnp.int16),
        scratch_shapes=[
            pltpu.VMEM((2 * rows, depth), near.dtype),
            pltpu.VMEM((tail, BLOCK), jnp.float32),
            pltpu.SemaphoreType.DMA((2,)),
        ],
        compiler_params=params(),
        cost_estimate=cost(6 * rows * depth * columns, 4 * rows * depth + 4 * depth * columns),
        name="partial_products",
    )(diag, right0, right1, near, far, *after)


def finish_kernel(start, keep, coded, square, tangent, *rest):
    out0, out1, mine, made, in_sems, out_sems = rest[-6:]
    rows, columns = mine.shape[1:]
    across = columns // BLOCK
    at = pl.ds(start, rows)
    arrivals = [
        pltpu.make_async_copy(x.at[at], mine.at[i], in_sems.at[i])
        for i, x in enumerate((square, tangent))
    ]
    results = [
        pltpu.make_async_copy(made.at[i], x.at[at], out_sems.at[i])
        for i, x in enumerate((out0, out1))
    ]
    for copy in arrivals:
        copy.start()
    tail = coded.shape[0] - 2 * across * rows
    levels = coded[coded.shape[0] - tail :, :].astype(jnp.int32).astype(jnp.float32)
    steps = jnp.exp(levels * (LN2 / STEPS)) * (1.0 / LEVELS)
    for which in range(2):
        arrivals[which].wait()
        for j in range(across):
            tile = which * across + j
            cut = slice(j * BLOCK, (j + 1) * BLOCK)
            other = coded[tile * rows : (tile + 1) * rows, :].astype(jnp.int32).astype(jnp.float32)
            total = mine[which, :, cut] + other * steps[tile : tile + 1, :]
            for row_block, piece in row_pieces(start, rows):
                kept = total[piece] * keep[row_block, j].astype(jnp.float32)
                made[which, piece, cut] = kept.astype(made.dtype)
        results[which].start()
    for copy in results:
        copy.wait()


def finished(keep, square, tangent, coded, before, start, stop):
    rows = stop - start
    columns = square.shape[1]
    out = jax.ShapeDtypeStruct(square.shape, jnp.bfloat16)
    handed = [] if before is None else list(before)
    return pl.pallas_call(
        functools.partial(finish_kernel, start),
        in_specs=[SM(), VM(), HB(), HB()] + [HB() for _ in handed],
        out_specs=[HB(), HB()],
        out_shape=[out, out],
        input_output_aliases={4: 0, 5: 1} if handed else {},
        scratch_shapes=[
            pltpu.VMEM((2, rows, columns), jnp.float32),
            pltpu.VMEM((2, rows, columns), jnp.bfloat16),
            pltpu.SemaphoreType.DMA((2,)),
            pltpu.SemaphoreType.DMA((2,)),
        ],
        compiler_params=params(),
        cost_estimate=cost(0, 16 * rows * columns),
        name="finish",
    )(keep, coded, square, tangent, *handed)


def per_device_pair(
    n_row, x0_rows, x1_rows, x0_cols, x1_cols, mask0_rows, mask1_rows, mask0_cols, mask1_cols, keep
):
    n_col = 2
    group = n_row // n_col
    panel = x0_cols.shape[0]
    all_rows = x0_rows.shape[0]
    row_index = lax.axis_index("row")
    half = row_index // group
    diag = (half == lax.axis_index("col")).astype(jnp.int32).reshape(1)
    place = (row_index % group).astype(jnp.int32).reshape(1)
    edges = [all_rows * e // 8 for e in (0, 2, 4, 6, 8)]
    spans = list(zip(edges, edges[1:]))
    wide = 256

    def device(h, q, c):
        return (h * group + q) * n_col + c

    spots = [(h, q, c) for h in range(2) for q in range(group) for c in range(2)]
    over_y = [(device(h, q, c), device(h, q, 1 - c)) for h, q, c in spots]
    over_z = [(device(h, q, c), device(1 - h, q, c)) for h, q, c in spots]

    def move(values, pairs):
        return lax.ppermute(values, ("row", "col"), pairs)

    def chunks(spans, with_slab, after=()):
        return masked_chunks(
            place, diag, mask0_rows, mask1_rows, x0_rows, x1_rows, spans, panel, with_slab, after
        )

    def product(i, after=()):
        return partial_products(diag, near[i], far[i], right0, right1, wide, after)

    many = len(spans)
    a, swap, passed, near, far, coded, back = ([None] * many for _ in range(7))
    a[0], swap[0] = chunks(spans[:1], False)
    *rest, own_b = chunks(spans[1:], True, (swap[0],))
    a[1:], swap[1:] = rest[0::2], rest[1::2]
    right0 = right1 = square = tangent = got_b = outs = None
    for i in range(many):
        passed[i] = move(swap[i], over_y)
        gate = [near[i - 1]] if i else []
        if i == 1:
            gate.append(right0)
        if i >= 2:
            gate.append(coded[i - 2])
        if i == many - 1:
            square, tangent = local_products(
                diag, (*a, own_b), (*passed, got_b), right0, right1, wide, (coded[0],)
            )
            outs = finished(keep, square, tangent, back[0], None, *spans[0])
            gate.append(outs[0])
        held = swap[i + 1 : i + 2] + ([own_b] if i == 1 else [])
        send, *held = chosen(diag, passed[i], a[i], held, gate)
        if i < many - 1:
            swap[i + 1] = held[0]
        near[i] = move(send, over_z)
        if i == 0:
            right0, right1 = masked_right(mask0_cols, mask1_cols, x0_cols, x1_cols, (send,))
        if i == 1:
            own_b = held[1]
            got_b = move(own_b, over_y)
        if i >= 1:
            far[i - 1] = move(near[i - 1], over_y)
            coded[i - 1] = product(i - 1)
            back[i - 1] = move(coded[i - 1], over_z)
    outs = finished(keep, square, tangent, back[1], outs, *spans[1])
    far[many - 1] = move(near[many - 1], over_y)
    coded[many - 1] = product(many - 1, (coded[many - 2], outs[0]))
    back[many - 1] = move(coded[many - 1], over_z)
    for i in range(2, many):
        outs = finished(keep, square, tangent, back[i], outs, *spans[i])
    return tuple(outs)


def passed_along(shard, axis, by):
    devices = lax.axis_size(axis)
    return lax.ppermute(shard, axis, [(i, (i + by) % devices) for i in range(devices)])


def masked(values, mask):
    rows_b, cols_b = mask.shape
    tiles = values.reshape(rows_b, BLOCK, cols_b, BLOCK)
    return (tiles * mask.astype(values.dtype)[:, None, :, None]).reshape(values.shape)


def per_device(
    x0_rows, x1_rows, x0_cols, x1_cols, mask0_rows, mask1_rows, mask0_cols, mask1_cols, keep_mask
):
    n_row = lax.axis_size("row")
    n_col = lax.axis_size("col")
    group = n_row // n_col
    row_index = lax.axis_index("row")
    col_index = lax.axis_index("col")
    panel = x0_cols.shape[0]
    start = row_index % group * panel
    block_start = row_index % group * (panel // BLOCK)
    left_zero = masked(
        lax.dynamic_slice_in_dim(x0_rows, start, panel, 1),
        lax.dynamic_slice_in_dim(mask0_rows, block_start, panel // BLOCK, 1),
    )
    left_one = masked(
        lax.dynamic_slice_in_dim(x1_rows, start, panel, 1),
        lax.dynamic_slice_in_dim(mask1_rows, block_start, panel // BLOCK, 1),
    )
    right_zero = masked(x0_cols, mask0_cols)
    right_one = masked(x1_cols, mask1_cols)
    left = jnp.stack([left_zero, left_one])
    right = jnp.stack([right_zero, right_one])
    left_offset = row_index // group % n_col
    right_offset = col_index % n_col
    levels = n_col.bit_length() - 1
    for level in range(levels):
        moved_left = passed_along(left, "col", -(1 << level))
        moved_right = passed_along(right, "row", -group * (1 << level))
        left = jnp.where(left_offset // (1 << level) % 2 == 1, moved_left, left)
        right = jnp.where(right_offset // (1 << level) % 2 == 1, moved_right, right)

    def accumulate(left_now, right_now, square, tangent):
        square = square + jnp.dot(left_now[0], right_now[0], preferred_element_type=jnp.float32)
        tangent = tangent + jnp.dot(left_now[0], right_now[1], preferred_element_type=jnp.float32)
        tangent = tangent + jnp.dot(left_now[1], right_now[0], preferred_element_type=jnp.float32)
        return (square, tangent)

    def section_body(section, carry):
        left_now, right_now, square, tangent = carry
        square, tangent = accumulate(left_now, right_now, square, tangent)
        left_now = passed_along(left_now, "col", -1)
        right_now = passed_along(right_now, "row", -group)
        return (left_now, right_now, square, tangent)

    zeros = jnp.zeros((left_zero.shape[0], right_zero.shape[1]), jnp.float32)
    left, right, square, tangent = lax.fori_loop(
        0, n_col - 1, section_body, (left, right, zeros, zeros)
    )
    square, tangent = accumulate(left, right, square, tangent)
    x_square = masked(square, keep_mask).astype(jnp.bfloat16)
    x_tangent = masked(tangent, keep_mask).astype(jnp.bfloat16)
    return (x_square, x_tangent)


def solution(mesh):
    if mesh.shape["col"] == 2:
        body = functools.partial(per_device_pair, mesh.shape["row"])
    else:
        body = per_device
    return jax.shard_map(
        body,
        mesh=mesh,
        in_specs=(P("row", "col"),) * 9,
        out_specs=(P("row", "col"), P("row", "col")),
        check_vma=False,
    )
```

```python
import functools
import math

import jax
import jax.numpy as jnp
from jax import lax
from jax.experimental import pallas as pl
from jax.experimental.pallas import tpu as pltpu
from jax.sharding import PartitionSpec as P

BLOCK = 128
LEVELS = 32000.0
STEPS = 32.0
LN2 = math.log(2.0)
VMEM_BYTES = 48 * 1024 * 1024

VM = functools.partial(pl.BlockSpec, memory_space=pltpu.VMEM)
SM = functools.partial(pl.BlockSpec, memory_space=pltpu.SMEM)
HB = functools.partial(pl.BlockSpec, memory_space=pl.ANY)


def params():
    return pltpu.CompilerParams(vmem_limit_bytes=VMEM_BYTES)


def cost(flops, moved):
    return pl.CostEstimate(flops=int(flops) // 64, bytes_accessed=int(moved) // 64, transcendentals=0)


def scaled(values, entry):
    return (values.astype(jnp.float32) * entry.astype(jnp.float32)).astype(values.dtype)


def row_pieces(start, rows):
    edges = sorted({start, start + rows} | {e for e in range(0, start + rows, BLOCK) if e > start})
    return [(lo // BLOCK, slice(lo - start, hi - start)) for lo, hi in zip(edges, edges[1:])]


def chunk_kernel(spans, slabs, panel, *refs):
    place, diag, mask0, mask1, x0, x1 = refs[:6]
    held, sems = refs[-2:]
    many = 2 * len(spans) + len(slabs)
    outs = refs[-2 - many : -2]
    with_slab = len(slabs) > 0
    blocks = panel // BLOCK
    first = place[0] * blocks
    at = pl.ds(pl.multiple_of(place[0] * panel, BLOCK), panel)
    origin = 0 if with_slab else spans[0][0]
    copies = []
    for n, (lo, hi) in enumerate(spans):
        lo = origin if n == 0 else lo
        for i, x in enumerate((x0, x1)):
            here = pl.ds(lo - origin, hi - lo)
            copies.append(
                pltpu.make_async_copy(x.at[pl.ds(lo, hi - lo), at], held.at[i, here], sems.at[n, i])
            )
    for copy in copies:
        copy.start()
    for copy in copies:
        copy.wait()
    for n, (lo, hi) in enumerate(slabs):
        for row_block, piece in row_pieces(lo, hi - lo):
            rows = slice(piece.start + lo, piece.stop + lo)
            for j in range(blocks):
                cut = slice(j * BLOCK, (j + 1) * BLOCK)
                product = scaled(held[1, rows, cut], mask1[row_block, first + j])
                outs[2 * len(spans) + n][piece, cut] = product
    for n, (lo, hi) in enumerate(spans):
        a_out, swap = outs[2 * n], outs[2 * n + 1]
        for row_block, piece in row_pieces(lo, hi - lo):
            rows = slice(piece.start + lo - origin, piece.stop + lo - origin)
            for j in range(blocks):
                cut = slice(j * BLOCK, (j + 1) * BLOCK)
                a_out[piece, cut] = scaled(held[0, rows, cut], mask0[row_block, first + j])

        @pl.when(diag[0] == 1)
        def _():
            swap[...] = a_out[...]

        @pl.when(diag[0] == 0)
        def _():
            for row_block, piece in row_pieces(lo, hi - lo):
                rows = slice(piece.start + lo - origin, piece.stop + lo - origin)
                for j in range(blocks):
                    cut = slice(j * BLOCK, (j + 1) * BLOCK)
                    swap[piece, cut] = scaled(held[1, rows, cut], mask1[row_block, first + j])


def masked_chunks(place, diag, mask0, mask1, x0, x1, spans, slabs, panel, after=()):
    outs = []
    for lo, hi in spans:
        outs += [jax.ShapeDtypeStruct((hi - lo, panel), x0.dtype)] * 2
    for lo, hi in slabs:
        outs.append(jax.ShapeDtypeStruct((hi - lo, panel), x0.dtype))
    high = spans[-1][1] - (0 if slabs else spans[0][0])
    return pl.pallas_call(
        functools.partial(chunk_kernel, spans, slabs, panel),
        in_specs=[SM(), SM(), SM(), SM(), HB(), HB()] + [HB() for _ in after],
        out_specs=[VM() for _ in outs],
        out_shape=outs,
        scratch_shapes=[
            pltpu.VMEM((2, high, panel), x0.dtype),
            pltpu.SemaphoreType.DMA((len(spans), 2)),
        ],
        compiler_params=params(),
        cost_estimate=cost(0, 8 * high * panel),
        name="left_chunks",
    )(place, diag, mask0, mask1, x0, x1, *after)


def choose_kernel(many, diag, one, other, *refs):
    held, outs, sems = refs[:many], refs[-many - 2 : -1], refs[-1]
    others = [
        pltpu.make_async_copy(x, out, sems.at[1 + i])
        for i, (x, out) in enumerate(zip(held, outs[1:]))
    ]
    for copy in others:
        copy.start()

    @pl.when(diag[0] == 1)
    def _():
        copy = pltpu.make_async_copy(one, outs[0], sems.at[0])
        copy.start()
        copy.wait()

    @pl.when(diag[0] == 0)
    def _():
        copy = pltpu.make_async_copy(other, outs[0], sems.at[0])
        copy.start()
        copy.wait()

    for copy in others:
        copy.wait()


def chosen(diag, one, other, held=(), after=()):
    outs = [jax.ShapeDtypeStruct(x.shape, x.dtype) for x in (one, *held)]
    return pl.pallas_call(
        functools.partial(choose_kernel, len(held)),
        in_specs=[SM(), HB(), HB()] + [HB() for _ in (*held, *after)],
        out_specs=[HB() for _ in outs],
        out_shape=outs,
        scratch_shapes=[pltpu.SemaphoreType.DMA((len(outs),))],
        compiler_params=params(),
        cost_estimate=cost(0, 4 * one.size),
        name="to_send",
    )(diag, one, other, *held, *after)


def right_kernel(mask0, mask1, x0, x1, *rest):
    out0, out1 = rest[-2:]
    step = pl.program_id(0)
    many = x0.shape[0] // BLOCK
    for i in range(many):
        for j in range(x0.shape[1] // BLOCK):
            at = (slice(i * BLOCK, (i + 1) * BLOCK), slice(j * BLOCK, (j + 1) * BLOCK))
            out0[at] = scaled(x0[at], mask0[step * many + i, j])
            out1[at] = scaled(x1[at], mask1[step * many + i, j])


def masked_right(mask0, mask1, x0, x1, after=()):
    depth, columns = x0.shape
    tall = 2 * BLOCK
    out = jax.ShapeDtypeStruct(x0.shape, x0.dtype)
    tile = pl.BlockSpec((tall, columns), lambda g: (g, 0))
    return pl.pallas_call(
        right_kernel,
        grid=(depth // tall,),
        in_specs=[SM(), SM(), tile, tile] + [HB() for _ in after],
        out_specs=[tile, tile],
        out_shape=[out, out],
        compiler_params=params(),
        cost_estimate=cost(0, 8 * depth * columns),
        name="right_panels",
    )(mask0, mask1, x0, x1, *after)


def both_products(held, right0, right1):
    rows = held.shape[0] // 2
    first = jnp.dot(held[...], right0[...], preferred_element_type=jnp.float32)
    second = jnp.dot(held[:rows], right1[...], preferred_element_type=jnp.float32)
    return first[:rows], first[rows:] + second


def fetched(pieces, held, sems):
    copies = []
    top = 0
    for i, piece in enumerate(pieces):
        rows = piece.shape[0]
        copies.append(pltpu.make_async_copy(piece, held.at[pl.ds(top, rows)], sems.at[i]))
        top += rows
    for copy in copies:
        copy.start()
    for copy in copies:
        copy.wait()


def fetch_left(diag, one, other, held, sems):
    first = pl.program_id(0) == 0

    @pl.when(first & (diag[0] == 1))
    def _():
        fetched(one, held, sems)

    @pl.when(first & (diag[0] == 0))
    def _():
        fetched(other, held, sems)


def local_kernel(many, diag, right0, right1, *refs):
    own, got = refs[:many], refs[many : 2 * many]
    square, tangent, held, sems = refs[-4:]
    fetch_left(diag, own, got, held, sems)
    square[...], tangent[...] = both_products(held, right0, right1)


def local_products(diag, own, got, right0, right1, wide, after=()):
    rows = sum(piece.shape[0] for piece in own) // 2
    depth, columns = right0.shape
    many = len(own)
    out = jax.ShapeDtypeStruct((rows, columns), jnp.float32)
    tile = pl.BlockSpec((rows, wide), lambda g: (0, g))
    return pl.pallas_call(
        functools.partial(local_kernel, many),
        grid=(columns // wide,),
        in_specs=[
            SM(),
            pl.BlockSpec((depth, wide), lambda g: (0, g)),
            pl.BlockSpec((depth, wide), lambda g: (0, g)),
        ]
        + [HB() for _ in (*own, *got, *after)],
        out_specs=[tile, tile],
        out_shape=[out, out],
        scratch_shapes=[
            pltpu.VMEM((2 * rows, depth), own[-1].dtype),
            pltpu.SemaphoreType.DMA((many,)),
        ],
        compiler_params=params(),
        cost_estimate=cost(6 * rows * depth * columns, 8 * rows * depth + 4 * depth * columns),
        name="own_products",
    )(diag, right0, right1, *own, *got, *after)


def partial_kernel(many, diag, right0, right1, *refs):
    near, far = refs[:many], refs[many : 2 * many]
    out, held, steps, sems = refs[-4:]
    rows, wide = held.shape[0] // 2, right0.shape[1]
    step = pl.program_id(0)
    tiles = wide // BLOCK
    across = pl.num_programs(0) * tiles
    fetch_left(diag, near + far, far + near, held, sems)
    for which, values in enumerate(both_products(held, right0, right1)):
        top = jnp.maximum(jnp.max(jnp.abs(values), axis=0, keepdims=True), 1e-30)
        level = jnp.ceil(jnp.log(top) * (STEPS / LN2)) + 1.0
        coded = jnp.round(values * (LEVELS * jnp.exp(level * (-LN2 / STEPS))))
        coded = jnp.clip(coded, -32767.0, 32767.0).astype(jnp.int32).astype(jnp.int16)
        for t in range(tiles):
            at = which * across + step * tiles + t
            cut = slice(t * BLOCK, (t + 1) * BLOCK)
            out[pl.ds(pl.multiple_of(at * rows, rows), rows), :] = coded[:, cut]
            steps[pl.ds(at, 1), :] = level[:, cut]

    @pl.when(step == pl.num_programs(0) - 1)
    def _():
        tail = steps.shape[0]
        out[out.shape[0] - tail :, :] = steps[...].astype(jnp.int32).astype(jnp.int16)


def partial_products(diag, near, far, right0, right1, wide, after=()):
    rows = sum(piece.shape[0] for piece in near)
    depth, columns = right0.shape
    tiles = 2 * columns // BLOCK
    tail = -(-tiles // 16) * 16
    return pl.pallas_call(
        functools.partial(partial_kernel, len(near)),
        grid=(columns // wide,),
        in_specs=[
            SM(),
            pl.BlockSpec((depth, wide), lambda g: (0, g)),
            pl.BlockSpec((depth, wide), lambda g: (0, g)),
        ]
        + [HB() for _ in (*near, *far, *after)],
        out_specs=pl.BlockSpec((tiles * rows + tail, BLOCK), lambda g: (0, 0)),
        out_shape=jax.ShapeDtypeStruct((tiles * rows + tail, BLOCK), jnp.int16),
        scratch_shapes=[
            pltpu.VMEM((2 * rows, depth), near[0].dtype),
            pltpu.VMEM((tail, BLOCK), jnp.float32),
            pltpu.SemaphoreType.DMA((2 * len(near),)),
        ],
        compiler_params=params(),
        cost_estimate=cost(6 * rows * depth * columns, 4 * rows * depth + 4 * depth * columns),
        name="partial_products",
    )(diag, right0, right1, *near, *far, *after)


def finish_kernel(start, many, keep, coded, square, tangent, *rest):
    given, outs, passed = rest[:many], rest[-5 - many : -3 - many], rest[-3 - many : -3]
    made, out_sems, sems = rest[-3:]
    rows, columns = square.shape
    across = columns // BLOCK
    others = [
        pltpu.make_async_copy(x, y, sems.at[i]) for i, (x, y) in enumerate(zip(given, passed))
    ]
    results = [
        pltpu.make_async_copy(made.at[i], x.at[pl.ds(start, rows)], out_sems.at[i])
        for i, x in enumerate(outs)
    ]
    for copy in others:
        copy.start()
    tail = coded.shape[0] - 2 * across * rows
    levels = coded[coded.shape[0] - tail :, :].astype(jnp.int32).astype(jnp.float32)
    steps = jnp.exp(levels * (LN2 / STEPS)) * (1.0 / LEVELS)
    for which, mine in enumerate((square, tangent)):
        for j in range(across):
            tile = which * across + j
            cut = slice(j * BLOCK, (j + 1) * BLOCK)
            other = coded[tile * rows : (tile + 1) * rows, :].astype(jnp.int32).astype(jnp.float32)
            total = mine[:, cut] + other * steps[tile : tile + 1, :]
            for row_block, piece in row_pieces(start, rows):
                kept = total[piece] * keep[row_block, j].astype(jnp.float32)
                made[which, piece, cut] = kept.astype(made.dtype)
        results[which].start()
    for copy in results + others:
        copy.wait()


def finished(keep, square, tangent, coded, before, start, all_rows, held=(), after=()):
    rows, columns = square.shape
    out = jax.ShapeDtypeStruct((all_rows, columns), jnp.bfloat16)
    held, before = list(held), list(before)
    passed = [jax.ShapeDtypeStruct(x.shape, x.dtype) for x in held]
    many = len(held)
    return pl.pallas_call(
        functools.partial(finish_kernel, start, many),
        in_specs=[SM(), VM(), VM(), VM()] + [HB() for _ in (*held, *before, *after)],
        out_specs=[HB() for _ in range(2 + many)],
        out_shape=[out, out] + passed,
        input_output_aliases={4 + many: 0, 5 + many: 1} if before else {},
        scratch_shapes=[
            pltpu.VMEM((2, rows, columns), jnp.bfloat16),
            pltpu.SemaphoreType.DMA((2,)),
            pltpu.SemaphoreType.DMA((max(many, 1),)),
        ],
        compiler_params=params(),
        cost_estimate=cost(0, 16 * rows * columns),
        name="finish",
    )(keep, coded, square, tangent, *held, *before, *after)


def per_device_pair(
    n_row, x0_rows, x1_rows, x0_cols, x1_cols, mask0_rows, mask1_rows, mask0_cols, mask1_cols, keep
):
    n_col = 2
    group = n_row // n_col
    panel = x0_cols.shape[0]
    all_rows = x0_rows.shape[0]
    row_index = lax.axis_index("row")
    half = row_index // group
    diag = (half == lax.axis_index("col")).astype(jnp.int32).reshape(1)
    place = (row_index % group).astype(jnp.int32).reshape(1)
    edges = [all_rows * e // 8 for e in (0, 1, 3, 5, 8)]
    spans = list(zip(edges, edges[1:]))
    many = len(spans)
    split = edges[-2]
    wide = 256

    def device(h, q, c):
        return (h * group + q) * n_col + c

    spots = [(h, q, c) for h in range(2) for q in range(group) for c in range(2)]
    over_y = [(device(h, q, c), device(h, q, 1 - c)) for h, q, c in spots]
    over_z = [(device(h, q, c), device(1 - h, q, c)) for h, q, c in spots]

    def move(values, pairs):
        return lax.ppermute(values, ("row", "col"), pairs)

    def chunks(spans, slabs, after=()):
        return masked_chunks(
            place, diag, mask0_rows, mask1_rows, x0_rows, x1_rows, spans, slabs, panel, after
        )

    def partials(which, after=()):
        return partial_products(diag, near[which], far[which], right0, right1, wide, after)

    def own(which, b, got, after=()):
        mine, other = (*a[which], b), (*passed[which], got)
        return local_products(diag, mine, other, right0, right1, wide, after)

    a, swap, passed, near, far = ([None] * many for _ in range(5))
    a[0], swap[0] = chunks(spans[:1], ())
    *rest, top_b, low_b = chunks(spans[1:], ((0, split), (split, all_rows)), (swap[0],))
    a[1:], swap[1:] = rest[0::2], rest[1::2]
    right0 = right1 = None
    for i in range(many):
        passed[i] = move(swap[i], over_y)
        last = i == many - 1
        held = (top_b,) if last else (swap[i + 1],)
        gate = {1: (near[0],), 2: (right0,), 3: (far[0], far[1])}.get(i, ())
        send, later = chosen(diag, passed[i], a[i], held, gate)
        if last:
            top_b = later
        else:
            swap[i + 1] = later
        near[i] = move(send, over_z)
        far[i] = move(near[i], over_y)
        if i == 1:
            right0, right1 = masked_right(mask0_cols, mask1_cols, x0_cols, x1_cols, (send,))
    early, late = slice(0, many - 1), slice(many - 1, many)
    back = move(partials(early), over_z)
    square, tangent = own(early, top_b, move(top_b, over_y))
    coded = partials(late)
    *outs, low_b = finished(keep, square, tangent, back, (), 0, all_rows, (low_b,), (coded,))
    back = move(coded, over_z)
    square, tangent = own(late, low_b, move(low_b, over_y))
    return tuple(finished(keep, square, tangent, back, outs, split, all_rows))


def passed_along(shard, axis, by):
    devices = lax.axis_size(axis)
    return lax.ppermute(shard, axis, [(i, (i + by) % devices) for i in range(devices)])


def masked(values, mask):
    rows_b, cols_b = mask.shape
    tiles = values.reshape(rows_b, BLOCK, cols_b, BLOCK)
    return (tiles * mask.astype(values.dtype)[:, None, :, None]).reshape(values.shape)


def per_device(
    x0_rows, x1_rows, x0_cols, x1_cols, mask0_rows, mask1_rows, mask0_cols, mask1_cols, keep_mask
):
    n_row = lax.axis_size("row")
    n_col = lax.axis_size("col")
    group = n_row // n_col
    row_index = lax.axis_index("row")
    col_index = lax.axis_index("col")
    panel = x0_cols.shape[0]
    start = row_index % group * panel
    block_start = row_index % group * (panel // BLOCK)
    left_zero = masked(
        lax.dynamic_slice_in_dim(x0_rows, start, panel, 1),
        lax.dynamic_slice_in_dim(mask0_rows, block_start, panel // BLOCK, 1),
    )
    left_one = masked(
        lax.dynamic_slice_in_dim(x1_rows, start, panel, 1),
        lax.dynamic_slice_in_dim(mask1_rows, block_start, panel // BLOCK, 1),
    )
    right_zero = masked(x0_cols, mask0_cols)
    right_one = masked(x1_cols, mask1_cols)
    left = jnp.stack([left_zero, left_one])
    right = jnp.stack([right_zero, right_one])
    left_offset = row_index // group % n_col
    right_offset = col_index % n_col
    levels = n_col.bit_length() - 1
    for level in range(levels):
        moved_left = passed_along(left, "col", -(1 << level))
        moved_right = passed_along(right, "row", -group * (1 << level))
        left = jnp.where(left_offset // (1 << level) % 2 == 1, moved_left, left)
        right = jnp.where(right_offset // (1 << level) % 2 == 1, moved_right, right)

    def accumulate(left_now, right_now, square, tangent):
        square = square + jnp.dot(left_now[0], right_now[0], preferred_element_type=jnp.float32)
        tangent = tangent + jnp.dot(left_now[0], right_now[1], preferred_element_type=jnp.float32)
        tangent = tangent + jnp.dot(left_now[1], right_now[0], preferred_element_type=jnp.float32)
        return (square, tangent)

    def section_body(section, carry):
        left_now, right_now, square, tangent = carry
        square, tangent = accumulate(left_now, right_now, square, tangent)
        left_now = passed_along(left_now, "col", -1)
        right_now = passed_along(right_now, "row", -group)
        return (left_now, right_now, square, tangent)

    zeros = jnp.zeros((left_zero.shape[0], right_zero.shape[1]), jnp.float32)
    left, right, square, tangent = lax.fori_loop(
        0, n_col - 1, section_body, (left, right, zeros, zeros)
    )
    square, tangent = accumulate(left, right, square, tangent)
    x_square = masked(square, keep_mask).astype(jnp.bfloat16)
    x_tangent = masked(tangent, keep_mask).astype(jnp.bfloat16)
    return (x_square, x_tangent)


def solution(mesh):
    if mesh.shape["col"] == 2:
        body = functools.partial(per_device_pair, mesh.shape["row"])
    else:
        body = per_device
    return jax.shard_map(
        body,
        mesh=mesh,
        in_specs=(P("row", "col"),) * 9,
        out_specs=(P("row", "col"), P("row", "col")),
        check_vma=False,
    )
```

```python
import functools
import math

import jax
import jax.numpy as jnp
from jax import lax
from jax.experimental import pallas as pl
from jax.experimental.pallas import tpu as pltpu
from jax.sharding import PartitionSpec as P

BLOCK = 128
LEVELS = 32000.0
STEPS = 32.0
LN2 = math.log(2.0)
VMEM_BYTES = 48 * 1024 * 1024

VM = functools.partial(pl.BlockSpec, memory_space=pltpu.VMEM)
SM = functools.partial(pl.BlockSpec, memory_space=pltpu.SMEM)
HB = functools.partial(pl.BlockSpec, memory_space=pl.ANY)


def params():
    return pltpu.CompilerParams(vmem_limit_bytes=VMEM_BYTES)


def cost(flops, moved, weight=1 / 64):
    return pl.CostEstimate(
        flops=int(flops * weight), bytes_accessed=int(moved * weight), transcendentals=0
    )


def scaled(values, entry):
    return (values.astype(jnp.float32) * entry.astype(jnp.float32)).astype(values.dtype)


def row_pieces(start, rows):
    edges = sorted({start, start + rows} | {e for e in range(0, start + rows, BLOCK) if e > start})
    return [(lo // BLOCK, slice(lo - start, hi - start)) for lo, hi in zip(edges, edges[1:])]


def chunk_kernel(spans, slabs, panel, *refs):
    place, diag, mask0_far, mask1_far, x0, x1 = refs[:6]
    held, mask0, mask1, mask_sems, sems = refs[-5:]
    many = 2 * len(spans) + len(slabs)
    outs = refs[-5 - many : -5]
    masks = [
        pltpu.make_async_copy(mask0_far, mask0, mask_sems.at[0]),
        pltpu.make_async_copy(mask1_far, mask1, mask_sems.at[1]),
    ]
    for copy in masks:
        copy.start()
    with_slab = len(slabs) > 0
    blocks = panel // BLOCK
    first = place[0] * blocks
    at = pl.ds(pl.multiple_of(place[0] * panel, BLOCK), panel)
    origin = 0 if with_slab else spans[0][0]
    copies = []
    for n, (lo, hi) in enumerate(spans):
        lo = origin if n == 0 else lo
        for i, x in enumerate((x0, x1)):
            here = pl.ds(lo - origin, hi - lo)
            copies.append(
                pltpu.make_async_copy(x.at[pl.ds(lo, hi - lo), at], held.at[i, here], sems.at[n, i])
            )
    for copy in copies:
        copy.start()
    for copy in masks + copies:
        copy.wait()
    for n, (lo, hi) in enumerate(slabs):
        for row_block, piece in row_pieces(lo, hi - lo):
            rows = slice(piece.start + lo, piece.stop + lo)
            for j in range(blocks):
                cut = slice(j * BLOCK, (j + 1) * BLOCK)
                product = scaled(held[1, rows, cut], mask1[row_block, first + j])
                outs[2 * len(spans) + n][piece, cut] = product
    for n, (lo, hi) in enumerate(spans):
        a_out, swap = outs[2 * n], outs[2 * n + 1]
        for row_block, piece in row_pieces(lo, hi - lo):
            rows = slice(piece.start + lo - origin, piece.stop + lo - origin)
            for j in range(blocks):
                cut = slice(j * BLOCK, (j + 1) * BLOCK)
                a_out[piece, cut] = scaled(held[0, rows, cut], mask0[row_block, first + j])

        @pl.when(diag[0] == 1)
        def _():
            swap[...] = a_out[...]

        @pl.when(diag[0] == 0)
        def _():
            for row_block, piece in row_pieces(lo, hi - lo):
                rows = slice(piece.start + lo - origin, piece.stop + lo - origin)
                for j in range(blocks):
                    cut = slice(j * BLOCK, (j + 1) * BLOCK)
                    swap[piece, cut] = scaled(held[1, rows, cut], mask1[row_block, first + j])


def masked_chunks(place, diag, mask0, mask1, x0, x1, spans, slabs, panel, after=()):
    outs = []
    for lo, hi in spans:
        outs += [jax.ShapeDtypeStruct((hi - lo, panel), x0.dtype)] * 2
    for lo, hi in slabs:
        outs.append(jax.ShapeDtypeStruct((hi - lo, panel), x0.dtype))
    high = spans[-1][1] - (0 if slabs else spans[0][0])
    return pl.pallas_call(
        functools.partial(chunk_kernel, spans, slabs, panel),
        in_specs=[SM(), SM()] + [HB() for _ in range(4 + len(after))],
        out_specs=[VM() for _ in outs],
        out_shape=outs,
        scratch_shapes=[
            pltpu.VMEM((2, high, panel), x0.dtype),
            pltpu.SMEM(mask0.shape, mask0.dtype),
            pltpu.SMEM(mask1.shape, mask1.dtype),
            pltpu.SemaphoreType.DMA((2,)),
            pltpu.SemaphoreType.DMA((len(spans), 2)),
        ],
        compiler_params=params(),
        cost_estimate=cost(0, 8 * high * panel),
        name="left_chunks",
    )(place, diag, mask0, mask1, x0, x1, *after)


def choose_kernel(gates, many, diag, *refs):
    one, other = refs[gates : gates + 2]
    held, outs, sems = refs[gates + 2 : gates + 2 + many], refs[-many - 2 : -1], refs[-1]
    others = [
        pltpu.make_async_copy(x, out, sems.at[1 + i])
        for i, (x, out) in enumerate(zip(held, outs[1:]))
    ]
    for copy in others:
        copy.start()

    @pl.when(diag[0] == 1)
    def _():
        copy = pltpu.make_async_copy(one, outs[0], sems.at[0])
        copy.start()
        copy.wait()

    @pl.when(diag[0] == 0)
    def _():
        copy = pltpu.make_async_copy(other, outs[0], sems.at[0])
        copy.start()
        copy.wait()

    for copy in others:
        copy.wait()


def chosen(diag, one, other, held=(), after=()):
    outs = [jax.ShapeDtypeStruct(x.shape, x.dtype) for x in (one, *held)]
    return pl.pallas_call(
        functools.partial(choose_kernel, len(after), len(held)),
        in_specs=[SM()] + [HB() for _ in (*after, one, other, *held)],
        out_specs=[HB() for _ in outs],
        out_shape=outs,
        scratch_shapes=[pltpu.SemaphoreType.DMA((len(outs),))],
        compiler_params=params(),
        cost_estimate=cost(0, 4 * one.size),
        name="to_send",
    )(diag, *after, one, other, *held)


def hand_kernel(one, gate, out, sem):
    copy = pltpu.make_async_copy(one, out, sem)
    copy.start()
    copy.wait()


def handed_on(one, gate):
    return pl.pallas_call(
        hand_kernel,
        in_specs=[HB(), HB()],
        out_specs=HB(),
        out_shape=jax.ShapeDtypeStruct(one.shape, one.dtype),
        scratch_shapes=[pltpu.SemaphoreType.DMA],
        compiler_params=params(),
        cost_estimate=cost(0, 4 * one.size),
        name="handed_on",
    )(one, gate)


def right_kernel(mask0, mask1, x0, x1, *rest):
    out0, out1 = rest[-2:]
    step = pl.program_id(0)
    many = x0.shape[0] // BLOCK
    for i in range(many):
        for j in range(x0.shape[1] // BLOCK):
            at = (slice(i * BLOCK, (i + 1) * BLOCK), slice(j * BLOCK, (j + 1) * BLOCK))
            out0[at] = scaled(x0[at], mask0[step * many + i, j])
            out1[at] = scaled(x1[at], mask1[step * many + i, j])


def masked_right(mask0, mask1, x0, x1, after=()):
    depth, columns = x0.shape
    tall = 2 * BLOCK
    out = jax.ShapeDtypeStruct(x0.shape, x0.dtype)
    tile = pl.BlockSpec((tall, columns), lambda g: (g, 0))
    return pl.pallas_call(
        right_kernel,
        grid=(depth // tall,),
        in_specs=[SM(), SM(), tile, tile] + [HB() for _ in after],
        out_specs=[tile, tile],
        out_shape=[out, out],
        compiler_params=params(),
        cost_estimate=cost(0, 8 * depth * columns),
        name="right_panels",
    )(mask0, mask1, x0, x1, *after)


def both_products(held, right0, right1):
    rows = held.shape[0] // 2
    first = jnp.dot(held[...], right0[...], preferred_element_type=jnp.float32)
    second = jnp.dot(held[:rows], right1[...], preferred_element_type=jnp.float32)
    return first[:rows], first[rows:] + second


def fetched(pieces, held, sems):
    copies = []
    top = 0
    for i, piece in enumerate(pieces):
        rows = piece.shape[0]
        copies.append(pltpu.make_async_copy(piece, held.at[pl.ds(top, rows)], sems.at[i]))
        top += rows
    for copy in copies:
        copy.start()
    for copy in copies:
        copy.wait()


def fetch_left(diag, one, other, held, sems):
    first = pl.program_id(0) == 0

    @pl.when(first & (diag[0] == 1))
    def _():
        fetched(one, held, sems)

    @pl.when(first & (diag[0] == 0))
    def _():
        fetched(other, held, sems)


def local_kernel(many, diag, right0, right1, *refs):
    own, got = refs[:many], refs[many : 2 * many]
    square, tangent, held, sems = refs[-4:]
    fetch_left(diag, own, got, held, sems)
    square[...], tangent[...] = both_products(held, right0, right1)


def local_products(diag, own, got, right0, right1, wide, after=()):
    rows = sum(piece.shape[0] for piece in own) // 2
    depth, columns = right0.shape
    many = len(own)
    out = jax.ShapeDtypeStruct((rows, columns), jnp.float32)
    tile = pl.BlockSpec((rows, wide), lambda g: (0, g))
    return pl.pallas_call(
        functools.partial(local_kernel, many),
        grid=(columns // wide,),
        in_specs=[
            SM(),
            pl.BlockSpec((depth, wide), lambda g: (0, g)),
            pl.BlockSpec((depth, wide), lambda g: (0, g)),
        ]
        + [HB() for _ in (*own, *got, *after)],
        out_specs=[tile, tile],
        out_shape=[out, out],
        scratch_shapes=[
            pltpu.VMEM((2 * rows, depth), own[-1].dtype),
            pltpu.SemaphoreType.DMA((many,)),
        ],
        compiler_params=params(),
        cost_estimate=cost(6 * rows * depth * columns, 8 * rows * depth + 4 * depth * columns),
        name="own_products",
    )(diag, right0, right1, *own, *got, *after)


def partial_kernel(many, given, diag, right0, right1, *refs):
    near, far = refs[:many], refs[many : 2 * many]
    out, passed = refs[-5 - given], refs[-4 - given : -4]
    held, steps, sems, hand_sems = refs[-4:]
    others = [
        pltpu.make_async_copy(x, y, hand_sems.at[i])
        for i, (x, y) in enumerate(zip(refs[2 * many : 2 * many + given], passed))
    ]

    @pl.when(pl.program_id(0) == 0)
    def _():
        for copy in others:
            copy.start()

    rows, wide = held.shape[0] // 2, right0.shape[1]
    step = pl.program_id(0)
    tiles = wide // BLOCK
    across = pl.num_programs(0) * tiles
    fetch_left(diag, near + far, far + near, held, sems)
    for which, values in enumerate(both_products(held, right0, right1)):
        top = jnp.maximum(jnp.max(jnp.abs(values), axis=0, keepdims=True), 1e-30)
        level = jnp.ceil(jnp.log(top) * (STEPS / LN2)) + 1.0
        coded = jnp.round(values * (LEVELS * jnp.exp(level * (-LN2 / STEPS))))
        coded = jnp.clip(coded, -32767.0, 32767.0).astype(jnp.int32).astype(jnp.int16)
        for t in range(tiles):
            at = which * across + step * tiles + t
            cut = slice(t * BLOCK, (t + 1) * BLOCK)
            out[pl.ds(pl.multiple_of(at * rows, rows), rows), :] = coded[:, cut]
            steps[pl.ds(at, 1), :] = level[:, cut]

    @pl.when(step == pl.num_programs(0) - 1)
    def _():
        tail = steps.shape[0]
        out[out.shape[0] - tail :, :] = steps[...].astype(jnp.int32).astype(jnp.int16)
        for copy in others:
            copy.wait()


def partial_products(diag, near, far, right0, right1, wide, given=(), weight=1 / 64):
    rows = sum(piece.shape[0] for piece in near)
    depth, columns = right0.shape
    tiles = 2 * columns // BLOCK
    tail = -(-tiles // 16) * 16
    return pl.pallas_call(
        functools.partial(partial_kernel, len(near), len(given)),
        grid=(columns // wide,),
        in_specs=[
            SM(),
            pl.BlockSpec((depth, wide), lambda g: (0, g)),
            pl.BlockSpec((depth, wide), lambda g: (0, g)),
        ]
        + [HB() for _ in (*near, *far, *given)],
        out_specs=[pl.BlockSpec((tiles * rows + tail, BLOCK), lambda g: (0, 0))]
        + [HB() for _ in given],
        out_shape=[jax.ShapeDtypeStruct((tiles * rows + tail, BLOCK), jnp.int16)]
        + [jax.ShapeDtypeStruct(x.shape, x.dtype) for x in given],
        scratch_shapes=[
            pltpu.VMEM((2 * rows, depth), near[0].dtype),
            pltpu.VMEM((tail, BLOCK), jnp.float32),
            pltpu.SemaphoreType.DMA((2 * len(near),)),
            pltpu.SemaphoreType.DMA((max(len(given), 1),)),
        ],
        compiler_params=params(),
        cost_estimate=cost(
            6 * rows * depth * columns, 4 * rows * depth + 4 * depth * columns, weight
        ),
        name="partial_products",
    )(diag, right0, right1, *near, *far, *given)


def finish_kernel(start, many, keep, coded, square, tangent, *rest):
    given, outs, passed = rest[:many], rest[-5 - many : -3 - many], rest[-3 - many : -3]
    made, out_sems, sems = rest[-3:]
    rows, columns = square.shape
    across = columns // BLOCK
    others = [
        pltpu.make_async_copy(x, y, sems.at[i]) for i, (x, y) in enumerate(zip(given, passed))
    ]
    results = [
        pltpu.make_async_copy(made.at[i], x.at[pl.ds(start, rows)], out_sems.at[i])
        for i, x in enumerate(outs)
    ]
    for copy in others:
        copy.start()
    tail = coded.shape[0] - 2 * across * rows
    levels = coded[coded.shape[0] - tail :, :].astype(jnp.int32).astype(jnp.float32)
    steps = jnp.exp(levels * (LN2 / STEPS)) * (1.0 / LEVELS)
    for which, mine in enumerate((square, tangent)):
        for j in range(across):
            tile = which * across + j
            cut = slice(j * BLOCK, (j + 1) * BLOCK)
            other = coded[tile * rows : (tile + 1) * rows, :].astype(jnp.int32).astype(jnp.float32)
            total = mine[:, cut] + other * steps[tile : tile + 1, :]
            for row_block, piece in row_pieces(start, rows):
                kept = total[piece] * keep[row_block, j].astype(jnp.float32)
                made[which, piece, cut] = kept.astype(made.dtype)
        results[which].start()
    for copy in results + others:
        copy.wait()


def finished(
    keep, square, tangent, coded, before, start, all_rows, held=(), after=(), weight=1 / 64
):
    rows, columns = square.shape
    out = jax.ShapeDtypeStruct((all_rows, columns), jnp.bfloat16)
    held, before = list(held), list(before)
    passed = [jax.ShapeDtypeStruct(x.shape, x.dtype) for x in held]
    many = len(held)
    return pl.pallas_call(
        functools.partial(finish_kernel, start, many),
        in_specs=[SM(), VM(), VM(), VM()] + [HB() for _ in (*held, *before, *after)],
        out_specs=[HB() for _ in range(2 + many)],
        out_shape=[out, out] + passed,
        input_output_aliases={4 + many: 0, 5 + many: 1} if before else {},
        scratch_shapes=[
            pltpu.VMEM((2, rows, columns), jnp.bfloat16),
            pltpu.SemaphoreType.DMA((2,)),
            pltpu.SemaphoreType.DMA((max(many, 1),)),
        ],
        compiler_params=params(),
        cost_estimate=cost(0, 16 * rows * columns, weight),
        name="finish",
    )(keep, coded, square, tangent, *held, *before, *after)


def per_device_pair(
    n_row, x0_rows, x1_rows, x0_cols, x1_cols, mask0_rows, mask1_rows, mask0_cols, mask1_cols, keep
):
    n_col = 2
    group = n_row // n_col
    panel = x0_cols.shape[0]
    all_rows = x0_rows.shape[0]
    row_index = lax.axis_index("row")
    half = row_index // group
    diag = (half == lax.axis_index("col")).astype(jnp.int32).reshape(1)
    place = (row_index % group).astype(jnp.int32).reshape(1)
    edges = [all_rows * e // 16 for e in (0, 3, 7, 13, 16)]
    spans = list(zip(edges, edges[1:]))
    many = len(spans)
    split = edges[2]
    final = all_rows * 10 // 16
    wide = 256

    def device(h, q, c):
        return (h * group + q) * n_col + c

    spots = [(h, q, c) for h in range(2) for q in range(group) for c in range(2)]
    over_y = [(device(h, q, c), device(h, q, 1 - c)) for h, q, c in spots]
    over_z = [(device(h, q, c), device(1 - h, q, c)) for h, q, c in spots]

    def move(values, pairs):
        return lax.ppermute(values, ("row", "col"), pairs)

    def chunks(spans, slabs, after=()):
        return masked_chunks(
            place, diag, mask0_rows, mask1_rows, x0_rows, x1_rows, spans, slabs, panel, after
        )

    def partials(which, given=(), **more):
        return partial_products(diag, near[which], far[which], right0, right1, wide, given, **more)

    def own(which, b, got):
        mine, other = (*a[which], *b), (*passed[which], *got)
        return local_products(diag, mine, other, right0, right1, wide)

    a, swap, passed, near, far = ([None] * many for _ in range(5))
    a[0], swap[0] = chunks(spans[:1], ())
    slabs = ((0, split), (split, final), (final, all_rows))
    *rest, b0, b1, b2 = chunks(spans[1:], slabs, (swap[0],))
    a[1:], swap[1:] = rest[0:-1:2], rest[1::2]
    early, late = slice(0, 2), slice(2, many)
    right0 = right1 = coded = None
    for i in range(many):
        passed[i] = move(swap[i], over_y)
        last = i == many - 1
        if last:
            (coded,) = partials(early)
        gate = {1: (near[0],), 2: (right0,), 3: (coded,)}.get(i, ())
        send, later = chosen(diag, passed[i], a[i], (b0 if last else swap[i + 1],), gate)
        if last:
            b0 = later
        else:
            swap[i + 1] = later
        near[i] = move(send, over_z)
        far[i] = move(near[i], over_y)
        if i == 1:
            right0, right1 = masked_right(mask0_cols, mask1_cols, x0_cols, x1_cols, (send,))
    back = move(handed_on(coded, near[-1]), over_z)
    square, tangent = own(early, (b0,), (move(b0, over_y),))
    coded, b1 = partials(late, (b1,), weight=16)
    *outs, b2 = finished(
        keep, square, tangent, back, (), 0, all_rows, (b2,), (coded,), weight=1024
    )
    back = move(coded, over_z)
    square, tangent = own(late, (b1, b2), (move(b1, over_y), move(b2, over_y)))
    return tuple(finished(keep, square, tangent, back, outs, split, all_rows))


def passed_along(shard, axis, by):
    devices = lax.axis_size(axis)
    return lax.ppermute(shard, axis, [(i, (i + by) % devices) for i in range(devices)])


def masked(values, mask):
    rows_b, cols_b = mask.shape
    tiles = values.reshape(rows_b, BLOCK, cols_b, BLOCK)
    return (tiles * mask.astype(values.dtype)[:, None, :, None]).reshape(values.shape)


def per_device(
    x0_rows, x1_rows, x0_cols, x1_cols, mask0_rows, mask1_rows, mask0_cols, mask1_cols, keep_mask
):
    n_row = lax.axis_size("row")
    n_col = lax.axis_size("col")
    group = n_row // n_col
    row_index = lax.axis_index("row")
    col_index = lax.axis_index("col")
    panel = x0_cols.shape[0]
    start = row_index % group * panel
    block_start = row_index % group * (panel // BLOCK)
    left_zero = masked(
        lax.dynamic_slice_in_dim(x0_rows, start, panel, 1),
        lax.dynamic_slice_in_dim(mask0_rows, block_start, panel // BLOCK, 1),
    )
    left_one = masked(
        lax.dynamic_slice_in_dim(x1_rows, start, panel, 1),
        lax.dynamic_slice_in_dim(mask1_rows, block_start, panel // BLOCK, 1),
    )
    right_zero = masked(x0_cols, mask0_cols)
    right_one = masked(x1_cols, mask1_cols)
    left = jnp.stack([left_zero, left_one])
    right = jnp.stack([right_zero, right_one])
    left_offset = row_index // group % n_col
    right_offset = col_index % n_col
    levels = n_col.bit_length() - 1
    for level in range(levels):
        moved_left = passed_along(left, "col", -(1 << level))
        moved_right = passed_along(right, "row", -group * (1 << level))
        left = jnp.where(left_offset // (1 << level) % 2 == 1, moved_left, left)
        right = jnp.where(right_offset // (1 << level) % 2 == 1, moved_right, right)

    def accumulate(left_now, right_now, square, tangent):
        square = square + jnp.dot(left_now[0], right_now[0], preferred_element_type=jnp.float32)
        tangent = tangent + jnp.dot(left_now[0], right_now[1], preferred_element_type=jnp.float32)
        tangent = tangent + jnp.dot(left_now[1], right_now[0], preferred_element_type=jnp.float32)
        return (square, tangent)

    def section_body(section, carry):
        left_now, right_now, square, tangent = carry
        square, tangent = accumulate(left_now, right_now, square, tangent)
        left_now = passed_along(left_now, "col", -1)
        right_now = passed_along(right_now, "row", -group)
        return (left_now, right_now, square, tangent)

    zeros = jnp.zeros((left_zero.shape[0], right_zero.shape[1]), jnp.float32)
    left, right, square, tangent = lax.fori_loop(
        0, n_col - 1, section_body, (left, right, zeros, zeros)
    )
    square, tangent = accumulate(left, right, square, tangent)
    x_square = masked(square, keep_mask).astype(jnp.bfloat16)
    x_tangent = masked(tangent, keep_mask).astype(jnp.bfloat16)
    return (x_square, x_tangent)


def solution(mesh):
    if mesh.shape["col"] == 2:
        body = functools.partial(per_device_pair, mesh.shape["row"])
    else:
        body = per_device
    return jax.shard_map(
        body,
        mesh=mesh,
        in_specs=(P("row", "col"),) * 9,
        out_specs=(P("row", "col"), P("row", "col")),
        check_vma=False,
    )
```

```python
import functools
import math

import jax
import jax.numpy as jnp
from jax import lax
from jax.experimental import pallas as pl
from jax.experimental.pallas import tpu as pltpu
from jax.sharding import PartitionSpec as P

BLOCK = 128
LEVELS = 32000.0
STEPS = 32.0
LN2 = math.log(2.0)
VMEM_BYTES = 48 * 1024 * 1024

VM = functools.partial(pl.BlockSpec, memory_space=pltpu.VMEM)
SM = functools.partial(pl.BlockSpec, memory_space=pltpu.SMEM)
HB = functools.partial(pl.BlockSpec, memory_space=pl.ANY)


def params():
    return pltpu.CompilerParams(vmem_limit_bytes=VMEM_BYTES)


def cost(flops, moved):
    return pl.CostEstimate(flops=int(flops) // 64, bytes_accessed=int(moved) // 64, transcendentals=0)


def scaled(values, entry):
    return (values.astype(jnp.float32) * entry.astype(jnp.float32)).astype(values.dtype)


def row_pieces(start, rows):
    edges = sorted({start, start + rows} | {e for e in range(0, start + rows, BLOCK) if e > start})
    return [(lo // BLOCK, slice(lo - start, hi - start)) for lo, hi in zip(edges, edges[1:])]


def chunk_kernel(spans, slabs, panel, *refs):
    place, diag, mask0_far, mask1_far, x0, x1 = refs[:6]
    held, mask0, mask1, mask_sems, sems = refs[-5:]
    many = 2 * len(spans) + len(slabs)
    outs = refs[-5 - many : -5]
    masks = [
        pltpu.make_async_copy(mask0_far, mask0, mask_sems.at[0]),
        pltpu.make_async_copy(mask1_far, mask1, mask_sems.at[1]),
    ]
    for copy in masks:
        copy.start()
    with_slab = len(slabs) > 0
    blocks = panel // BLOCK
    first = place[0] * blocks
    at = pl.ds(pl.multiple_of(place[0] * panel, BLOCK), panel)
    origin = 0 if with_slab else spans[0][0]
    copies = []
    for n, (lo, hi) in enumerate(spans):
        lo = origin if n == 0 else lo
        for i, x in enumerate((x0, x1)):
            here = pl.ds(lo - origin, hi - lo)
            copies.append(
                pltpu.make_async_copy(x.at[pl.ds(lo, hi - lo), at], held.at[i, here], sems.at[n, i])
            )
    for copy in copies:
        copy.start()
    for copy in masks + copies:
        copy.wait()
    for n, (lo, hi) in enumerate(slabs):
        for row_block, piece in row_pieces(lo, hi - lo):
            rows = slice(piece.start + lo, piece.stop + lo)
            for j in range(blocks):
                cut = slice(j * BLOCK, (j + 1) * BLOCK)
                product = scaled(held[1, rows, cut], mask1[row_block, first + j])
                outs[2 * len(spans) + n][piece, cut] = product
    for n, (lo, hi) in enumerate(spans):
        a_out, swap = outs[2 * n], outs[2 * n + 1]
        for row_block, piece in row_pieces(lo, hi - lo):
            rows = slice(piece.start + lo - origin, piece.stop + lo - origin)
            for j in range(blocks):
                cut = slice(j * BLOCK, (j + 1) * BLOCK)
                a_out[piece, cut] = scaled(held[0, rows, cut], mask0[row_block, first + j])

        @pl.when(diag[0] == 1)
        def _():
            swap[...] = a_out[...]

        @pl.when(diag[0] == 0)
        def _():
            for row_block, piece in row_pieces(lo, hi - lo):
                rows = slice(piece.start + lo - origin, piece.stop + lo - origin)
                for j in range(blocks):
                    cut = slice(j * BLOCK, (j + 1) * BLOCK)
                    swap[piece, cut] = scaled(held[1, rows, cut], mask1[row_block, first + j])


def masked_chunks(place, diag, mask0, mask1, x0, x1, spans, slabs, panel, after=()):
    outs = []
    for lo, hi in spans:
        outs += [jax.ShapeDtypeStruct((hi - lo, panel), x0.dtype)] * 2
    for lo, hi in slabs:
        outs.append(jax.ShapeDtypeStruct((hi - lo, panel), x0.dtype))
    high = spans[-1][1] - (0 if slabs else spans[0][0])
    return pl.pallas_call(
        functools.partial(chunk_kernel, spans, slabs, panel),
        in_specs=[SM(), SM()] + [HB() for _ in range(4 + len(after))],
        out_specs=[VM() for _ in outs],
        out_shape=outs,
        scratch_shapes=[
            pltpu.VMEM((2, high, panel), x0.dtype),
            pltpu.SMEM(mask0.shape, mask0.dtype),
            pltpu.SMEM(mask1.shape, mask1.dtype),
            pltpu.SemaphoreType.DMA((2,)),
            pltpu.SemaphoreType.DMA((len(spans), 2)),
        ],
        compiler_params=params(),
        cost_estimate=cost(0, 8 * high * panel),
        name="left_chunks",
    )(place, diag, mask0, mask1, x0, x1, *after)


def choose_kernel(gates, many, diag, *refs):
    one, other = refs[gates : gates + 2]
    held, outs, sems = refs[gates + 2 : gates + 2 + many], refs[-many - 2 : -1], refs[-1]
    others = [
        pltpu.make_async_copy(x, out, sems.at[1 + i])
        for i, (x, out) in enumerate(zip(held, outs[1:]))
    ]
    for copy in others:
        copy.start()

    @pl.when(diag[0] == 1)
    def _():
        copy = pltpu.make_async_copy(one, outs[0], sems.at[0])
        copy.start()
        copy.wait()

    @pl.when(diag[0] == 0)
    def _():
        copy = pltpu.make_async_copy(other, outs[0], sems.at[0])
        copy.start()
        copy.wait()

    for copy in others:
        copy.wait()


def chosen(diag, one, other, held=(), after=()):
    outs = [jax.ShapeDtypeStruct(x.shape, x.dtype) for x in (one, *held)]
    return pl.pallas_call(
        functools.partial(choose_kernel, len(after), len(held)),
        in_specs=[SM()] + [HB() for _ in (*after, one, other, *held)],
        out_specs=[HB() for _ in outs],
        out_shape=outs,
        scratch_shapes=[pltpu.SemaphoreType.DMA((len(outs),))],
        compiler_params=params(),
        cost_estimate=cost(0, 4 * one.size),
        name="to_send",
    )(diag, *after, one, other, *held)


def hand_kernel(many, *refs):
    sems = refs[-1]
    copies = [
        pltpu.make_async_copy(refs[i], refs[i - many - 1], sems.at[i]) for i in range(many)
    ]
    for copy in copies:
        copy.start()
    for copy in copies:
        copy.wait()


def handed_on(values, gates):
    outs = [jax.ShapeDtypeStruct(x.shape, x.dtype) for x in values]
    return pl.pallas_call(
        functools.partial(hand_kernel, len(values)),
        in_specs=[HB() for _ in (*values, *gates)],
        out_specs=[HB() for _ in outs],
        out_shape=outs,
        scratch_shapes=[pltpu.SemaphoreType.DMA((len(outs),))],
        compiler_params=params(),
        cost_estimate=cost(0, 4 * sum(x.size for x in values)),
        name="handed_on",
    )(*values, *gates)


def right_kernel(mask0, mask1, x0, x1, *rest):
    out0, out1 = rest[-2:]
    step = pl.program_id(0)
    many = x0.shape[0] // BLOCK
    for i in range(many):
        for j in range(x0.shape[1] // BLOCK):
            at = (slice(i * BLOCK, (i + 1) * BLOCK), slice(j * BLOCK, (j + 1) * BLOCK))
            out0[at] = scaled(x0[at], mask0[step * many + i, j])
            out1[at] = scaled(x1[at], mask1[step * many + i, j])


def masked_right(mask0, mask1, x0, x1, after=()):
    depth, columns = x0.shape
    tall = 2 * BLOCK
    out = jax.ShapeDtypeStruct(x0.shape, x0.dtype)
    tile = pl.BlockSpec((tall, columns), lambda g: (g, 0))
    return pl.pallas_call(
        right_kernel,
        grid=(depth // tall,),
        in_specs=[SM(), SM(), tile, tile] + [HB() for _ in after],
        out_specs=[tile, tile],
        out_shape=[out, out],
        compiler_params=params(),
        cost_estimate=cost(0, 8 * depth * columns),
        name="right_panels",
    )(mask0, mask1, x0, x1, *after)


def both_products(held, right0, right1):
    rows = held.shape[0] // 2
    first = jnp.dot(held[...], right0[...], preferred_element_type=jnp.float32)
    second = jnp.dot(held[:rows], right1[...], preferred_element_type=jnp.float32)
    return first[:rows], first[rows:] + second


def fetched(pieces, held, sems):
    copies = []
    top = 0
    for i, piece in enumerate(pieces):
        rows = piece.shape[0]
        copies.append(pltpu.make_async_copy(piece, held.at[pl.ds(top, rows)], sems.at[i]))
        top += rows
    for copy in copies:
        copy.start()
    for copy in copies:
        copy.wait()


def fetch_left(diag, one, other, held, sems):
    first = pl.program_id(0) == 0

    @pl.when(first & (diag[0] == 1))
    def _():
        fetched(one, held, sems)

    @pl.when(first & (diag[0] == 0))
    def _():
        fetched(other, held, sems)


def local_kernel(many, diag, right0, right1, *refs):
    own, got = refs[:many], refs[many : 2 * many]
    square, tangent, held, sems = refs[-4:]
    fetch_left(diag, own, got, held, sems)
    square[...], tangent[...] = both_products(held, right0, right1)


def local_products(diag, own, got, right0, right1, wide, after=()):
    rows = sum(piece.shape[0] for piece in own) // 2
    depth, columns = right0.shape
    many = len(own)
    out = jax.ShapeDtypeStruct((rows, columns), jnp.float32)
    tile = pl.BlockSpec((rows, wide), lambda g: (0, g))
    return pl.pallas_call(
        functools.partial(local_kernel, many),
        grid=(columns // wide,),
        in_specs=[
            SM(),
            pl.BlockSpec((depth, wide), lambda g: (0, g)),
            pl.BlockSpec((depth, wide), lambda g: (0, g)),
        ]
        + [HB() for _ in (*own, *got, *after)],
        out_specs=[tile, tile],
        out_shape=[out, out],
        scratch_shapes=[
            pltpu.VMEM((2 * rows, depth), own[-1].dtype),
            pltpu.SemaphoreType.DMA((many,)),
        ],
        compiler_params=params(),
        cost_estimate=cost(6 * rows * depth * columns, 8 * rows * depth + 4 * depth * columns),
        name="own_products",
    )(diag, right0, right1, *own, *got, *after)


def partial_kernel(many, given, diag, right0, right1, *refs):
    near, far = refs[:many], refs[many : 2 * many]
    out, passed = refs[-5 - given], refs[-4 - given : -4]
    held, steps, sems, hand_sems = refs[-4:]
    others = [
        pltpu.make_async_copy(x, y, hand_sems.at[i])
        for i, (x, y) in enumerate(zip(refs[2 * many : 2 * many + given], passed))
    ]

    @pl.when(pl.program_id(0) == 0)
    def _():
        for copy in others:
            copy.start()

    rows, wide = held.shape[0] // 2, right0.shape[1]
    step = pl.program_id(0)
    tiles = wide // BLOCK
    across = pl.num_programs(0) * tiles
    fetch_left(diag, near + far, far + near, held, sems)
    for which, values in enumerate(both_products(held, right0, right1)):
        top = jnp.maximum(jnp.max(jnp.abs(values), axis=0, keepdims=True), 1e-30)
        level = jnp.ceil(jnp.log(top) * (STEPS / LN2)) + 1.0
        coded = jnp.round(values * (LEVELS * jnp.exp(level * (-LN2 / STEPS))))
        coded = jnp.clip(coded, -32767.0, 32767.0).astype(jnp.int32).astype(jnp.int16)
        for t in range(tiles):
            at = which * across + step * tiles + t
            cut = slice(t * BLOCK, (t + 1) * BLOCK)
            out[pl.ds(pl.multiple_of(at * rows, rows), rows), :] = coded[:, cut]
            steps[pl.ds(at, 1), :] = level[:, cut]

    @pl.when(step == pl.num_programs(0) - 1)
    def _():
        tail = steps.shape[0]
        out[out.shape[0] - tail :, :] = steps[...].astype(jnp.int32).astype(jnp.int16)
        for copy in others:
            copy.wait()


def partial_products(diag, near, far, right0, right1, wide, given=(), gates=()):
    rows = sum(piece.shape[0] for piece in near)
    depth, columns = right0.shape
    tiles = 2 * columns // BLOCK
    tail = -(-tiles // 16) * 16
    return pl.pallas_call(
        functools.partial(partial_kernel, len(near), len(given)),
        grid=(columns // wide,),
        in_specs=[
            SM(),
            pl.BlockSpec((depth, wide), lambda g: (0, g)),
            pl.BlockSpec((depth, wide), lambda g: (0, g)),
        ]
        + [HB() for _ in (*near, *far, *given, *gates)],
        out_specs=[pl.BlockSpec((tiles * rows + tail, BLOCK), lambda g: (0, 0))]
        + [HB() for _ in given],
        out_shape=[jax.ShapeDtypeStruct((tiles * rows + tail, BLOCK), jnp.int16)]
        + [jax.ShapeDtypeStruct(x.shape, x.dtype) for x in given],
        scratch_shapes=[
            pltpu.VMEM((2 * rows, depth), near[0].dtype),
            pltpu.VMEM((tail, BLOCK), jnp.float32),
            pltpu.SemaphoreType.DMA((2 * len(near),)),
            pltpu.SemaphoreType.DMA((max(len(given), 1),)),
        ],
        compiler_params=params(),
        cost_estimate=cost(6 * rows * depth * columns, 4 * rows * depth + 4 * depth * columns),
        name="partial_products",
    )(diag, right0, right1, *near, *far, *given, *gates)


def finish_kernel(start, many, keep, coded, square, tangent, *rest):
    given, outs, passed = rest[:many], rest[-5 - many : -3 - many], rest[-3 - many : -3]
    made, out_sems, sems = rest[-3:]
    rows, columns = square.shape
    across = columns // BLOCK
    others = [
        pltpu.make_async_copy(x, y, sems.at[i]) for i, (x, y) in enumerate(zip(given, passed))
    ]
    results = [
        pltpu.make_async_copy(made.at[i], x.at[pl.ds(start, rows)], out_sems.at[i])
        for i, x in enumerate(outs)
    ]
    for copy in others:
        copy.start()
    tail = coded.shape[0] - 2 * across * rows
    levels = coded[coded.shape[0] - tail :, :].astype(jnp.int32).astype(jnp.float32)
    steps = jnp.exp(levels * (LN2 / STEPS)) * (1.0 / LEVELS)
    for which, mine in enumerate((square, tangent)):
        for j in range(across):
            tile = which * across + j
            cut = slice(j * BLOCK, (j + 1) * BLOCK)
            other = coded[tile * rows : (tile + 1) * rows, :].astype(jnp.int32).astype(jnp.float32)
            total = mine[:, cut] + other * steps[tile : tile + 1, :]
            for row_block, piece in row_pieces(start, rows):
                kept = total[piece] * keep[row_block, j].astype(jnp.float32)
                made[which, piece, cut] = kept.astype(made.dtype)
        results[which].start()
    for copy in results + others:
        copy.wait()


def finished(keep, square, tangent, coded, before, start, all_rows, held=(), after=()):
    rows, columns = square.shape
    out = jax.ShapeDtypeStruct((all_rows, columns), jnp.bfloat16)
    held, before = list(held), list(before)
    passed = [jax.ShapeDtypeStruct(x.shape, x.dtype) for x in held]
    many = len(held)
    return pl.pallas_call(
        functools.partial(finish_kernel, start, many),
        in_specs=[SM(), VM(), VM(), VM()] + [HB() for _ in (*held, *before, *after)],
        out_specs=[HB() for _ in range(2 + many)],
        out_shape=[out, out] + passed,
        input_output_aliases={4 + many: 0, 5 + many: 1} if before else {},
        scratch_shapes=[
            pltpu.VMEM((2, rows, columns), jnp.bfloat16),
            pltpu.SemaphoreType.DMA((2,)),
            pltpu.SemaphoreType.DMA((max(many, 1),)),
        ],
        compiler_params=params(),
        cost_estimate=cost(0, 16 * rows * columns),
        name="finish",
    )(keep, coded, square, tangent, *held, *before, *after)


def per_device_pair(
    n_row, x0_rows, x1_rows, x0_cols, x1_cols, mask0_rows, mask1_rows, mask0_cols, mask1_cols, keep
):
    n_col = 2
    group = n_row // n_col
    panel = x0_cols.shape[0]
    all_rows = x0_rows.shape[0]
    row_index = lax.axis_index("row")
    half = row_index // group
    diag = (half == lax.axis_index("col")).astype(jnp.int32).reshape(1)
    place = (row_index % group).astype(jnp.int32).reshape(1)
    edges = [all_rows * e // 16 for e in (0, 3, 7, 13, 16)]
    spans = list(zip(edges, edges[1:]))
    many = len(spans)
    split = edges[2]
    wide = 256

    def device(h, q, c):
        return (h * group + q) * n_col + c

    spots = [(h, q, c) for h in range(2) for q in range(group) for c in range(2)]
    over_y = [(device(h, q, c), device(h, q, 1 - c)) for h, q, c in spots]
    over_z = [(device(h, q, c), device(1 - h, q, c)) for h, q, c in spots]

    def move(values, pairs):
        return lax.ppermute(values, ("row", "col"), pairs)

    def chunks(spans, slabs, after=()):
        return masked_chunks(
            place, diag, mask0_rows, mask1_rows, x0_rows, x1_rows, spans, slabs, panel, after
        )

    def partials(which, given=(), **more):
        return partial_products(diag, near[which], far[which], right0, right1, wide, given, **more)

    def own(which, b, got):
        mine, other = (*a[which], *b), (*passed[which], *got)
        return local_products(diag, mine, other, right0, right1, wide)

    a, swap, passed, near, far = ([None] * many for _ in range(5))
    early, late = slice(0, 2), slice(2, many)
    a[0], swap[0] = chunks(spans[:1], ())
    *rest, b0, b1 = chunks(spans[1:], ((0, split), (split, all_rows)), (swap[0],))
    a[1:], swap[1:] = rest[0::2], rest[1::2]
    right0 = right1 = None
    for i in range(many):
        passed[i] = move(swap[i], over_y)
        last = i == many - 1
        gate = {1: (near[0],), 2: (right0,)}.get(i, ())
        send, later = chosen(diag, passed[i], a[i], (b0 if last else swap[i + 1],), gate)
        if last:
            b0 = later
        else:
            swap[i + 1] = later
        near[i] = move(send, over_z)
        if i == 1:
            right0, right1 = masked_right(mask0_cols, mask1_cols, x0_cols, x1_cols, (send,))
    far[0], far[1], far[3] = (move(near[i], over_y) for i in (0, 1, 3))
    (coded,) = partials(early)
    coded, last_near = handed_on((coded, near[2]), (near[3],))
    back = move(coded, over_z)
    far[2] = move(last_near, over_y)
    mine = own(early, (b0,), (move(b0, over_y),))
    coded, b1 = partials(late, given=(b1,), gates=mine[:1])
    (coded,) = handed_on((coded,), (back,))
    outs = finished(keep, *mine, back, (), 0, all_rows)
    back = move(coded, over_z)
    mine = own(late, (b1,), (move(b1, over_y),))
    return tuple(finished(keep, *mine, back, outs, split, all_rows))


def passed_along(shard, axis, by):
    devices = lax.axis_size(axis)
    return lax.ppermute(shard, axis, [(i, (i + by) % devices) for i in range(devices)])


def masked(values, mask):
    rows_b, cols_b = mask.shape
    tiles = values.reshape(rows_b, BLOCK, cols_b, BLOCK)
    return (tiles * mask.astype(values.dtype)[:, None, :, None]).reshape(values.shape)


def per_device(
    x0_rows, x1_rows, x0_cols, x1_cols, mask0_rows, mask1_rows, mask0_cols, mask1_cols, keep_mask
):
    n_row = lax.axis_size("row")
    n_col = lax.axis_size("col")
    group = n_row // n_col
    row_index = lax.axis_index("row")
    col_index = lax.axis_index("col")
    panel = x0_cols.shape[0]
    start = row_index % group * panel
    block_start = row_index % group * (panel // BLOCK)
    left_zero = masked(
        lax.dynamic_slice_in_dim(x0_rows, start, panel, 1),
        lax.dynamic_slice_in_dim(mask0_rows, block_start, panel // BLOCK, 1),
    )
    left_one = masked(
        lax.dynamic_slice_in_dim(x1_rows, start, panel, 1),
        lax.dynamic_slice_in_dim(mask1_rows, block_start, panel // BLOCK, 1),
    )
    right_zero = masked(x0_cols, mask0_cols)
    right_one = masked(x1_cols, mask1_cols)
    left = jnp.stack([left_zero, left_one])
    right = jnp.stack([right_zero, right_one])
    left_offset = row_index // group % n_col
    right_offset = col_index % n_col
    levels = n_col.bit_length() - 1
    for level in range(levels):
        moved_left = passed_along(left, "col", -(1 << level))
        moved_right = passed_along(right, "row", -group * (1 << level))
        left = jnp.where(left_offset // (1 << level) % 2 == 1, moved_left, left)
        right = jnp.where(right_offset // (1 << level) % 2 == 1, moved_right, right)

    def accumulate(left_now, right_now, square, tangent):
        square = square + jnp.dot(left_now[0], right_now[0], preferred_element_type=jnp.float32)
        tangent = tangent + jnp.dot(left_now[0], right_now[1], preferred_element_type=jnp.float32)
        tangent = tangent + jnp.dot(left_now[1], right_now[0], preferred_element_type=jnp.float32)
        return (square, tangent)

    def section_body(section, carry):
        left_now, right_now, square, tangent = carry
        square, tangent = accumulate(left_now, right_now, square, tangent)
        left_now = passed_along(left_now, "col", -1)
        right_now = passed_along(right_now, "row", -group)
        return (left_now, right_now, square, tangent)

    zeros = jnp.zeros((left_zero.shape[0], right_zero.shape[1]), jnp.float32)
    left, right, square, tangent = lax.fori_loop(
        0, n_col - 1, section_body, (left, right, zeros, zeros)
    )
    square, tangent = accumulate(left, right, square, tangent)
    x_square = masked(square, keep_mask).astype(jnp.bfloat16)
    x_tangent = masked(tangent, keep_mask).astype(jnp.bfloat16)
    return (x_square, x_tangent)


def solution(mesh):
    if mesh.shape["col"] == 2:
        body = functools.partial(per_device_pair, mesh.shape["row"])
    else:
        body = per_device
    return jax.shard_map(
        body,
        mesh=mesh,
        in_specs=(P("row", "col"),) * 9,
        out_specs=(P("row", "col"), P("row", "col")),
        check_vma=False,
    )
```

```python
import functools
import math

import jax
import jax.numpy as jnp
from jax import lax
from jax.experimental import pallas as pl
from jax.experimental.pallas import tpu as pltpu
from jax.sharding import PartitionSpec as P

BLOCK = 128
LEVELS = 32000.0
STEPS = 32.0
LN2 = math.log(2.0)
VMEM_BYTES = 48 * 1024 * 1024
ALL_VMEM_BYTES = 62 * 1024 * 1024

VM = functools.partial(pl.BlockSpec, memory_space=pltpu.VMEM)
SM = functools.partial(pl.BlockSpec, memory_space=pltpu.SMEM)
HB = functools.partial(pl.BlockSpec, memory_space=pl.ANY)


def params(limit=VMEM_BYTES):
    return pltpu.CompilerParams(vmem_limit_bytes=limit)


def cost(flops, moved):
    return pl.CostEstimate(flops=int(flops) // 64, bytes_accessed=int(moved) // 64, transcendentals=0)


def scaled(values, entry):
    return (values.astype(jnp.float32) * entry.astype(jnp.float32)).astype(values.dtype)


def row_pieces(start, rows):
    edges = sorted({start, start + rows} | {e for e in range(0, start + rows, BLOCK) if e > start})
    return [(lo // BLOCK, slice(lo - start, hi - start)) for lo, hi in zip(edges, edges[1:])]


def chunk_kernel(spans, slabs, panel, *refs):
    place, diag, mask0_far, mask1_far, x0, x1 = refs[:6]
    held, mask0, mask1, mask_sems, sems = refs[-5:]
    many = 2 * len(spans) + len(slabs)
    outs = refs[-5 - many : -5]
    masks = [
        pltpu.make_async_copy(mask0_far, mask0, mask_sems.at[0]),
        pltpu.make_async_copy(mask1_far, mask1, mask_sems.at[1]),
    ]
    for copy in masks:
        copy.start()
    with_slab = len(slabs) > 0
    blocks = panel // BLOCK
    first = place[0] * blocks
    at = pl.ds(pl.multiple_of(place[0] * panel, BLOCK), panel)
    origin = 0 if with_slab else spans[0][0]
    copies = []
    for n, (lo, hi) in enumerate(spans):
        lo = origin if n == 0 else lo
        for i, x in enumerate((x0, x1)):
            here = pl.ds(lo - origin, hi - lo)
            copies.append(
                pltpu.make_async_copy(x.at[pl.ds(lo, hi - lo), at], held.at[i, here], sems.at[n, i])
            )
    for copy in copies:
        copy.start()
    for copy in masks + copies:
        copy.wait()
    for n, (lo, hi) in enumerate(slabs):
        for row_block, piece in row_pieces(lo, hi - lo):
            rows = slice(piece.start + lo, piece.stop + lo)
            for j in range(blocks):
                cut = slice(j * BLOCK, (j + 1) * BLOCK)
                product = scaled(held[1, rows, cut], mask1[row_block, first + j])
                outs[2 * len(spans) + n][piece, cut] = product
    for n, (lo, hi) in enumerate(spans):
        a_out, swap = outs[2 * n], outs[2 * n + 1]
        for row_block, piece in row_pieces(lo, hi - lo):
            rows = slice(piece.start + lo - origin, piece.stop + lo - origin)
            for j in range(blocks):
                cut = slice(j * BLOCK, (j + 1) * BLOCK)
                a_out[piece, cut] = scaled(held[0, rows, cut], mask0[row_block, first + j])

        @pl.when(diag[0] == 1)
        def _():
            swap[...] = a_out[...]

        @pl.when(diag[0] == 0)
        def _():
            for row_block, piece in row_pieces(lo, hi - lo):
                rows = slice(piece.start + lo - origin, piece.stop + lo - origin)
                for j in range(blocks):
                    cut = slice(j * BLOCK, (j + 1) * BLOCK)
                    swap[piece, cut] = scaled(held[1, rows, cut], mask1[row_block, first + j])


def masked_chunks(place, diag, mask0, mask1, x0, x1, spans, slabs, panel, after=()):
    outs = []
    for lo, hi in spans:
        outs += [jax.ShapeDtypeStruct((hi - lo, panel), x0.dtype)] * 2
    for lo, hi in slabs:
        outs.append(jax.ShapeDtypeStruct((hi - lo, panel), x0.dtype))
    high = spans[-1][1] - (0 if slabs else spans[0][0])
    return pl.pallas_call(
        functools.partial(chunk_kernel, spans, slabs, panel),
        in_specs=[SM(), SM()] + [HB() for _ in range(4 + len(after))],
        out_specs=[VM() for _ in outs],
        out_shape=outs,
        scratch_shapes=[
            pltpu.VMEM((2, high, panel), x0.dtype),
            pltpu.SMEM(mask0.shape, mask0.dtype),
            pltpu.SMEM(mask1.shape, mask1.dtype),
            pltpu.SemaphoreType.DMA((2,)),
            pltpu.SemaphoreType.DMA((len(spans), 2)),
        ],
        compiler_params=params(VMEM_BYTES if slabs else ALL_VMEM_BYTES),
        cost_estimate=cost(0, 8 * high * panel),
        name="left_chunks",
    )(place, diag, mask0, mask1, x0, x1, *after)


def choose_kernel(gates, many, diag, *refs):
    one, other = refs[gates : gates + 2]
    held, outs, sems = refs[gates + 2 : gates + 2 + many], refs[-many - 2 : -1], refs[-1]
    others = [
        pltpu.make_async_copy(x, out, sems.at[1 + i])
        for i, (x, out) in enumerate(zip(held, outs[1:]))
    ]
    for copy in others:
        copy.start()

    @pl.when(diag[0] == 1)
    def _():
        copy = pltpu.make_async_copy(one, outs[0], sems.at[0])
        copy.start()
        copy.wait()

    @pl.when(diag[0] == 0)
    def _():
        copy = pltpu.make_async_copy(other, outs[0], sems.at[0])
        copy.start()
        copy.wait()

    for copy in others:
        copy.wait()


def chosen(diag, one, other, held=(), after=()):
    outs = [jax.ShapeDtypeStruct(x.shape, x.dtype) for x in (one, *held)]
    return pl.pallas_call(
        functools.partial(choose_kernel, len(after), len(held)),
        in_specs=[SM()] + [HB() for _ in (*after, one, other, *held)],
        out_specs=[HB() for _ in outs],
        out_shape=outs,
        scratch_shapes=[pltpu.SemaphoreType.DMA((len(outs),))],
        compiler_params=params(),
        cost_estimate=cost(0, 4 * one.size),
        name="to_send",
    )(diag, *after, one, other, *held)


def hand_kernel(many, *refs):
    sems = refs[-1]
    copies = [
        pltpu.make_async_copy(refs[i], refs[i - many - 1], sems.at[i]) for i in range(many)
    ]
    for copy in copies:
        copy.start()
    for copy in copies:
        copy.wait()


def handed_on(values, gates):
    outs = [jax.ShapeDtypeStruct(x.shape, x.dtype) for x in values]
    return pl.pallas_call(
        functools.partial(hand_kernel, len(values)),
        in_specs=[HB() for _ in (*values, *gates)],
        out_specs=[HB() for _ in outs],
        out_shape=outs,
        scratch_shapes=[pltpu.SemaphoreType.DMA((len(outs),))],
        compiler_params=params(),
        cost_estimate=cost(0, 4 * sum(x.size for x in values)),
        name="handed_on",
    )(*values, *gates)


def right_kernel(mask0, mask1, x0, x1, *rest):
    out0, out1 = rest[-2:]
    step = pl.program_id(0)
    many = x0.shape[0] // BLOCK
    for i in range(many):
        for j in range(x0.shape[1] // BLOCK):
            at = (slice(i * BLOCK, (i + 1) * BLOCK), slice(j * BLOCK, (j + 1) * BLOCK))
            out0[at] = scaled(x0[at], mask0[step * many + i, j])
            out1[at] = scaled(x1[at], mask1[step * many + i, j])


def masked_right(mask0, mask1, x0, x1, after=()):
    depth, columns = x0.shape
    tall = 2 * BLOCK
    out = jax.ShapeDtypeStruct(x0.shape, x0.dtype)
    tile = pl.BlockSpec((tall, columns), lambda g: (g, 0))
    return pl.pallas_call(
        right_kernel,
        grid=(depth // tall,),
        in_specs=[SM(), SM(), tile, tile] + [HB() for _ in after],
        out_specs=[tile, tile],
        out_shape=[out, out],
        compiler_params=params(),
        cost_estimate=cost(0, 8 * depth * columns),
        name="right_panels",
    )(mask0, mask1, x0, x1, *after)


def both_products(held, right0, right1):
    rows = held.shape[0] // 2
    first = jnp.dot(held[...], right0[...], preferred_element_type=jnp.float32)
    second = jnp.dot(held[:rows], right1[...], preferred_element_type=jnp.float32)
    return first[:rows], first[rows:] + second


def fetched(pieces, held, sems):
    copies = []
    top = 0
    for i, piece in enumerate(pieces):
        rows = piece.shape[0]
        copies.append(pltpu.make_async_copy(piece, held.at[pl.ds(top, rows)], sems.at[i]))
        top += rows
    for copy in copies:
        copy.start()
    for copy in copies:
        copy.wait()


def fetch_left(diag, one, other, held, sems):
    first = pl.program_id(0) == 0

    @pl.when(first & (diag[0] == 1))
    def _():
        fetched(one, held, sems)

    @pl.when(first & (diag[0] == 0))
    def _():
        fetched(other, held, sems)


def local_kernel(many, diag, right0, right1, *refs):
    own, got = refs[:many], refs[many : 2 * many]
    square, tangent, held, sems = refs[-4:]
    fetch_left(diag, own, got, held, sems)
    square[...], tangent[...] = both_products(held, right0, right1)


def local_products(diag, own, got, right0, right1, wide, after=()):
    rows = sum(piece.shape[0] for piece in own) // 2
    depth, columns = right0.shape
    many = len(own)
    out = jax.ShapeDtypeStruct((rows, columns), jnp.float32)
    tile = pl.BlockSpec((rows, wide), lambda g: (0, g))
    return pl.pallas_call(
        functools.partial(local_kernel, many),
        grid=(columns // wide,),
        in_specs=[
            SM(),
            pl.BlockSpec((depth, wide), lambda g: (0, g)),
            pl.BlockSpec((depth, wide), lambda g: (0, g)),
        ]
        + [HB() for _ in (*own, *got, *after)],
        out_specs=[tile, tile],
        out_shape=[out, out],
        scratch_shapes=[
            pltpu.VMEM((2 * rows, depth), own[-1].dtype),
            pltpu.SemaphoreType.DMA((many,)),
        ],
        compiler_params=params(),
        cost_estimate=cost(6 * rows * depth * columns, 8 * rows * depth + 4 * depth * columns),
        name="own_products",
    )(diag, right0, right1, *own, *got, *after)


def partial_kernel(many, given, diag, right0, right1, *refs):
    near, far = refs[:many], refs[many : 2 * many]
    out, passed = refs[-5 - given], refs[-4 - given : -4]
    held, steps, sems, hand_sems = refs[-4:]
    others = [
        pltpu.make_async_copy(x, y, hand_sems.at[i])
        for i, (x, y) in enumerate(zip(refs[2 * many : 2 * many + given], passed))
    ]

    @pl.when(pl.program_id(0) == 0)
    def _():
        for copy in others:
            copy.start()

    rows, wide = held.shape[0] // 2, right0.shape[1]
    step = pl.program_id(0)
    tiles = wide // BLOCK
    across = pl.num_programs(0) * tiles
    fetch_left(diag, near + far, far + near, held, sems)
    for which, values in enumerate(both_products(held, right0, right1)):
        top = jnp.maximum(jnp.max(jnp.abs(values), axis=0, keepdims=True), 1e-30)
        level = jnp.ceil(jnp.log(top) * (STEPS / LN2)) + 1.0
        coded = jnp.round(values * (LEVELS * jnp.exp(level * (-LN2 / STEPS))))
        coded = jnp.clip(coded, -32767.0, 32767.0).astype(jnp.int32).astype(jnp.int16)
        for t in range(tiles):
            at = which * across + step * tiles + t
            cut = slice(t * BLOCK, (t + 1) * BLOCK)
            out[pl.ds(pl.multiple_of(at * rows, rows), rows), :] = coded[:, cut]
            steps[pl.ds(at, 1), :] = level[:, cut]

    @pl.when(step == pl.num_programs(0) - 1)
    def _():
        tail = steps.shape[0]
        out[out.shape[0] - tail :, :] = steps[...].astype(jnp.int32).astype(jnp.int16)
        for copy in others:
            copy.wait()


def partial_products(diag, near, far, right0, right1, wide, given=(), gates=()):
    rows = sum(piece.shape[0] for piece in near)
    depth, columns = right0.shape
    tiles = 2 * columns // BLOCK
    tail = -(-tiles // 16) * 16
    return pl.pallas_call(
        functools.partial(partial_kernel, len(near), len(given)),
        grid=(columns // wide,),
        in_specs=[
            SM(),
            pl.BlockSpec((depth, wide), lambda g: (0, g)),
            pl.BlockSpec((depth, wide), lambda g: (0, g)),
        ]
        + [HB() for _ in (*near, *far, *given, *gates)],
        out_specs=[pl.BlockSpec((tiles * rows + tail, BLOCK), lambda g: (0, 0))]
        + [HB() for _ in given],
        out_shape=[jax.ShapeDtypeStruct((tiles * rows + tail, BLOCK), jnp.int16)]
        + [jax.ShapeDtypeStruct(x.shape, x.dtype) for x in given],
        scratch_shapes=[
            pltpu.VMEM((2 * rows, depth), near[0].dtype),
            pltpu.VMEM((tail, BLOCK), jnp.float32),
            pltpu.SemaphoreType.DMA((2 * len(near),)),
            pltpu.SemaphoreType.DMA((max(len(given), 1),)),
        ],
        compiler_params=params(),
        cost_estimate=cost(6 * rows * depth * columns, 4 * rows * depth + 4 * depth * columns),
        name="partial_products",
    )(diag, right0, right1, *near, *far, *given, *gates)


def finish_kernel(start, many, keep, coded, square, tangent, *rest):
    given, outs, passed = rest[:many], rest[-5 - many : -3 - many], rest[-3 - many : -3]
    made, out_sems, sems = rest[-3:]
    rows, columns = square.shape
    across = columns // BLOCK
    others = [
        pltpu.make_async_copy(x, y, sems.at[i]) for i, (x, y) in enumerate(zip(given, passed))
    ]
    results = [
        pltpu.make_async_copy(made.at[i], x.at[pl.ds(start, rows)], out_sems.at[i])
        for i, x in enumerate(outs)
    ]
    for copy in others:
        copy.start()
    tail = coded.shape[0] - 2 * across * rows
    levels = coded[coded.shape[0] - tail :, :].astype(jnp.int32).astype(jnp.float32)
    steps = jnp.exp(levels * (LN2 / STEPS)) * (1.0 / LEVELS)
    for which, mine in enumerate((square, tangent)):
        for j in range(across):
            tile = which * across + j
            cut = slice(j * BLOCK, (j + 1) * BLOCK)
            other = coded[tile * rows : (tile + 1) * rows, :].astype(jnp.int32).astype(jnp.float32)
            total = mine[:, cut] + other * steps[tile : tile + 1, :]
            for row_block, piece in row_pieces(start, rows):
                kept = total[piece] * keep[row_block, j].astype(jnp.float32)
                made[which, piece, cut] = kept.astype(made.dtype)
        results[which].start()
    for copy in results + others:
        copy.wait()


def finished(keep, square, tangent, coded, before, start, all_rows, held=(), after=()):
    rows, columns = square.shape
    out = jax.ShapeDtypeStruct((all_rows, columns), jnp.bfloat16)
    held, before = list(held), list(before)
    passed = [jax.ShapeDtypeStruct(x.shape, x.dtype) for x in held]
    many = len(held)
    return pl.pallas_call(
        functools.partial(finish_kernel, start, many),
        in_specs=[SM(), VM(), VM(), VM()] + [HB() for _ in (*held, *before, *after)],
        out_specs=[HB() for _ in range(2 + many)],
        out_shape=[out, out] + passed,
        input_output_aliases={4 + many: 0, 5 + many: 1} if before else {},
        scratch_shapes=[
            pltpu.VMEM((2, rows, columns), jnp.bfloat16),
            pltpu.SemaphoreType.DMA((2,)),
            pltpu.SemaphoreType.DMA((max(many, 1),)),
        ],
        compiler_params=params(),
        cost_estimate=cost(0, 16 * rows * columns),
        name="finish",
    )(keep, coded, square, tangent, *held, *before, *after)


def per_device_pair(
    n_row, x0_rows, x1_rows, x0_cols, x1_cols, mask0_rows, mask1_rows, mask0_cols, mask1_cols, keep
):
    n_col = 2
    group = n_row // n_col
    panel = x0_cols.shape[0]
    all_rows = x0_rows.shape[0]
    row_index = lax.axis_index("row")
    half = row_index // group
    diag = (half == lax.axis_index("col")).astype(jnp.int32).reshape(1)
    place = (row_index % group).astype(jnp.int32).reshape(1)
    edges = [all_rows * e // 16 for e in (0, 3, 8, 13, 16)]
    spans = list(zip(edges, edges[1:]))
    many = len(spans)
    split = edges[2]
    wide = 256

    def device(h, q, c):
        return (h * group + q) * n_col + c

    spots = [(h, q, c) for h in range(2) for q in range(group) for c in range(2)]
    over_y = [(device(h, q, c), device(h, q, 1 - c)) for h, q, c in spots]
    over_z = [(device(h, q, c), device(1 - h, q, c)) for h, q, c in spots]

    def move(values, pairs):
        return lax.ppermute(values, ("row", "col"), pairs)

    def chunks(spans, slabs, after=()):
        return masked_chunks(
            place, diag, mask0_rows, mask1_rows, x0_rows, x1_rows, spans, slabs, panel, after
        )

    def partials(which, given=(), **more):
        return partial_products(diag, near[which], far[which], right0, right1, wide, given, **more)

    def own(which, b, got):
        mine, other = (*a[which], *b), (*passed[which], *got)
        return local_products(diag, mine, other, right0, right1, wide)

    a, swap, passed, near, far = ([None] * many for _ in range(5))
    early, late = slice(0, 2), slice(2, many)
    a[0], swap[0] = chunks(spans[:1], ())
    *rest, b0, b1 = chunks(spans[1:], ((0, split), (split, all_rows)), (swap[0],))
    a[1:], swap[1:] = rest[0::2], rest[1::2]
    right0 = right1 = None
    for i in range(many):
        passed[i] = move(swap[i], over_y)
        last = i == many - 1
        gate = {1: (near[0],), 2: (right0,)}.get(i, ())
        send, later = chosen(diag, passed[i], a[i], (b0 if last else swap[i + 1],), gate)
        if last:
            b0 = later
        else:
            swap[i + 1] = later
        near[i] = move(send, over_z)
        if i == 1:
            right0, right1 = masked_right(mask0_cols, mask1_cols, x0_cols, x1_cols, (send,))
    far[0], far[1], far[3] = (move(near[i], over_y) for i in (0, 1, 3))
    (coded,) = partials(early)
    coded, last_near = handed_on((coded, near[2]), (near[3],))
    back = move(coded, over_z)
    far[2] = move(last_near, over_y)
    mine = own(early, (b0,), (move(b0, over_y),))
    coded, b1 = partials(late, given=(b1,), gates=mine[:1])
    (coded,) = handed_on((coded,), (back,))
    outs = finished(keep, *mine, back, (), 0, all_rows)
    back = move(coded, over_z)
    mine = own(late, (b1,), (move(b1, over_y),))
    return tuple(finished(keep, *mine, back, outs, split, all_rows))


def passed_along(shard, axis, by):
    devices = lax.axis_size(axis)
    return lax.ppermute(shard, axis, [(i, (i + by) % devices) for i in range(devices)])


def masked(values, mask):
    rows_b, cols_b = mask.shape
    tiles = values.reshape(rows_b, BLOCK, cols_b, BLOCK)
    return (tiles * mask.astype(values.dtype)[:, None, :, None]).reshape(values.shape)


def per_device(
    x0_rows, x1_rows, x0_cols, x1_cols, mask0_rows, mask1_rows, mask0_cols, mask1_cols, keep_mask
):
    n_row = lax.axis_size("row")
    n_col = lax.axis_size("col")
    group = n_row // n_col
    row_index = lax.axis_index("row")
    col_index = lax.axis_index("col")
    panel = x0_cols.shape[0]
    start = row_index % group * panel
    block_start = row_index % group * (panel // BLOCK)
    left_zero = masked(
        lax.dynamic_slice_in_dim(x0_rows, start, panel, 1),
        lax.dynamic_slice_in_dim(mask0_rows, block_start, panel // BLOCK, 1),
    )
    left_one = masked(
        lax.dynamic_slice_in_dim(x1_rows, start, panel, 1),
        lax.dynamic_slice_in_dim(mask1_rows, block_start, panel // BLOCK, 1),
    )
    right_zero = masked(x0_cols, mask0_cols)
    right_one = masked(x1_cols, mask1_cols)
    left = jnp.stack([left_zero, left_one])
    right = jnp.stack([right_zero, right_one])
    left_offset = row_index // group % n_col
    right_offset = col_index % n_col
    levels = n_col.bit_length() - 1
    for level in range(levels):
        moved_left = passed_along(left, "col", -(1 << level))
        moved_right = passed_along(right, "row", -group * (1 << level))
        left = jnp.where(left_offset // (1 << level) % 2 == 1, moved_left, left)
        right = jnp.where(right_offset // (1 << level) % 2 == 1, moved_right, right)

    def accumulate(left_now, right_now, square, tangent):
        square = square + jnp.dot(left_now[0], right_now[0], preferred_element_type=jnp.float32)
        tangent = tangent + jnp.dot(left_now[0], right_now[1], preferred_element_type=jnp.float32)
        tangent = tangent + jnp.dot(left_now[1], right_now[0], preferred_element_type=jnp.float32)
        return (square, tangent)

    def section_body(section, carry):
        left_now, right_now, square, tangent = carry
        square, tangent = accumulate(left_now, right_now, square, tangent)
        left_now = passed_along(left_now, "col", -1)
        right_now = passed_along(right_now, "row", -group)
        return (left_now, right_now, square, tangent)

    zeros = jnp.zeros((left_zero.shape[0], right_zero.shape[1]), jnp.float32)
    left, right, square, tangent = lax.fori_loop(
        0, n_col - 1, section_body, (left, right, zeros, zeros)
    )
    square, tangent = accumulate(left, right, square, tangent)
    x_square = masked(square, keep_mask).astype(jnp.bfloat16)
    x_tangent = masked(tangent, keep_mask).astype(jnp.bfloat16)
    return (x_square, x_tangent)


def solution(mesh):
    if mesh.shape["col"] == 2:
        body = functools.partial(per_device_pair, mesh.shape["row"])
    else:
        body = per_device
    return jax.shard_map(
        body,
        mesh=mesh,
        in_specs=(P("row", "col"),) * 9,
        out_specs=(P("row", "col"), P("row", "col")),
        check_vma=False,
    )
```

```python
import functools
import math

import jax
import jax.numpy as jnp
from jax import lax
from jax.experimental import pallas as pl
from jax.experimental.pallas import tpu as pltpu
from jax.sharding import PartitionSpec as P

BLOCK = 128
LEVELS = 32000.0
STEPS = 32.0
LN2 = math.log(2.0)
VMEM_BYTES = 48 * 1024 * 1024
ALL_VMEM_BYTES = 62 * 1024 * 1024

VM = functools.partial(pl.BlockSpec, memory_space=pltpu.VMEM)
SM = functools.partial(pl.BlockSpec, memory_space=pltpu.SMEM)
HB = functools.partial(pl.BlockSpec, memory_space=pl.ANY)


def params(limit=VMEM_BYTES):
    return pltpu.CompilerParams(vmem_limit_bytes=limit)


def cost(flops, moved):
    return pl.CostEstimate(flops=int(flops) // 64, bytes_accessed=int(moved) // 64, transcendentals=0)


def scaled(values, entry):
    return (values.astype(jnp.float32) * entry.astype(jnp.float32)).astype(values.dtype)


def row_pieces(start, rows):
    edges = sorted({start, start + rows} | {e for e in range(0, start + rows, BLOCK) if e > start})
    return [(lo // BLOCK, slice(lo - start, hi - start)) for lo, hi in zip(edges, edges[1:])]


def chunk_kernel(start, panel, *refs):
    place, mask0_far, mask1_far, x0, x1 = refs[:5]
    a_out, b_out, held, mask0, mask1, mask_sems, sems = refs[-7:]
    rows = a_out.shape[0]
    blocks = panel // BLOCK
    first = place[0] * blocks
    at = pl.ds(pl.multiple_of(place[0] * panel, BLOCK), panel)
    copies = [
        pltpu.make_async_copy(mask0_far, mask0, mask_sems.at[0]),
        pltpu.make_async_copy(mask1_far, mask1, mask_sems.at[1]),
        pltpu.make_async_copy(x0.at[pl.ds(start, rows), at], held.at[0], sems.at[0]),
        pltpu.make_async_copy(x1.at[pl.ds(start, rows), at], held.at[1], sems.at[1]),
    ]
    for copy in copies:
        copy.start()
    for copy in copies:
        copy.wait()
    for which, (mask, out) in enumerate(((mask0, a_out), (mask1, b_out))):
        for row_block, piece in row_pieces(start, rows):
            for j in range(blocks):
                cut = slice(j * BLOCK, (j + 1) * BLOCK)
                out[piece, cut] = scaled(held[which, piece, cut], mask[row_block, first + j])


def masked_chunk(place, mask0, mask1, x0, x1, span, panel, limit, after=()):
    rows = span[1] - span[0]
    out = jax.ShapeDtypeStruct((rows, panel), x0.dtype)
    return pl.pallas_call(
        functools.partial(chunk_kernel, span[0], panel),
        in_specs=[SM()] + [HB() for _ in range(4 + len(after))],
        out_specs=[VM(), VM()],
        out_shape=[out, out],
        scratch_shapes=[
            pltpu.VMEM((2, rows, panel), x0.dtype),
            pltpu.SMEM(mask0.shape, mask0.dtype),
            pltpu.SMEM(mask1.shape, mask1.dtype),
            pltpu.SemaphoreType.DMA((2,)),
            pltpu.SemaphoreType.DMA((2,)),
        ],
        compiler_params=params(limit),
        cost_estimate=cost(0, 8 * rows * panel),
        name="left_chunk",
    )(place, mask0, mask1, x0, x1, *after)


def choose_kernel(gates, many, diag, *refs):
    one, other = refs[gates : gates + 2]
    held, outs, sems = refs[gates + 2 : gates + 2 + many], refs[-many - 2 : -1], refs[-1]
    others = [
        pltpu.make_async_copy(x, out, sems.at[1 + i])
        for i, (x, out) in enumerate(zip(held, outs[1:]))
    ]
    for copy in others:
        copy.start()

    @pl.when(diag[0] == 1)
    def _():
        copy = pltpu.make_async_copy(one, outs[0], sems.at[0])
        copy.start()
        copy.wait()

    @pl.when(diag[0] == 0)
    def _():
        copy = pltpu.make_async_copy(other, outs[0], sems.at[0])
        copy.start()
        copy.wait()

    for copy in others:
        copy.wait()


def chosen(diag, one, other, held=(), after=()):
    outs = [jax.ShapeDtypeStruct(x.shape, x.dtype) for x in (one, *held)]
    return pl.pallas_call(
        functools.partial(choose_kernel, len(after), len(held)),
        in_specs=[SM()] + [HB() for _ in (*after, one, other, *held)],
        out_specs=[HB() for _ in outs],
        out_shape=outs,
        scratch_shapes=[pltpu.SemaphoreType.DMA((len(outs),))],
        compiler_params=params(),
        cost_estimate=cost(0, 4 * one.size),
        name="to_send",
    )(diag, *after, one, other, *held)


def hand_kernel(many, *refs):
    sems = refs[-1]
    copies = [
        pltpu.make_async_copy(refs[i], refs[i - many - 1], sems.at[i]) for i in range(many)
    ]
    for copy in copies:
        copy.start()
    for copy in copies:
        copy.wait()


def handed_on(values, gates):
    outs = [jax.ShapeDtypeStruct(x.shape, x.dtype) for x in values]
    return pl.pallas_call(
        functools.partial(hand_kernel, len(values)),
        in_specs=[HB() for _ in (*values, *gates)],
        out_specs=[HB() for _ in outs],
        out_shape=outs,
        scratch_shapes=[pltpu.SemaphoreType.DMA((len(outs),))],
        compiler_params=params(),
        cost_estimate=cost(0, 4 * sum(x.size for x in values)),
        name="handed_on",
    )(*values, *gates)


def right_kernel(mask0, mask1, x0, x1, *rest):
    out0, out1 = rest[-2:]
    step = pl.program_id(0)
    many = x0.shape[0] // BLOCK
    for i in range(many):
        for j in range(x0.shape[1] // BLOCK):
            at = (slice(i * BLOCK, (i + 1) * BLOCK), slice(j * BLOCK, (j + 1) * BLOCK))
            out0[at] = scaled(x0[at], mask0[step * many + i, j])
            out1[at] = scaled(x1[at], mask1[step * many + i, j])


def masked_right(mask0, mask1, x0, x1, after=()):
    depth, columns = x0.shape
    tall = 2 * BLOCK
    out = jax.ShapeDtypeStruct(x0.shape, x0.dtype)
    tile = pl.BlockSpec((tall, columns), lambda g: (g, 0))
    return pl.pallas_call(
        right_kernel,
        grid=(depth // tall,),
        in_specs=[SM(), SM(), tile, tile] + [HB() for _ in after],
        out_specs=[tile, tile],
        out_shape=[out, out],
        compiler_params=params(),
        cost_estimate=cost(0, 8 * depth * columns),
        name="right_panels",
    )(mask0, mask1, x0, x1, *after)


def both_products(held, right0, right1):
    rows = held.shape[0] // 2
    first = jnp.dot(held[...], right0[...], preferred_element_type=jnp.float32)
    second = jnp.dot(held[:rows], right1[...], preferred_element_type=jnp.float32)
    return first[:rows], first[rows:] + second


def fetched(pieces, held, sems):
    copies = []
    top = 0
    for i, piece in enumerate(pieces):
        rows = piece.shape[0]
        copies.append(pltpu.make_async_copy(piece, held.at[pl.ds(top, rows)], sems.at[i]))
        top += rows
    for copy in copies:
        copy.start()
    for copy in copies:
        copy.wait()


def fetch_left(diag, one, other, held, sems):
    first = pl.program_id(0) == 0

    @pl.when(first & (diag[0] == 1))
    def _():
        fetched(one, held, sems)

    @pl.when(first & (diag[0] == 0))
    def _():
        fetched(other, held, sems)


def local_kernel(many, diag, right0, right1, *refs):
    own, got = refs[:many], refs[many : 2 * many]
    square, tangent, held, sems = refs[-4:]
    fetch_left(diag, own, got, held, sems)
    square[...], tangent[...] = both_products(held, right0, right1)


def local_products(diag, own, got, right0, right1, wide, after=()):
    rows = sum(piece.shape[0] for piece in own) // 2
    depth, columns = right0.shape
    many = len(own)
    out = jax.ShapeDtypeStruct((rows, columns), jnp.float32)
    tile = pl.BlockSpec((rows, wide), lambda g: (0, g))
    return pl.pallas_call(
        functools.partial(local_kernel, many),
        grid=(columns // wide,),
        in_specs=[
            SM(),
            pl.BlockSpec((depth, wide), lambda g: (0, g)),
            pl.BlockSpec((depth, wide), lambda g: (0, g)),
        ]
        + [HB() for _ in (*own, *got, *after)],
        out_specs=[tile, tile],
        out_shape=[out, out],
        scratch_shapes=[
            pltpu.VMEM((2 * rows, depth), own[-1].dtype),
            pltpu.SemaphoreType.DMA((many,)),
        ],
        compiler_params=params(),
        cost_estimate=cost(6 * rows * depth * columns, 8 * rows * depth + 4 * depth * columns),
        name="own_products",
    )(diag, right0, right1, *own, *got, *after)


def partial_kernel(many, given, diag, right0, right1, *refs):
    near, far = refs[:many], refs[many : 2 * many]
    out, passed = refs[-5 - given], refs[-4 - given : -4]
    held, steps, sems, hand_sems = refs[-4:]
    others = [
        pltpu.make_async_copy(x, y, hand_sems.at[i])
        for i, (x, y) in enumerate(zip(refs[2 * many : 2 * many + given], passed))
    ]

    @pl.when(pl.program_id(0) == 0)
    def _():
        for copy in others:
            copy.start()

    rows, wide = held.shape[0] // 2, right0.shape[1]
    step = pl.program_id(0)
    tiles = wide // BLOCK
    across = pl.num_programs(0) * tiles
    fetch_left(diag, near + far, far + near, held, sems)
    for which, values in enumerate(both_products(held, right0, right1)):
        top = jnp.maximum(jnp.max(jnp.abs(values), axis=0, keepdims=True), 1e-30)
        level = jnp.ceil(jnp.log(top) * (STEPS / LN2)) + 1.0
        coded = jnp.round(values * (LEVELS * jnp.exp(level * (-LN2 / STEPS))))
        coded = jnp.clip(coded, -32767.0, 32767.0).astype(jnp.int32).astype(jnp.int16)
        for t in range(tiles):
            at = which * across + step * tiles + t
            cut = slice(t * BLOCK, (t + 1) * BLOCK)
            out[pl.ds(pl.multiple_of(at * rows, rows), rows), :] = coded[:, cut]
            steps[pl.ds(at, 1), :] = level[:, cut]

    @pl.when(step == pl.num_programs(0) - 1)
    def _():
        tail = steps.shape[0]
        out[out.shape[0] - tail :, :] = steps[...].astype(jnp.int32).astype(jnp.int16)
        for copy in others:
            copy.wait()


def partial_products(diag, near, far, right0, right1, wide, given=(), gates=()):
    rows = sum(piece.shape[0] for piece in near)
    depth, columns = right0.shape
    tiles = 2 * columns // BLOCK
    tail = -(-tiles // 16) * 16
    return pl.pallas_call(
        functools.partial(partial_kernel, len(near), len(given)),
        grid=(columns // wide,),
        in_specs=[
            SM(),
            pl.BlockSpec((depth, wide), lambda g: (0, g)),
            pl.BlockSpec((depth, wide), lambda g: (0, g)),
        ]
        + [HB() for _ in (*near, *far, *given, *gates)],
        out_specs=[pl.BlockSpec((tiles * rows + tail, BLOCK), lambda g: (0, 0))]
        + [HB() for _ in given],
        out_shape=[jax.ShapeDtypeStruct((tiles * rows + tail, BLOCK), jnp.int16)]
        + [jax.ShapeDtypeStruct(x.shape, x.dtype) for x in given],
        scratch_shapes=[
            pltpu.VMEM((2 * rows, depth), near[0].dtype),
            pltpu.VMEM((tail, BLOCK), jnp.float32),
            pltpu.SemaphoreType.DMA((2 * len(near),)),
            pltpu.SemaphoreType.DMA((max(len(given), 1),)),
        ],
        compiler_params=params(),
        cost_estimate=cost(6 * rows * depth * columns, 4 * rows * depth + 4 * depth * columns),
        name="partial_products",
    )(diag, right0, right1, *near, *far, *given, *gates)


def finish_kernel(start, many, keep, coded, square, tangent, *rest):
    given, outs, passed = rest[:many], rest[-5 - many : -3 - many], rest[-3 - many : -3]
    made, out_sems, sems = rest[-3:]
    rows, columns = square.shape
    across = columns // BLOCK
    others = [
        pltpu.make_async_copy(x, y, sems.at[i]) for i, (x, y) in enumerate(zip(given, passed))
    ]
    results = [
        pltpu.make_async_copy(made.at[i], x.at[pl.ds(start, rows)], out_sems.at[i])
        for i, x in enumerate(outs)
    ]
    for copy in others:
        copy.start()
    tail = coded.shape[0] - 2 * across * rows
    levels = coded[coded.shape[0] - tail :, :].astype(jnp.int32).astype(jnp.float32)
    steps = jnp.exp(levels * (LN2 / STEPS)) * (1.0 / LEVELS)
    for which, mine in enumerate((square, tangent)):
        for j in range(across):
            tile = which * across + j
            cut = slice(j * BLOCK, (j + 1) * BLOCK)
            other = coded[tile * rows : (tile + 1) * rows, :].astype(jnp.int32).astype(jnp.float32)
            total = mine[:, cut] + other * steps[tile : tile + 1, :]
            for row_block, piece in row_pieces(start, rows):
                kept = total[piece] * keep[row_block, j].astype(jnp.float32)
                made[which, piece, cut] = kept.astype(made.dtype)
        results[which].start()
    for copy in results + others:
        copy.wait()


def finished(keep, square, tangent, coded, before, start, all_rows, held=(), after=()):
    rows, columns = square.shape
    out = jax.ShapeDtypeStruct((all_rows, columns), jnp.bfloat16)
    held, before = list(held), list(before)
    passed = [jax.ShapeDtypeStruct(x.shape, x.dtype) for x in held]
    many = len(held)
    return pl.pallas_call(
        functools.partial(finish_kernel, start, many),
        in_specs=[SM(), VM(), VM(), VM()] + [HB() for _ in (*held, *before, *after)],
        out_specs=[HB() for _ in range(2 + many)],
        out_shape=[out, out] + passed,
        input_output_aliases={4 + many: 0, 5 + many: 1} if before else {},
        scratch_shapes=[
            pltpu.VMEM((2, rows, columns), jnp.bfloat16),
            pltpu.SemaphoreType.DMA((2,)),
            pltpu.SemaphoreType.DMA((max(many, 1),)),
        ],
        compiler_params=params(),
        cost_estimate=cost(0, 16 * rows * columns),
        name="finish",
    )(keep, coded, square, tangent, *held, *before, *after)


def per_device_pair(
    n_row, x0_rows, x1_rows, x0_cols, x1_cols, mask0_rows, mask1_rows, mask0_cols, mask1_cols, keep
):
    n_col = 2
    group = n_row // n_col
    panel = x0_cols.shape[0]
    all_rows = x0_rows.shape[0]
    row_index = lax.axis_index("row")
    half = row_index // group
    diag = (half == lax.axis_index("col")).astype(jnp.int32).reshape(1)
    place = (row_index % group).astype(jnp.int32).reshape(1)
    split = all_rows * 7 // 16
    spans = ((0, split), (split, all_rows))
    wide = 256

    def device(h, q, c):
        return (h * group + q) * n_col + c

    spots = [(h, q, c) for h in range(2) for q in range(group) for c in range(2)]
    over_y = [(device(h, q, c), device(h, q, 1 - c)) for h, q, c in spots]
    over_z = [(device(h, q, c), device(1 - h, q, c)) for h, q, c in spots]
    ring = [
        (device(h, q, c), device(h, q, 1 - c) if h == c else device(1 - h, q, c))
        for h, q, c in spots
    ]
    across = [
        (device(h, q, c), device(h, q, c) if h == c else device(1 - h, q, 1 - c))
        for h, q, c in spots
    ]

    def move(values, pairs):
        return lax.ppermute(values, ("row", "col"), pairs)

    def chunk(i, limit, after=()):
        return masked_chunk(
            place, mask0_rows, mask1_rows, x0_rows, x1_rows, spans[i], panel, limit, after
        )

    def partials(near, far, **more):
        return partial_products(diag, (near,), (far,), right0, right1, wide, **more)

    def own(mine, other):
        return local_products(diag, mine, other, right0, right1, wide)

    a0, b0 = chunk(0, ALL_VMEM_BYTES)
    from_ring, from_across, got_b = move(a0, ring), move(b0, across), move(b0, over_y)
    a1, b1 = chunk(1, VMEM_BYTES, (a0,))
    right0, right1 = masked_right(mask0_cols, mask1_cols, x0_cols, x1_cols, (a1,))
    near, a1, b1 = chosen(diag, from_ring, from_across, (a1, b1), (right0, got_b))
    mine0, other0 = (a0, b0), (from_ring, got_b)
    from_ring, from_across = move(a1, ring), move(b1, across)
    coded, *_ = partials(near, move(near, over_y))
    near, coded = chosen(diag, from_ring, from_across, (coded,))
    back = move(coded, over_z)
    far = move(near, over_y)
    sums = own(mine0, other0)
    coded, b1 = partials(near, far, given=(b1,), gates=sums[:1])
    (coded,) = handed_on((coded,), (back,))
    outs = finished(keep, *sums, back, (), 0, all_rows)
    back = move(coded, over_z)
    sums = own((a1, b1), (from_ring, move(b1, over_y)))
    return tuple(finished(keep, *sums, back, outs, split, all_rows))


def passed_along(shard, axis, by):
    devices = lax.axis_size(axis)
    return lax.ppermute(shard, axis, [(i, (i + by) % devices) for i in range(devices)])


def masked(values, mask):
    rows_b, cols_b = mask.shape
    tiles = values.reshape(rows_b, BLOCK, cols_b, BLOCK)
    return (tiles * mask.astype(values.dtype)[:, None, :, None]).reshape(values.shape)


def per_device(
    x0_rows, x1_rows, x0_cols, x1_cols, mask0_rows, mask1_rows, mask0_cols, mask1_cols, keep_mask
):
    n_row = lax.axis_size("row")
    n_col = lax.axis_size("col")
    group = n_row // n_col
    row_index = lax.axis_index("row")
    col_index = lax.axis_index("col")
    panel = x0_cols.shape[0]
    start = row_index % group * panel
    block_start = row_index % group * (panel // BLOCK)
    left_zero = masked(
        lax.dynamic_slice_in_dim(x0_rows, start, panel, 1),
        lax.dynamic_slice_in_dim(mask0_rows, block_start, panel // BLOCK, 1),
    )
    left_one = masked(
        lax.dynamic_slice_in_dim(x1_rows, start, panel, 1),
        lax.dynamic_slice_in_dim(mask1_rows, block_start, panel // BLOCK, 1),
    )
    right_zero = masked(x0_cols, mask0_cols)
    right_one = masked(x1_cols, mask1_cols)
    left = jnp.stack([left_zero, left_one])
    right = jnp.stack([right_zero, right_one])
    left_offset = row_index // group % n_col
    right_offset = col_index % n_col
    levels = n_col.bit_length() - 1
    for level in range(levels):
        moved_left = passed_along(left, "col", -(1 << level))
        moved_right = passed_along(right, "row", -group * (1 << level))
        left = jnp.where(left_offset // (1 << level) % 2 == 1, moved_left, left)
        right = jnp.where(right_offset // (1 << level) % 2 == 1, moved_right, right)

    def accumulate(left_now, right_now, square, tangent):
        square = square + jnp.dot(left_now[0], right_now[0], preferred_element_type=jnp.float32)
        tangent = tangent + jnp.dot(left_now[0], right_now[1], preferred_element_type=jnp.float32)
        tangent = tangent + jnp.dot(left_now[1], right_now[0], preferred_element_type=jnp.float32)
        return (square, tangent)

    def section_body(section, carry):
        left_now, right_now, square, tangent = carry
        square, tangent = accumulate(left_now, right_now, square, tangent)
        left_now = passed_along(left_now, "col", -1)
        right_now = passed_along(right_now, "row", -group)
        return (left_now, right_now, square, tangent)

    zeros = jnp.zeros((left_zero.shape[0], right_zero.shape[1]), jnp.float32)
    left, right, square, tangent = lax.fori_loop(
        0, n_col - 1, section_body, (left, right, zeros, zeros)
    )
    square, tangent = accumulate(left, right, square, tangent)
    x_square = masked(square, keep_mask).astype(jnp.bfloat16)
    x_tangent = masked(tangent, keep_mask).astype(jnp.bfloat16)
    return (x_square, x_tangent)


def solution(mesh):
    if mesh.shape["col"] == 2:
        body = functools.partial(per_device_pair, mesh.shape["row"])
    else:
        body = per_device
    return jax.shard_map(
        body,
        mesh=mesh,
        in_specs=(P("row", "col"),) * 9,
        out_specs=(P("row", "col"), P("row", "col")),
        check_vma=False,
    )
```

```python
import functools
import math

import jax
import jax.numpy as jnp
from jax import lax
from jax.experimental import pallas as pl
from jax.experimental.pallas import tpu as pltpu
from jax.sharding import PartitionSpec as P

BLOCK = 128
LEVELS = 32000.0
STEPS = 32.0
LN2 = math.log(2.0)
VMEM_BYTES = 48 * 1024 * 1024
ALL_VMEM_BYTES = 62 * 1024 * 1024

VM = functools.partial(pl.BlockSpec, memory_space=pltpu.VMEM)
SM = functools.partial(pl.BlockSpec, memory_space=pltpu.SMEM)
HB = functools.partial(pl.BlockSpec, memory_space=pl.ANY)


def params(limit=VMEM_BYTES):
    return pltpu.CompilerParams(vmem_limit_bytes=limit)


def cost(flops, moved):
    return pl.CostEstimate(flops=int(flops) // 64, bytes_accessed=int(moved) // 64, transcendentals=0)


def scaled(values, entry):
    return (values.astype(jnp.float32) * entry.astype(jnp.float32)).astype(values.dtype)


def row_pieces(start, rows):
    edges = sorted({start, start + rows} | {e for e in range(0, start + rows, BLOCK) if e > start})
    return [(lo // BLOCK, slice(lo - start, hi - start)) for lo, hi in zip(edges, edges[1:])]


def chunk_kernel(spans, stacked, panel, *refs):
    place, mask0_far, mask1_far, x0, x1 = refs[:5]
    outs = refs[-5 - 2 * len(spans) + stacked : -5]
    held, mask0, mask1, mask_sems, sems = refs[-5:]
    start, rows = spans[0][0], held.shape[1]
    blocks = panel // BLOCK
    first = place[0] * blocks
    at = pl.ds(pl.multiple_of(place[0] * panel, BLOCK), panel)
    copies = [
        pltpu.make_async_copy(mask0_far, mask0, mask_sems.at[0]),
        pltpu.make_async_copy(mask1_far, mask1, mask_sems.at[1]),
        pltpu.make_async_copy(x0.at[pl.ds(start, rows), at], held.at[0], sems.at[0]),
        pltpu.make_async_copy(x1.at[pl.ds(start, rows), at], held.at[1], sems.at[1]),
    ]
    for copy in copies:
        copy.start()
    for copy in copies:
        copy.wait()
    for n, (lo, hi) in enumerate(spans):
        for which, mask in enumerate((mask0, mask1)):
            joint = stacked and n == 0
            out = outs[0] if joint else outs[2 * n - stacked + which]
            down = which * (hi - lo) if joint else 0
            for row_block, part in row_pieces(lo, hi - lo):
                source = slice(part.start + lo - start, part.stop + lo - start)
                target = slice(part.start + down, part.stop + down)
                for j in range(blocks):
                    cut = slice(j * BLOCK, (j + 1) * BLOCK)
                    values = scaled(held[which, source, cut], mask[row_block, first + j])
                    out[target, cut] = values


def masked_chunks(place, mask0, mask1, x0, x1, spans, stacked, panel, limit, after=()):
    rows = spans[-1][1] - spans[0][0]
    outs = []
    for n, (lo, hi) in enumerate(spans):
        if stacked and n == 0:
            outs.append(jax.ShapeDtypeStruct((2 * (hi - lo), panel), x0.dtype))
        else:
            outs += [jax.ShapeDtypeStruct((hi - lo, panel), x0.dtype)] * 2
    return pl.pallas_call(
        functools.partial(chunk_kernel, spans, int(stacked), panel),
        in_specs=[SM()] + [HB() for _ in range(4 + len(after))],
        out_specs=[VM() for _ in outs],
        out_shape=outs,
        scratch_shapes=[
            pltpu.VMEM((2, rows, panel), x0.dtype),
            pltpu.SMEM(mask0.shape, mask0.dtype),
            pltpu.SMEM(mask1.shape, mask1.dtype),
            pltpu.SemaphoreType.DMA((2,)),
            pltpu.SemaphoreType.DMA((2,)),
        ],
        compiler_params=params(limit),
        cost_estimate=cost(0, 8 * rows * panel),
        name="left_chunks",
    )(place, mask0, mask1, x0, x1, *after)


def choose_kernel(gates, many, diag, *refs):
    one, other = refs[gates : gates + 2]
    held, outs, sems = refs[gates + 2 : gates + 2 + many], refs[-many - 2 : -1], refs[-1]
    others = [
        pltpu.make_async_copy(x, out, sems.at[1 + i])
        for i, (x, out) in enumerate(zip(held, outs[1:]))
    ]
    for copy in others:
        copy.start()

    @pl.when(diag[0] == 1)
    def _():
        copy = pltpu.make_async_copy(one, outs[0], sems.at[0])
        copy.start()
        copy.wait()

    @pl.when(diag[0] == 0)
    def _():
        copy = pltpu.make_async_copy(other, outs[0], sems.at[0])
        copy.start()
        copy.wait()

    for copy in others:
        copy.wait()


def chosen(diag, one, other, held=(), after=()):
    outs = [jax.ShapeDtypeStruct(x.shape, x.dtype) for x in (one, *held)]
    return pl.pallas_call(
        functools.partial(choose_kernel, len(after), len(held)),
        in_specs=[SM()] + [HB() for _ in (*after, one, other, *held)],
        out_specs=[HB() for _ in outs],
        out_shape=outs,
        scratch_shapes=[pltpu.SemaphoreType.DMA((len(outs),))],
        compiler_params=params(),
        cost_estimate=cost(0, 4 * one.size),
        name="to_send",
    )(diag, *after, one, other, *held)


def hand_kernel(many, *refs):
    sems = refs[-1]
    copies = [
        pltpu.make_async_copy(refs[i], refs[i - many - 1], sems.at[i]) for i in range(many)
    ]
    for copy in copies:
        copy.start()
    for copy in copies:
        copy.wait()


def handed_on(values, gates):
    outs = [jax.ShapeDtypeStruct(x.shape, x.dtype) for x in values]
    return pl.pallas_call(
        functools.partial(hand_kernel, len(values)),
        in_specs=[HB() for _ in (*values, *gates)],
        out_specs=[HB() for _ in outs],
        out_shape=outs,
        scratch_shapes=[pltpu.SemaphoreType.DMA((len(outs),))],
        compiler_params=params(),
        cost_estimate=cost(0, 4 * sum(x.size for x in values)),
        name="handed_on",
    )(*values, *gates)


def right_kernel(mask0, mask1, x0, x1, *rest):
    out0, out1 = rest[-2:]
    step = pl.program_id(0)
    many = x0.shape[0] // BLOCK
    for i in range(many):
        for j in range(x0.shape[1] // BLOCK):
            at = (slice(i * BLOCK, (i + 1) * BLOCK), slice(j * BLOCK, (j + 1) * BLOCK))
            out0[at] = scaled(x0[at], mask0[step * many + i, j])
            out1[at] = scaled(x1[at], mask1[step * many + i, j])


def masked_right(mask0, mask1, x0, x1, after=()):
    depth, columns = x0.shape
    tall = 2 * BLOCK
    out = jax.ShapeDtypeStruct(x0.shape, x0.dtype)
    tile = pl.BlockSpec((tall, columns), lambda g: (g, 0))
    return pl.pallas_call(
        right_kernel,
        grid=(depth // tall,),
        in_specs=[SM(), SM(), tile, tile] + [HB() for _ in after],
        out_specs=[tile, tile],
        out_shape=[out, out],
        compiler_params=params(),
        cost_estimate=cost(0, 8 * depth * columns),
        name="right_panels",
    )(mask0, mask1, x0, x1, *after)


def both_products(held, right0, right1):
    rows = held.shape[0] // 2
    first = jnp.dot(held[...], right0[...], preferred_element_type=jnp.float32)
    second = jnp.dot(held[:rows], right1[...], preferred_element_type=jnp.float32)
    return first[:rows], first[rows:] + second


def piece(array, lo=0, hi=None):
    return (array, lo, array.shape[0] if hi is None else hi)


def numbered(one, other):
    arrays = []
    for array, _, _ in (*one, *other):
        if all(array is not known for known in arrays):
            arrays.append(array)
    number = {id(array): i for i, array in enumerate(arrays)}
    return arrays, *(
        tuple((number[id(array)], lo, hi) for array, lo, hi in pieces) for pieces in (one, other)
    )


def fetched(pieces, refs, held, sems):
    copies = []
    top = 0
    for i, (which, lo, hi) in enumerate(pieces):
        source = refs[which].at[pl.ds(lo, hi - lo)]
        copies.append(pltpu.make_async_copy(source, held.at[pl.ds(top, hi - lo)], sems.at[i]))
        top += hi - lo
    for copy in copies:
        copy.start()
    for copy in copies:
        copy.wait()


def fetch_left(diag, one, other, refs, held, sems):
    first = pl.program_id(0) == 0

    @pl.when(first & (diag[0] == 1))
    def _():
        fetched(one, refs, held, sems)

    @pl.when(first & (diag[0] == 0))
    def _():
        fetched(other, refs, held, sems)


def local_kernel(one, other, diag, right0, right1, *refs):
    square, tangent, held, sems = refs[-4:]
    fetch_left(diag, one, other, refs, held, sems)
    square[...], tangent[...] = both_products(held, right0, right1)


def local_products(diag, one, other, right0, right1, wide):
    arrays, one, other = numbered(one, other)
    rows = sum(hi - lo for _, lo, hi in one) // 2
    depth, columns = right0.shape
    out = jax.ShapeDtypeStruct((rows, columns), jnp.float32)
    tile = pl.BlockSpec((rows, wide), lambda g: (0, g))
    return pl.pallas_call(
        functools.partial(local_kernel, one, other),
        grid=(columns // wide,),
        in_specs=[
            SM(),
            pl.BlockSpec((depth, wide), lambda g: (0, g)),
            pl.BlockSpec((depth, wide), lambda g: (0, g)),
        ]
        + [HB() for _ in arrays],
        out_specs=[tile, tile],
        out_shape=[out, out],
        scratch_shapes=[
            pltpu.VMEM((2 * rows, depth), right0.dtype),
            pltpu.SemaphoreType.DMA((len(one),)),
        ],
        compiler_params=params(),
        cost_estimate=cost(6 * rows * depth * columns, 8 * rows * depth + 4 * depth * columns),
        name="own_products",
    )(diag, right0, right1, *arrays)


def partial_kernel(one, other, many, given, diag, right0, right1, *refs):
    out, passed = refs[-5 - given], refs[-4 - given : -4]
    held, steps, sems, hand_sems = refs[-4:]
    others = [
        pltpu.make_async_copy(x, y, hand_sems.at[i])
        for i, (x, y) in enumerate(zip(refs[many : many + given], passed))
    ]

    @pl.when(pl.program_id(0) == 0)
    def _():
        for copy in others:
            copy.start()

    rows, wide = held.shape[0] // 2, right0.shape[1]
    step = pl.program_id(0)
    tiles = wide // BLOCK
    across = pl.num_programs(0) * tiles
    fetch_left(diag, one, other, refs, held, sems)
    for which, values in enumerate(both_products(held, right0, right1)):
        top = jnp.maximum(jnp.max(jnp.abs(values), axis=0, keepdims=True), 1e-30)
        level = jnp.ceil(jnp.log(top) * (STEPS / LN2)) + 1.0
        coded = jnp.round(values * (LEVELS * jnp.exp(level * (-LN2 / STEPS))))
        coded = jnp.clip(coded, -32767.0, 32767.0).astype(jnp.int32).astype(jnp.int16)
        for t in range(tiles):
            at = which * across + step * tiles + t
            cut = slice(t * BLOCK, (t + 1) * BLOCK)
            out[pl.ds(pl.multiple_of(at * rows, rows), rows), :] = coded[:, cut]
            steps[pl.ds(at, 1), :] = level[:, cut]

    @pl.when(step == pl.num_programs(0) - 1)
    def _():
        tail = steps.shape[0]
        out[out.shape[0] - tail :, :] = steps[...].astype(jnp.int32).astype(jnp.int16)
        for copy in others:
            copy.wait()


def partial_products(diag, one, other, right0, right1, wide, given=(), gates=()):
    arrays, one, other = numbered(one, other)
    rows = sum(hi - lo for _, lo, hi in one) // 2
    depth, columns = right0.shape
    tiles = 2 * columns // BLOCK
    tail = -(-tiles // 16) * 16
    return pl.pallas_call(
        functools.partial(partial_kernel, one, other, len(arrays), len(given)),
        grid=(columns // wide,),
        in_specs=[
            SM(),
            pl.BlockSpec((depth, wide), lambda g: (0, g)),
            pl.BlockSpec((depth, wide), lambda g: (0, g)),
        ]
        + [HB() for _ in (*arrays, *given, *gates)],
        out_specs=[pl.BlockSpec((tiles * rows + tail, BLOCK), lambda g: (0, 0))]
        + [HB() for _ in given],
        out_shape=[jax.ShapeDtypeStruct((tiles * rows + tail, BLOCK), jnp.int16)]
        + [jax.ShapeDtypeStruct(x.shape, x.dtype) for x in given],
        scratch_shapes=[
            pltpu.VMEM((2 * rows, depth), right0.dtype),
            pltpu.VMEM((tail, BLOCK), jnp.float32),
            pltpu.SemaphoreType.DMA((len(one),)),
            pltpu.SemaphoreType.DMA((max(len(given), 1),)),
        ],
        compiler_params=params(),
        cost_estimate=cost(6 * rows * depth * columns, 4 * rows * depth + 4 * depth * columns),
        name="partial_products",
    )(diag, right0, right1, *arrays, *given, *gates)


def finish_kernel(start, many, keep, coded, square, tangent, *rest):
    given, outs, passed = rest[:many], rest[-5 - many : -3 - many], rest[-3 - many : -3]
    made, out_sems, sems = rest[-3:]
    rows, columns = square.shape
    across = columns // BLOCK
    others = [
        pltpu.make_async_copy(x, y, sems.at[i]) for i, (x, y) in enumerate(zip(given, passed))
    ]
    results = [
        pltpu.make_async_copy(made.at[i], x.at[pl.ds(start, rows)], out_sems.at[i])
        for i, x in enumerate(outs)
    ]
    for copy in others:
        copy.start()
    tail = coded.shape[0] - 2 * across * rows
    levels = coded[coded.shape[0] - tail :, :].astype(jnp.int32).astype(jnp.float32)
    steps = jnp.exp(levels * (LN2 / STEPS)) * (1.0 / LEVELS)
    for which, mine in enumerate((square, tangent)):
        for j in range(across):
            tile = which * across + j
            cut = slice(j * BLOCK, (j + 1) * BLOCK)
            other = coded[tile * rows : (tile + 1) * rows, :].astype(jnp.int32).astype(jnp.float32)
            total = mine[:, cut] + other * steps[tile : tile + 1, :]
            for row_block, part in row_pieces(start, rows):
                kept = total[part] * keep[row_block, j].astype(jnp.float32)
                made[which, part, cut] = kept.astype(made.dtype)
        results[which].start()
    for copy in results + others:
        copy.wait()


def finished(keep, square, tangent, coded, before, start, all_rows, held=(), after=()):
    rows, columns = square.shape
    out = jax.ShapeDtypeStruct((all_rows, columns), jnp.bfloat16)
    held, before = list(held), list(before)
    passed = [jax.ShapeDtypeStruct(x.shape, x.dtype) for x in held]
    many = len(held)
    return pl.pallas_call(
        functools.partial(finish_kernel, start, many),
        in_specs=[SM(), VM(), VM(), VM()] + [HB() for _ in (*held, *before, *after)],
        out_specs=[HB() for _ in range(2 + many)],
        out_shape=[out, out] + passed,
        input_output_aliases={4 + many: 0, 5 + many: 1} if before else {},
        scratch_shapes=[
            pltpu.VMEM((2, rows, columns), jnp.bfloat16),
            pltpu.SemaphoreType.DMA((2,)),
            pltpu.SemaphoreType.DMA((max(many, 1),)),
        ],
        compiler_params=params(),
        cost_estimate=cost(0, 16 * rows * columns),
        name="finish",
    )(keep, coded, square, tangent, *held, *before, *after)


def per_device_pair(
    n_row, x0_rows, x1_rows, x0_cols, x1_cols, mask0_rows, mask1_rows, mask0_cols, mask1_cols, keep
):
    n_col = 2
    group = n_row // n_col
    panel = x0_cols.shape[0]
    all_rows = x0_rows.shape[0]
    row_index = lax.axis_index("row")
    half = row_index // group
    diag = (half == lax.axis_index("col")).astype(jnp.int32).reshape(1)
    place = (row_index % group).astype(jnp.int32).reshape(1)
    direct = all_rows // 8
    split = all_rows // 2
    wide = 256

    def device(h, q, c):
        return (h * group + q) * n_col + c

    spots = [(h, q, c) for h in range(2) for q in range(group) for c in range(2)]
    over_y = [(device(h, q, c), device(h, q, 1 - c)) for h, q, c in spots]
    over_z = [(device(h, q, c), device(1 - h, q, c)) for h, q, c in spots]
    ring = [
        (device(h, q, c), device(h, q, 1 - c) if h == c else device(1 - h, q, c))
        for h, q, c in spots
    ]
    def move(values, pairs):
        return lax.ppermute(values, ("row", "col"), pairs)

    def chunks(spans, stacked, limit, after=()):
        inputs = (place, mask0_rows, mask1_rows, x0_rows, x1_rows)
        return masked_chunks(*inputs, spans, stacked, panel, limit, after)

    def partials(one, other, **more):
        return partial_products(diag, one, other, right0, right1, wide, **more)

    def own(one, other):
        return local_products(diag, one, other, right0, right1, wide)

    def parts(joint, a, b):
        top, low = piece(joint, 0, direct), piece(joint, direct)
        return (top, piece(a), low, piece(b))

    joint, a1, b1 = chunks(((0, direct), (direct, split)), True, ALL_VMEM_BYTES)
    passed1 = move(b1, over_y)
    near0 = move(joint, ring)
    a2, b2 = chunks(((split, all_rows),), False, VMEM_BYTES, (a1,))
    right0, right1 = masked_right(mask0_cols, mask1_cols, x0_cols, x1_cols, (a2,))
    send, b2 = chosen(diag, passed1, a1, (b2,), (near0, right0))
    near1 = move(send, over_z)
    passed2 = move(b2, over_y)
    far0 = move(near0, over_y)
    send, a1 = chosen(diag, passed2, a2, (a1,), (far0,))
    near2 = move(send, over_z)
    got1 = move(a1, over_y)
    far1 = move(near1, over_y)
    (coded,) = partials(parts(near0, near1, far1), parts(far0, far1, near1))
    coded, near2 = handed_on((coded, near2), (got1,))
    back = move(coded, over_z)
    far2 = move(near2, over_y)
    sums = own(parts(joint, a1, b1), parts(near0, got1, passed1))
    coded, a2 = partials(
        (piece(near2), piece(far2)), (piece(far2), piece(near2)), given=(a2,), gates=sums[:1]
    )
    (coded,) = handed_on((coded,), (back,))
    outs = finished(keep, *sums, back, (), 0, all_rows)
    back = move(coded, over_z)
    got2 = move(a2, over_y)
    sums = own((piece(a2), piece(b2)), (piece(got2), piece(passed2)))
    return tuple(finished(keep, *sums, back, outs, split, all_rows))


def passed_along(shard, axis, by):
    devices = lax.axis_size(axis)
    return lax.ppermute(shard, axis, [(i, (i + by) % devices) for i in range(devices)])


def masked(values, mask):
    rows_b, cols_b = mask.shape
    tiles = values.reshape(rows_b, BLOCK, cols_b, BLOCK)
    return (tiles * mask.astype(values.dtype)[:, None, :, None]).reshape(values.shape)


def per_device(
    x0_rows, x1_rows, x0_cols, x1_cols, mask0_rows, mask1_rows, mask0_cols, mask1_cols, keep_mask
):
    n_row = lax.axis_size("row")
    n_col = lax.axis_size("col")
    group = n_row // n_col
    row_index = lax.axis_index("row")
    col_index = lax.axis_index("col")
    panel = x0_cols.shape[0]
    start = row_index % group * panel
    block_start = row_index % group * (panel // BLOCK)
    left_zero = masked(
        lax.dynamic_slice_in_dim(x0_rows, start, panel, 1),
        lax.dynamic_slice_in_dim(mask0_rows, block_start, panel // BLOCK, 1),
    )
    left_one = masked(
        lax.dynamic_slice_in_dim(x1_rows, start, panel, 1),
        lax.dynamic_slice_in_dim(mask1_rows, block_start, panel // BLOCK, 1),
    )
    right_zero = masked(x0_cols, mask0_cols)
    right_one = masked(x1_cols, mask1_cols)
    left = jnp.stack([left_zero, left_one])
    right = jnp.stack([right_zero, right_one])
    left_offset = row_index // group % n_col
    right_offset = col_index % n_col
    levels = n_col.bit_length() - 1
    for level in range(levels):
        moved_left = passed_along(left, "col", -(1 << level))
        moved_right = passed_along(right, "row", -group * (1 << level))
        left = jnp.where(left_offset // (1 << level) % 2 == 1, moved_left, left)
        right = jnp.where(right_offset // (1 << level) % 2 == 1, moved_right, right)

    def accumulate(left_now, right_now, square, tangent):
        square = square + jnp.dot(left_now[0], right_now[0], preferred_element_type=jnp.float32)
        tangent = tangent + jnp.dot(left_now[0], right_now[1], preferred_element_type=jnp.float32)
        tangent = tangent + jnp.dot(left_now[1], right_now[0], preferred_element_type=jnp.float32)
        return (square, tangent)

    def section_body(section, carry):
        left_now, right_now, square, tangent = carry
        square, tangent = accumulate(left_now, right_now, square, tangent)
        left_now = passed_along(left_now, "col", -1)
        right_now = passed_along(right_now, "row", -group)
        return (left_now, right_now, square, tangent)

    zeros = jnp.zeros((left_zero.shape[0], right_zero.shape[1]), jnp.float32)
    left, right, square, tangent = lax.fori_loop(
        0, n_col - 1, section_body, (left, right, zeros, zeros)
    )
    square, tangent = accumulate(left, right, square, tangent)
    x_square = masked(square, keep_mask).astype(jnp.bfloat16)
    x_tangent = masked(tangent, keep_mask).astype(jnp.bfloat16)
    return (x_square, x_tangent)


def solution(mesh):
    if mesh.shape["col"] == 2:
        body = functools.partial(per_device_pair, mesh.shape["row"])
    else:
        body = per_device
    return jax.shard_map(
        body,
        mesh=mesh,
        in_specs=(P("row", "col"),) * 9,
        out_specs=(P("row", "col"), P("row", "col")),
        check_vma=False,
    )
```

```python
import functools
import math

import jax
import jax.numpy as jnp
from jax import lax
from jax.experimental import pallas as pl
from jax.experimental.pallas import tpu as pltpu
from jax.sharding import PartitionSpec as P

BLOCK = 128
LEVELS = 32000.0
STEPS = 32.0
LN2 = math.log(2.0)
VMEM_BYTES = 48 * 1024 * 1024
ALL_VMEM_BYTES = 62 * 1024 * 1024

VM = functools.partial(pl.BlockSpec, memory_space=pltpu.VMEM)
SM = functools.partial(pl.BlockSpec, memory_space=pltpu.SMEM)
HB = functools.partial(pl.BlockSpec, memory_space=pl.ANY)


def params(limit=VMEM_BYTES):
    return pltpu.CompilerParams(vmem_limit_bytes=limit)


def cost(flops, moved):
    return pl.CostEstimate(flops=int(flops) // 64, bytes_accessed=int(moved) // 64, transcendentals=0)


def scaled(values, entry):
    return (values.astype(jnp.float32) * entry.astype(jnp.float32)).astype(values.dtype)


def row_pieces(start, rows):
    edges = sorted({start, start + rows} | {e for e in range(0, start + rows, BLOCK) if e > start})
    return [(lo // BLOCK, slice(lo - start, hi - start)) for lo, hi in zip(edges, edges[1:])]


def chunk_kernel(spans, stacked, panel, *refs):
    place, mask0_far, mask1_far, x0, x1 = refs[:5]
    outs = refs[-5 - 2 * len(spans) + stacked : -5]
    held, mask0, mask1, mask_sems, sems = refs[-5:]
    start, rows = spans[0][0], held.shape[1]
    blocks = panel // BLOCK
    first = place[0] * blocks
    at = pl.ds(pl.multiple_of(place[0] * panel, BLOCK), panel)
    copies = [
        pltpu.make_async_copy(mask0_far, mask0, mask_sems.at[0]),
        pltpu.make_async_copy(mask1_far, mask1, mask_sems.at[1]),
        pltpu.make_async_copy(x0.at[pl.ds(start, rows), at], held.at[0], sems.at[0]),
        pltpu.make_async_copy(x1.at[pl.ds(start, rows), at], held.at[1], sems.at[1]),
    ]
    for copy in copies:
        copy.start()
    for copy in copies:
        copy.wait()
    for n, (lo, hi) in enumerate(spans):
        for which, mask in enumerate((mask0, mask1)):
            joint = stacked and n == 0
            out = outs[0] if joint else outs[2 * n - stacked + which]
            down = which * (hi - lo) if joint else 0
            for row_block, part in row_pieces(lo, hi - lo):
                source = slice(part.start + lo - start, part.stop + lo - start)
                target = slice(part.start + down, part.stop + down)
                for j in range(blocks):
                    cut = slice(j * BLOCK, (j + 1) * BLOCK)
                    values = scaled(held[which, source, cut], mask[row_block, first + j])
                    out[target, cut] = values


def masked_chunks(place, mask0, mask1, x0, x1, spans, stacked, panel, limit, after=()):
    rows = spans[-1][1] - spans[0][0]
    outs = []
    for n, (lo, hi) in enumerate(spans):
        if stacked and n == 0:
            outs.append(jax.ShapeDtypeStruct((2 * (hi - lo), panel), x0.dtype))
        else:
            outs += [jax.ShapeDtypeStruct((hi - lo, panel), x0.dtype)] * 2
    return pl.pallas_call(
        functools.partial(chunk_kernel, spans, int(stacked), panel),
        in_specs=[SM()] + [HB() for _ in range(4 + len(after))],
        out_specs=[VM() for _ in outs],
        out_shape=outs,
        scratch_shapes=[
            pltpu.VMEM((2, rows, panel), x0.dtype),
            pltpu.SMEM(mask0.shape, mask0.dtype),
            pltpu.SMEM(mask1.shape, mask1.dtype),
            pltpu.SemaphoreType.DMA((2,)),
            pltpu.SemaphoreType.DMA((2,)),
        ],
        compiler_params=params(limit),
        cost_estimate=cost(0, 8 * rows * panel),
        name="left_chunks",
    )(place, mask0, mask1, x0, x1, *after)


def choose_kernel(gates, many, diag, *refs):
    one, other = refs[gates : gates + 2]
    held, outs, sems = refs[gates + 2 : gates + 2 + many], refs[-many - 2 : -1], refs[-1]
    others = [
        pltpu.make_async_copy(x, out, sems.at[1 + i])
        for i, (x, out) in enumerate(zip(held, outs[1:]))
    ]
    for copy in others:
        copy.start()

    @pl.when(diag[0] == 1)
    def _():
        copy = pltpu.make_async_copy(one, outs[0], sems.at[0])
        copy.start()
        copy.wait()

    @pl.when(diag[0] == 0)
    def _():
        copy = pltpu.make_async_copy(other, outs[0], sems.at[0])
        copy.start()
        copy.wait()

    for copy in others:
        copy.wait()


def chosen(diag, one, other, held=(), after=()):
    outs = [jax.ShapeDtypeStruct(x.shape, x.dtype) for x in (one, *held)]
    return pl.pallas_call(
        functools.partial(choose_kernel, len(after), len(held)),
        in_specs=[SM()] + [HB() for _ in (*after, one, other, *held)],
        out_specs=[HB() for _ in outs],
        out_shape=outs,
        scratch_shapes=[pltpu.SemaphoreType.DMA((len(outs),))],
        compiler_params=params(),
        cost_estimate=cost(0, 4 * one.size),
        name="to_send",
    )(diag, *after, one, other, *held)


def hand_kernel(many, *refs):
    sems = refs[-1]
    copies = [
        pltpu.make_async_copy(refs[i], refs[i - many - 1], sems.at[i]) for i in range(many)
    ]
    for copy in copies:
        copy.start()
    for copy in copies:
        copy.wait()


def handed_on(values, gates):
    outs = [jax.ShapeDtypeStruct(x.shape, x.dtype) for x in values]
    return pl.pallas_call(
        functools.partial(hand_kernel, len(values)),
        in_specs=[HB() for _ in (*values, *gates)],
        out_specs=[HB() for _ in outs],
        out_shape=outs,
        scratch_shapes=[pltpu.SemaphoreType.DMA((len(outs),))],
        compiler_params=params(),
        cost_estimate=cost(0, 4 * sum(x.size for x in values)),
        name="handed_on",
    )(*values, *gates)


def right_kernel(mask0, mask1, x0, x1, *rest):
    out0, out1 = rest[-2:]
    step = pl.program_id(0)
    many = x0.shape[0] // BLOCK
    for i in range(many):
        for j in range(x0.shape[1] // BLOCK):
            at = (slice(i * BLOCK, (i + 1) * BLOCK), slice(j * BLOCK, (j + 1) * BLOCK))
            out0[at] = scaled(x0[at], mask0[step * many + i, j])
            out1[at] = scaled(x1[at], mask1[step * many + i, j])


def masked_right(mask0, mask1, x0, x1, after=()):
    depth, columns = x0.shape
    tall = 2 * BLOCK
    out = jax.ShapeDtypeStruct(x0.shape, x0.dtype)
    tile = pl.BlockSpec((tall, columns), lambda g: (g, 0))
    return pl.pallas_call(
        right_kernel,
        grid=(depth // tall,),
        in_specs=[SM(), SM(), tile, tile] + [HB() for _ in after],
        out_specs=[tile, tile],
        out_shape=[out, out],
        compiler_params=params(),
        cost_estimate=cost(0, 8 * depth * columns),
        name="right_panels",
    )(mask0, mask1, x0, x1, *after)


def both_products(held, right0, right1):
    rows = held.shape[0] // 2
    first = jnp.dot(held[...], right0[...], preferred_element_type=jnp.float32)
    second = jnp.dot(held[:rows], right1[...], preferred_element_type=jnp.float32)
    return first[:rows], first[rows:] + second


def piece(array, lo=0, hi=None):
    return (array, lo, array.shape[0] if hi is None else hi)


def numbered(one, other):
    arrays = []
    for array, _, _ in (*one, *other):
        if all(array is not known for known in arrays):
            arrays.append(array)
    number = {id(array): i for i, array in enumerate(arrays)}
    return arrays, *(
        tuple((number[id(array)], lo, hi) for array, lo, hi in pieces) for pieces in (one, other)
    )


def fetched(pieces, refs, held, sems):
    copies = []
    top = 0
    for i, (which, lo, hi) in enumerate(pieces):
        source = refs[which].at[pl.ds(lo, hi - lo)]
        copies.append(pltpu.make_async_copy(source, held.at[pl.ds(top, hi - lo)], sems.at[i]))
        top += hi - lo
    for copy in copies:
        copy.start()
    for copy in copies:
        copy.wait()


def fetch_left(diag, one, other, refs, held, sems):
    first = pl.program_id(0) == 0

    @pl.when(first & (diag[0] == 1))
    def _():
        fetched(one, refs, held, sems)

    @pl.when(first & (diag[0] == 0))
    def _():
        fetched(other, refs, held, sems)


def local_kernel(one, other, diag, right0, right1, *refs):
    square, tangent, held, sems = refs[-4:]
    fetch_left(diag, one, other, refs, held, sems)
    square[...], tangent[...] = both_products(held, right0, right1)


def local_products(diag, one, other, right0, right1, wide):
    arrays, one, other = numbered(one, other)
    rows = sum(hi - lo for _, lo, hi in one) // 2
    depth, columns = right0.shape
    out = jax.ShapeDtypeStruct((rows, columns), jnp.float32)
    tile = pl.BlockSpec((rows, wide), lambda g: (0, g))
    return pl.pallas_call(
        functools.partial(local_kernel, one, other),
        grid=(columns // wide,),
        in_specs=[
            SM(),
            pl.BlockSpec((depth, wide), lambda g: (0, g)),
            pl.BlockSpec((depth, wide), lambda g: (0, g)),
        ]
        + [HB() for _ in arrays],
        out_specs=[tile, tile],
        out_shape=[out, out],
        scratch_shapes=[
            pltpu.VMEM((2 * rows, depth), right0.dtype),
            pltpu.SemaphoreType.DMA((max(len(one), len(other)),)),
        ],
        compiler_params=params(),
        cost_estimate=cost(6 * rows * depth * columns, 8 * rows * depth + 4 * depth * columns),
        name="own_products",
    )(diag, right0, right1, *arrays)


def partial_kernel(one, other, many, cuts, diag, right0, right1, *refs):
    given = len(cuts)
    out, passed = refs[-5 - given], refs[-4 - given : -4]
    held, steps, sems, hand_sems = refs[-4:]
    others = [
        pltpu.make_async_copy(x.at[pl.ds(lo, hi - lo)], y, hand_sems.at[i])
        for i, (x, y, (lo, hi)) in enumerate(zip(refs[many : many + given], passed, cuts))
    ]

    @pl.when(pl.program_id(0) == 0)
    def _():
        for copy in others:
            copy.start()

    rows, wide = held.shape[0] // 2, right0.shape[1]
    step = pl.program_id(0)
    tiles = wide // BLOCK
    across = pl.num_programs(0) * tiles
    fetch_left(diag, one, other, refs, held, sems)
    for which, values in enumerate(both_products(held, right0, right1)):
        top = jnp.maximum(jnp.max(jnp.abs(values), axis=0, keepdims=True), 1e-30)
        level = jnp.ceil(jnp.log(top) * (STEPS / LN2)) + 1.0
        coded = jnp.round(values * (LEVELS * jnp.exp(level * (-LN2 / STEPS))))
        coded = jnp.clip(coded, -32767.0, 32767.0).astype(jnp.int32).astype(jnp.int16)
        for t in range(tiles):
            at = which * across + step * tiles + t
            cut = slice(t * BLOCK, (t + 1) * BLOCK)
            out[pl.ds(pl.multiple_of(at * rows, rows), rows), :] = coded[:, cut]
            steps[pl.ds(at, 1), :] = level[:, cut]

    @pl.when(step == pl.num_programs(0) - 1)
    def _():
        tail = steps.shape[0]
        out[out.shape[0] - tail :, :] = steps[...].astype(jnp.int32).astype(jnp.int16)
        for copy in others:
            copy.wait()


def partial_products(diag, one, other, right0, right1, wide, given=(), gates=()):
    arrays, one, other = numbered(one, other)
    rows = sum(hi - lo for _, lo, hi in one) // 2
    depth, columns = right0.shape
    tiles = 2 * columns // BLOCK
    tail = -(-tiles // 16) * 16
    return pl.pallas_call(
        functools.partial(partial_kernel, one, other, len(arrays), [cut for _, *cut in given]),
        grid=(columns // wide,),
        in_specs=[
            SM(),
            pl.BlockSpec((depth, wide), lambda g: (0, g)),
            pl.BlockSpec((depth, wide), lambda g: (0, g)),
        ]
        + [HB() for _ in (*arrays, *given, *gates)],
        out_specs=[pl.BlockSpec((tiles * rows + tail, BLOCK), lambda g: (0, 0))]
        + [HB() for _ in given],
        out_shape=[jax.ShapeDtypeStruct((tiles * rows + tail, BLOCK), jnp.int16)]
        + [jax.ShapeDtypeStruct((hi - lo, x.shape[1]), x.dtype) for x, lo, hi in given],
        scratch_shapes=[
            pltpu.VMEM((2 * rows, depth), right0.dtype),
            pltpu.VMEM((tail, BLOCK), jnp.float32),
            pltpu.SemaphoreType.DMA((max(len(one), len(other)),)),
            pltpu.SemaphoreType.DMA((max(len(given), 1),)),
        ],
        compiler_params=params(),
        cost_estimate=cost(6 * rows * depth * columns, 4 * rows * depth + 4 * depth * columns),
        name="partial_products",
    )(diag, right0, right1, *arrays, *(x for x, _, _ in given), *gates)


def finish_kernel(start, cuts, keep, coded, square, tangent, *rest):
    many = len(cuts)
    given, outs, passed = rest[:many], rest[-5 - many : -3 - many], rest[-3 - many : -3]
    made, out_sems, sems = rest[-3:]
    rows, columns = square.shape
    across = columns // BLOCK
    others = [
        pltpu.make_async_copy(x.at[pl.ds(lo, hi - lo)], y, sems.at[i])
        for i, (x, y, (lo, hi)) in enumerate(zip(given, passed, cuts))
    ]
    results = [
        pltpu.make_async_copy(made.at[i], x.at[pl.ds(start, rows)], out_sems.at[i])
        for i, x in enumerate(outs)
    ]
    for copy in others:
        copy.start()
    tail = coded.shape[0] - 2 * across * rows
    levels = coded[coded.shape[0] - tail :, :].astype(jnp.int32).astype(jnp.float32)
    steps = jnp.exp(levels * (LN2 / STEPS)) * (1.0 / LEVELS)
    for which, mine in enumerate((square, tangent)):
        for j in range(across):
            tile = which * across + j
            cut = slice(j * BLOCK, (j + 1) * BLOCK)
            other = coded[tile * rows : (tile + 1) * rows, :].astype(jnp.int32).astype(jnp.float32)
            total = mine[:, cut] + other * steps[tile : tile + 1, :]
            for row_block, part in row_pieces(start, rows):
                kept = total[part] * keep[row_block, j].astype(jnp.float32)
                made[which, part, cut] = kept.astype(made.dtype)
        results[which].start()
    for copy in results + others:
        copy.wait()


def finished(keep, square, tangent, coded, before, start, all_rows, held=(), after=()):
    rows, columns = square.shape
    out = jax.ShapeDtypeStruct((all_rows, columns), jnp.bfloat16)
    held, before = list(held), list(before)
    passed = [jax.ShapeDtypeStruct((hi - lo, x.shape[1]), x.dtype) for x, lo, hi in held]
    many = len(held)
    return pl.pallas_call(
        functools.partial(finish_kernel, start, [cut for _, *cut in held]),
        in_specs=[SM(), VM(), VM(), VM()] + [HB() for _ in (*held, *before, *after)],
        out_specs=[HB() for _ in range(2 + many)],
        out_shape=[out, out] + passed,
        input_output_aliases={4 + many: 0, 5 + many: 1} if before else {},
        scratch_shapes=[
            pltpu.VMEM((2, rows, columns), jnp.bfloat16),
            pltpu.SemaphoreType.DMA((2,)),
            pltpu.SemaphoreType.DMA((max(many, 1),)),
        ],
        compiler_params=params(),
        cost_estimate=cost(0, 16 * rows * columns),
        name="finish",
    )(keep, coded, square, tangent, *(x for x, _, _ in held), *before, *after)


def per_device_pair(
    n_row, x0_rows, x1_rows, x0_cols, x1_cols, mask0_rows, mask1_rows, mask0_cols, mask1_cols, keep
):
    n_col = 2
    group = n_row // n_col
    panel = x0_cols.shape[0]
    all_rows = x0_rows.shape[0]
    row_index = lax.axis_index("row")
    half = row_index // group
    diag = (half == lax.axis_index("col")).astype(jnp.int32).reshape(1)
    place = (row_index % group).astype(jnp.int32).reshape(1)
    direct = all_rows // 8
    split = all_rows // 2
    wide = 256

    def device(h, q, c):
        return (h * group + q) * n_col + c

    spots = [(h, q, c) for h in range(2) for q in range(group) for c in range(2)]
    over_y = [(device(h, q, c), device(h, q, 1 - c)) for h, q, c in spots]
    over_z = [(device(h, q, c), device(1 - h, q, c)) for h, q, c in spots]
    ring = [
        (device(h, q, c), device(h, q, 1 - c) if h == c else device(1 - h, q, c))
        for h, q, c in spots
    ]
    def move(values, pairs):
        return lax.ppermute(values, ("row", "col"), pairs)

    def chunks(spans, stacked, limit, after=()):
        inputs = (place, mask0_rows, mask1_rows, x0_rows, x1_rows)
        return masked_chunks(*inputs, spans, stacked, panel, limit, after)

    def partials(one, other, **more):
        return partial_products(diag, one, other, right0, right1, wide, **more)

    def own(one, other):
        return local_products(diag, one, other, right0, right1, wide)

    def parts(joint, a, b):
        top, low = piece(joint, 0, direct), piece(joint, direct)
        return (top, piece(a), low, piece(b))

    joint, a1, b1 = chunks(((0, direct), (direct, split)), True, ALL_VMEM_BYTES)
    passed1 = move(b1, over_y)
    near0 = move(joint, ring)
    a2, b2 = chunks(((split, all_rows),), False, VMEM_BYTES, (a1,))
    right0, right1 = masked_right(mask0_cols, mask1_cols, x0_cols, x1_cols, (a2,))
    send, b2 = chosen(diag, passed1, a1, (b2,), (near0, right0))
    near1 = move(send, over_z)
    passed2 = move(b2, over_y)
    far0 = move(near0, over_y)
    send, a1 = chosen(diag, passed2, a2, (a1,), (far0,))
    near2 = move(send, over_z)
    got1 = move(a1, over_y)
    far1 = move(near1, over_y)
    (coded,) = partials(parts(near0, near1, far1), parts(far0, far1, near1))
    coded, near2 = handed_on((coded, near2), (got1,))
    back = move(coded, over_z)
    far2 = move(near2, over_y)
    sums = own(parts(joint, a1, b1), parts(near0, got1, passed1))
    late = a2.shape[0] * 3 // 4
    coded, top2, low2 = partials(
        (piece(near2), piece(far2)),
        (piece(far2), piece(near2)),
        given=(piece(a2, 0, late), piece(a2, late)),
        gates=sums[:1],
    )
    (low2,) = handed_on((low2,), (back,))
    outs = finished(keep, *sums, back, (), 0, all_rows)
    back = move(coded, over_z)
    got2 = (piece(move(top2, over_y)), piece(move(low2, over_y)))
    sums = own((piece(a2), piece(b2)), (*got2, piece(passed2)))
    return tuple(finished(keep, *sums, back, outs, split, all_rows))


def passed_along(shard, axis, by):
    devices = lax.axis_size(axis)
    return lax.ppermute(shard, axis, [(i, (i + by) % devices) for i in range(devices)])


def masked(values, mask):
    rows_b, cols_b = mask.shape
    tiles = values.reshape(rows_b, BLOCK, cols_b, BLOCK)
    return (tiles * mask.astype(values.dtype)[:, None, :, None]).reshape(values.shape)


def per_device(
    x0_rows, x1_rows, x0_cols, x1_cols, mask0_rows, mask1_rows, mask0_cols, mask1_cols, keep_mask
):
    n_row = lax.axis_size("row")
    n_col = lax.axis_size("col")
    group = n_row // n_col
    row_index = lax.axis_index("row")
    col_index = lax.axis_index("col")
    panel = x0_cols.shape[0]
    start = row_index % group * panel
    block_start = row_index % group * (panel // BLOCK)
    left_zero = masked(
        lax.dynamic_slice_in_dim(x0_rows, start, panel, 1),
        lax.dynamic_slice_in_dim(mask0_rows, block_start, panel // BLOCK, 1),
    )
    left_one = masked(
        lax.dynamic_slice_in_dim(x1_rows, start, panel, 1),
        lax.dynamic_slice_in_dim(mask1_rows, block_start, panel // BLOCK, 1),
    )
    right_zero = masked(x0_cols, mask0_cols)
    right_one = masked(x1_cols, mask1_cols)
    left = jnp.stack([left_zero, left_one])
    right = jnp.stack([right_zero, right_one])
    left_offset = row_index // group % n_col
    right_offset = col_index % n_col
    levels = n_col.bit_length() - 1
    for level in range(levels):
        moved_left = passed_along(left, "col", -(1 << level))
        moved_right = passed_along(right, "row", -group * (1 << level))
        left = jnp.where(left_offset // (1 << level) % 2 == 1, moved_left, left)
        right = jnp.where(right_offset // (1 << level) % 2 == 1, moved_right, right)

    def accumulate(left_now, right_now, square, tangent):
        square = square + jnp.dot(left_now[0], right_now[0], preferred_element_type=jnp.float32)
        tangent = tangent + jnp.dot(left_now[0], right_now[1], preferred_element_type=jnp.float32)
        tangent = tangent + jnp.dot(left_now[1], right_now[0], preferred_element_type=jnp.float32)
        return (square, tangent)

    def section_body(section, carry):
        left_now, right_now, square, tangent = carry
        square, tangent = accumulate(left_now, right_now, square, tangent)
        left_now = passed_along(left_now, "col", -1)
        right_now = passed_along(right_now, "row", -group)
        return (left_now, right_now, square, tangent)

    zeros = jnp.zeros((left_zero.shape[0], right_zero.shape[1]), jnp.float32)
    left, right, square, tangent = lax.fori_loop(
        0, n_col - 1, section_body, (left, right, zeros, zeros)
    )
    square, tangent = accumulate(left, right, square, tangent)
    x_square = masked(square, keep_mask).astype(jnp.bfloat16)
    x_tangent = masked(tangent, keep_mask).astype(jnp.bfloat16)
    return (x_square, x_tangent)


def solution(mesh):
    if mesh.shape["col"] == 2:
        body = functools.partial(per_device_pair, mesh.shape["row"])
    else:
        body = per_device
    return jax.shard_map(
        body,
        mesh=mesh,
        in_specs=(P("row", "col"),) * 9,
        out_specs=(P("row", "col"), P("row", "col")),
        check_vma=False,
    )
```

```python
import functools
import math

import jax
import jax.numpy as jnp
from jax import lax
from jax.experimental import pallas as pl
from jax.experimental.pallas import tpu as pltpu
from jax.sharding import PartitionSpec as P

BLOCK = 128
LEVELS = 32000.0
STEPS = 32.0
LN2 = math.log(2.0)
VMEM_BYTES = 48 * 1024 * 1024
ALL_VMEM_BYTES = 62 * 1024 * 1024

VM = functools.partial(pl.BlockSpec, memory_space=pltpu.VMEM)
SM = functools.partial(pl.BlockSpec, memory_space=pltpu.SMEM)
HB = functools.partial(pl.BlockSpec, memory_space=pl.ANY)


def params(limit=VMEM_BYTES):
    return pltpu.CompilerParams(vmem_limit_bytes=limit)


def cost(flops, moved):
    return pl.CostEstimate(flops=int(flops) // 64, bytes_accessed=int(moved) // 64, transcendentals=0)


def scaled(values, entry):
    return (values.astype(jnp.float32) * entry.astype(jnp.float32)).astype(values.dtype)


def row_pieces(start, rows):
    edges = sorted({start, start + rows} | {e for e in range(0, start + rows, BLOCK) if e > start})
    return [(lo // BLOCK, slice(lo - start, hi - start)) for lo, hi in zip(edges, edges[1:])]


def chunk_kernel(spans, stacked, panel, *refs):
    place, mask0_far, mask1_far, x0, x1 = refs[:5]
    outs = refs[-5 - 2 * len(spans) + stacked : -5]
    held, mask0, mask1, mask_sems, sems = refs[-5:]
    start, rows = spans[0][0], held.shape[1]
    blocks = panel // BLOCK
    first = place[0] * blocks
    at = pl.ds(pl.multiple_of(place[0] * panel, BLOCK), panel)
    copies = [
        pltpu.make_async_copy(mask0_far, mask0, mask_sems.at[0]),
        pltpu.make_async_copy(mask1_far, mask1, mask_sems.at[1]),
        pltpu.make_async_copy(x0.at[pl.ds(start, rows), at], held.at[0], sems.at[0]),
        pltpu.make_async_copy(x1.at[pl.ds(start, rows), at], held.at[1], sems.at[1]),
    ]
    for copy in copies:
        copy.start()
    for copy in copies:
        copy.wait()
    for n, (lo, hi) in enumerate(spans):
        for which, mask in enumerate((mask0, mask1)):
            joint = stacked and n == 0
            out = outs[0] if joint else outs[2 * n - stacked + which]
            down = which * (hi - lo) if joint else 0
            for row_block, part in row_pieces(lo, hi - lo):
                source = slice(part.start + lo - start, part.stop + lo - start)
                target = slice(part.start + down, part.stop + down)
                for j in range(blocks):
                    cut = slice(j * BLOCK, (j + 1) * BLOCK)
                    values = scaled(held[which, source, cut], mask[row_block, first + j])
                    out[target, cut] = values


def masked_chunks(place, mask0, mask1, x0, x1, spans, stacked, panel, limit, after=()):
    rows = spans[-1][1] - spans[0][0]
    outs = []
    for n, (lo, hi) in enumerate(spans):
        if stacked and n == 0:
            outs.append(jax.ShapeDtypeStruct((2 * (hi - lo), panel), x0.dtype))
        else:
            outs += [jax.ShapeDtypeStruct((hi - lo, panel), x0.dtype)] * 2
    return pl.pallas_call(
        functools.partial(chunk_kernel, spans, int(stacked), panel),
        in_specs=[SM()] + [HB() for _ in range(4 + len(after))],
        out_specs=[VM() for _ in outs],
        out_shape=outs,
        scratch_shapes=[
            pltpu.VMEM((2, rows, panel), x0.dtype),
            pltpu.SMEM(mask0.shape, mask0.dtype),
            pltpu.SMEM(mask1.shape, mask1.dtype),
            pltpu.SemaphoreType.DMA((2,)),
            pltpu.SemaphoreType.DMA((2,)),
        ],
        compiler_params=params(limit),
        cost_estimate=cost(0, 8 * rows * panel),
        name="left_chunks",
    )(place, mask0, mask1, x0, x1, *after)


def choose_kernel(gates, cuts, diag, *refs):
    one, other = refs[gates : gates + 2]
    held = refs[gates + 2 : gates + 2 + len(cuts)]
    send, joint, sems = refs[-3:]
    others = []
    top = 0
    for i, (x, (lo, hi)) in enumerate(zip(held, cuts)):
        target = joint.at[pl.ds(top, hi - lo)]
        others.append(pltpu.make_async_copy(x.at[pl.ds(lo, hi - lo)], target, sems.at[1 + i]))
        top += hi - lo
    for copy in others:
        copy.start()

    @pl.when(diag[0] == 1)
    def _():
        copy = pltpu.make_async_copy(one, send, sems.at[0])
        copy.start()
        copy.wait()

    @pl.when(diag[0] == 0)
    def _():
        copy = pltpu.make_async_copy(other, send, sems.at[0])
        copy.start()
        copy.wait()

    for copy in others:
        copy.wait()


def chosen(diag, one, other, held, after=()):
    rows = sum(hi - lo for _, lo, hi in held)
    outs = [
        jax.ShapeDtypeStruct(one.shape, one.dtype),
        jax.ShapeDtypeStruct((rows, one.shape[1]), one.dtype),
    ]
    return pl.pallas_call(
        functools.partial(choose_kernel, len(after), [cut for _, *cut in held]),
        in_specs=[SM()] + [HB() for _ in (*after, one, other, *held)],
        out_specs=[HB() for _ in outs],
        out_shape=outs,
        scratch_shapes=[pltpu.SemaphoreType.DMA((1 + len(held),))],
        compiler_params=params(),
        cost_estimate=cost(0, 4 * one.size),
        name="to_send",
    )(diag, *after, one, other, *(x for x, _, _ in held))


def hand_kernel(many, *refs):
    sems = refs[-1]
    copies = [
        pltpu.make_async_copy(refs[i], refs[i - many - 1], sems.at[i]) for i in range(many)
    ]
    for copy in copies:
        copy.start()
    for copy in copies:
        copy.wait()


def handed_on(values, gates):
    outs = [jax.ShapeDtypeStruct(x.shape, x.dtype) for x in values]
    return pl.pallas_call(
        functools.partial(hand_kernel, len(values)),
        in_specs=[HB() for _ in (*values, *gates)],
        out_specs=[HB() for _ in outs],
        out_shape=outs,
        scratch_shapes=[pltpu.SemaphoreType.DMA((len(outs),))],
        compiler_params=params(),
        cost_estimate=cost(0, 4 * sum(x.size for x in values)),
        name="handed_on",
    )(*values, *gates)


def right_kernel(mask0, mask1, x0, x1, *rest):
    out0, out1 = rest[-2:]
    step = pl.program_id(0)
    many = x0.shape[0] // BLOCK
    for i in range(many):
        for j in range(x0.shape[1] // BLOCK):
            at = (slice(i * BLOCK, (i + 1) * BLOCK), slice(j * BLOCK, (j + 1) * BLOCK))
            out0[at] = scaled(x0[at], mask0[step * many + i, j])
            out1[at] = scaled(x1[at], mask1[step * many + i, j])


def masked_right(mask0, mask1, x0, x1, after=()):
    depth, columns = x0.shape
    tall = 2 * BLOCK
    out = jax.ShapeDtypeStruct(x0.shape, x0.dtype)
    tile = pl.BlockSpec((tall, columns), lambda g: (g, 0))
    return pl.pallas_call(
        right_kernel,
        grid=(depth // tall,),
        in_specs=[SM(), SM(), tile, tile] + [HB() for _ in after],
        out_specs=[tile, tile],
        out_shape=[out, out],
        compiler_params=params(),
        cost_estimate=cost(0, 8 * depth * columns),
        name="right_panels",
    )(mask0, mask1, x0, x1, *after)


def both_products(held, right0, right1):
    rows = held.shape[0] // 2
    first = jnp.dot(held[...], right0[...], preferred_element_type=jnp.float32)
    second = jnp.dot(held[:rows], right1[...], preferred_element_type=jnp.float32)
    return first[:rows], first[rows:] + second


def piece(array, lo=0, hi=None):
    return (array, lo, array.shape[0] if hi is None else hi)


def numbered(one, other):
    arrays = []
    for array, _, _ in (*one, *other):
        if all(array is not known for known in arrays):
            arrays.append(array)
    number = {id(array): i for i, array in enumerate(arrays)}
    return arrays, *(
        tuple((number[id(array)], lo, hi) for array, lo, hi in pieces) for pieces in (one, other)
    )


def fetched(pieces, refs, held, sems):
    copies = []
    top = 0
    for i, (which, lo, hi) in enumerate(pieces):
        source = refs[which].at[pl.ds(lo, hi - lo)]
        copies.append(pltpu.make_async_copy(source, held.at[pl.ds(top, hi - lo)], sems.at[i]))
        top += hi - lo
    for copy in copies:
        copy.start()
    for copy in copies:
        copy.wait()


def fetch_left(diag, one, other, refs, held, sems):
    first = pl.program_id(0) == 0

    @pl.when(first & (diag[0] == 1))
    def _():
        fetched(one, refs, held, sems)

    @pl.when(first & (diag[0] == 0))
    def _():
        fetched(other, refs, held, sems)


def local_kernel(one, other, diag, right0, right1, *refs):
    square, tangent, held, sems = refs[-4:]
    fetch_left(diag, one, other, refs, held, sems)
    square[...], tangent[...] = both_products(held, right0, right1)


def local_products(diag, one, other, right0, right1, wide):
    arrays, one, other = numbered(one, other)
    rows = sum(hi - lo for _, lo, hi in one) // 2
    depth, columns = right0.shape
    out = jax.ShapeDtypeStruct((rows, columns), jnp.float32)
    tile = pl.BlockSpec((rows, wide), lambda g: (0, g))
    return pl.pallas_call(
        functools.partial(local_kernel, one, other),
        grid=(columns // wide,),
        in_specs=[
            SM(),
            pl.BlockSpec((depth, wide), lambda g: (0, g)),
            pl.BlockSpec((depth, wide), lambda g: (0, g)),
        ]
        + [HB() for _ in arrays],
        out_specs=[tile, tile],
        out_shape=[out, out],
        scratch_shapes=[
            pltpu.VMEM((2 * rows, depth), right0.dtype),
            pltpu.SemaphoreType.DMA((max(len(one), len(other)),)),
        ],
        compiler_params=params(),
        cost_estimate=cost(6 * rows * depth * columns, 8 * rows * depth + 4 * depth * columns),
        name="own_products",
    )(diag, right0, right1, *arrays)


def partial_kernel(one, other, many, cuts, diag, right0, right1, *refs):
    given = len(cuts)
    out, passed = refs[-5 - given], refs[-4 - given : -4]
    held, steps, sems, hand_sems = refs[-4:]
    others = [
        pltpu.make_async_copy(x.at[pl.ds(lo, hi - lo)], y, hand_sems.at[i])
        for i, (x, y, (lo, hi)) in enumerate(zip(refs[many : many + given], passed, cuts))
    ]

    @pl.when(pl.program_id(0) == 0)
    def _():
        for copy in others:
            copy.start()

    rows, wide = held.shape[0] // 2, right0.shape[1]
    step = pl.program_id(0)
    tiles = wide // BLOCK
    across = pl.num_programs(0) * tiles
    fetch_left(diag, one, other, refs, held, sems)
    for which, values in enumerate(both_products(held, right0, right1)):
        top = jnp.maximum(jnp.max(jnp.abs(values), axis=0, keepdims=True), 1e-30)
        level = jnp.ceil(jnp.log(top) * (STEPS / LN2)) + 1.0
        coded = jnp.round(values * (LEVELS * jnp.exp(level * (-LN2 / STEPS))))
        coded = jnp.clip(coded, -32767.0, 32767.0).astype(jnp.int32).astype(jnp.int16)
        for t in range(tiles):
            at = which * across + step * tiles + t
            cut = slice(t * BLOCK, (t + 1) * BLOCK)
            out[pl.ds(pl.multiple_of(at * rows, rows), rows), :] = coded[:, cut]
            steps[pl.ds(at, 1), :] = level[:, cut]

    @pl.when(step == pl.num_programs(0) - 1)
    def _():
        tail = steps.shape[0]
        out[out.shape[0] - tail :, :] = steps[...].astype(jnp.int32).astype(jnp.int16)
        for copy in others:
            copy.wait()


def partial_products(diag, one, other, right0, right1, wide, given=(), gates=()):
    arrays, one, other = numbered(one, other)
    rows = sum(hi - lo for _, lo, hi in one) // 2
    depth, columns = right0.shape
    tiles = 2 * columns // BLOCK
    tail = -(-tiles // 16) * 16
    return pl.pallas_call(
        functools.partial(partial_kernel, one, other, len(arrays), [cut for _, *cut in given]),
        grid=(columns // wide,),
        in_specs=[
            SM(),
            pl.BlockSpec((depth, wide), lambda g: (0, g)),
            pl.BlockSpec((depth, wide), lambda g: (0, g)),
        ]
        + [HB() for _ in (*arrays, *given, *gates)],
        out_specs=[pl.BlockSpec((tiles * rows + tail, BLOCK), lambda g: (0, 0))]
        + [HB() for _ in given],
        out_shape=[jax.ShapeDtypeStruct((tiles * rows + tail, BLOCK), jnp.int16)]
        + [jax.ShapeDtypeStruct((hi - lo, x.shape[1]), x.dtype) for x, lo, hi in given],
        scratch_shapes=[
            pltpu.VMEM((2 * rows, depth), right0.dtype),
            pltpu.VMEM((tail, BLOCK), jnp.float32),
            pltpu.SemaphoreType.DMA((max(len(one), len(other)),)),
            pltpu.SemaphoreType.DMA((max(len(given), 1),)),
        ],
        compiler_params=params(),
        cost_estimate=cost(6 * rows * depth * columns, 4 * rows * depth + 4 * depth * columns),
        name="partial_products",
    )(diag, right0, right1, *arrays, *(x for x, _, _ in given), *gates)


def finish_kernel(start, many, keep, coded, square, tangent, *rest):
    given, outs, passed = rest[:many], rest[-5 - many : -3 - many], rest[-3 - many : -3]
    made, out_sems, sems = rest[-3:]
    rows, columns = square.shape
    across = columns // BLOCK
    others = [
        pltpu.make_async_copy(x, y, sems.at[i]) for i, (x, y) in enumerate(zip(given, passed))
    ]
    results = [
        pltpu.make_async_copy(made.at[i], x.at[pl.ds(start, rows)], out_sems.at[i])
        for i, x in enumerate(outs)
    ]
    for copy in others:
        copy.start()
    tail = coded.shape[0] - 2 * across * rows
    levels = coded[coded.shape[0] - tail :, :].astype(jnp.int32).astype(jnp.float32)
    steps = jnp.exp(levels * (LN2 / STEPS)) * (1.0 / LEVELS)
    for which, mine in enumerate((square, tangent)):
        for j in range(across):
            tile = which * across + j
            cut = slice(j * BLOCK, (j + 1) * BLOCK)
            other = coded[tile * rows : (tile + 1) * rows, :].astype(jnp.int32).astype(jnp.float32)
            total = mine[:, cut] + other * steps[tile : tile + 1, :]
            for row_block, part in row_pieces(start, rows):
                kept = total[part] * keep[row_block, j].astype(jnp.float32)
                made[which, part, cut] = kept.astype(made.dtype)
        results[which].start()
    for copy in results + others:
        copy.wait()


def finished(keep, square, tangent, coded, before, start, all_rows, held=(), after=()):
    rows, columns = square.shape
    out = jax.ShapeDtypeStruct((all_rows, columns), jnp.bfloat16)
    held, before = list(held), list(before)
    passed = [jax.ShapeDtypeStruct(x.shape, x.dtype) for x in held]
    many = len(held)
    return pl.pallas_call(
        functools.partial(finish_kernel, start, many),
        in_specs=[SM(), VM(), VM(), VM()] + [HB() for _ in (*held, *before, *after)],
        out_specs=[HB() for _ in range(2 + many)],
        out_shape=[out, out] + passed,
        input_output_aliases={4 + many: 0, 5 + many: 1} if before else {},
        scratch_shapes=[
            pltpu.VMEM((2, rows, columns), jnp.bfloat16),
            pltpu.SemaphoreType.DMA((2,)),
            pltpu.SemaphoreType.DMA((max(many, 1),)),
        ],
        compiler_params=params(),
        cost_estimate=cost(0, 16 * rows * columns),
        name="finish",
    )(keep, coded, square, tangent, *held, *before, *after)


def per_device_pair(
    n_row, x0_rows, x1_rows, x0_cols, x1_cols, mask0_rows, mask1_rows, mask0_cols, mask1_cols, keep
):
    n_col = 2
    group = n_row // n_col
    panel = x0_cols.shape[0]
    all_rows = x0_rows.shape[0]
    row_index = lax.axis_index("row")
    half = row_index // group
    diag = (half == lax.axis_index("col")).astype(jnp.int32).reshape(1)
    place = (row_index % group).astype(jnp.int32).reshape(1)
    split = all_rows * 7 // 16
    ahead = all_rows // 8
    wide = 256

    def device(h, q, c):
        return (h * group + q) * n_col + c

    spots = [(h, q, c) for h in range(2) for q in range(group) for c in range(2)]
    over_y = [(device(h, q, c), device(h, q, 1 - c)) for h, q, c in spots]
    over_z = [(device(h, q, c), device(1 - h, q, c)) for h, q, c in spots]
    def move(values, pairs):
        return lax.ppermute(values, ("row", "col"), pairs)

    def chunks(spans, stacked, limit, after=()):
        inputs = (place, mask0_rows, mask1_rows, x0_rows, x1_rows)
        return masked_chunks(*inputs, spans, stacked, panel, limit, after)

    def partials(one, other, **more):
        return partial_products(diag, one, other, right0, right1, wide, **more)

    def own(one, other):
        return local_products(diag, one, other, right0, right1, wide)

    a1, b1 = chunks(((0, split),), False, ALL_VMEM_BYTES)
    passed1 = move(b1, over_y)
    a2, b2 = chunks(((split, all_rows),), False, VMEM_BYTES, (a1,))
    right0, right1 = masked_right(mask0_cols, mask1_cols, x0_cols, x1_cols, (a2,))
    send, b2 = chosen(diag, passed1, a1, (piece(b2),), (right0,))
    near1 = move(send, over_z)
    passed2 = move(b2, over_y)
    send, most = chosen(diag, passed2, a2, (piece(a1), piece(a2, 0, ahead)))
    near2 = move(send, over_z)
    got1 = move(most, over_y)
    far1 = move(near1, over_y)
    (coded,) = partials((piece(near1), piece(far1)), (piece(far1), piece(near1)))
    coded, near2 = handed_on((coded, near2), (got1,))
    back = move(coded, over_z)
    far2 = move(near2, over_y)
    sums = own((piece(a1), piece(b1)), (piece(got1, 0, split), piece(passed1)))
    coded, rest = partials(
        (piece(near2), piece(far2)),
        (piece(far2), piece(near2)),
        given=(piece(a2, ahead),),
        gates=sums[:1],
    )
    (coded,) = handed_on((coded,), (back,))
    outs = finished(keep, *sums, back, (), 0, all_rows)
    back = move(coded, over_z)
    got2 = move(rest, over_y)
    sums = own((piece(a2), piece(b2)), (piece(got1, split), piece(got2), piece(passed2)))
    return tuple(finished(keep, *sums, back, outs, split, all_rows))


def passed_along(shard, axis, by):
    devices = lax.axis_size(axis)
    return lax.ppermute(shard, axis, [(i, (i + by) % devices) for i in range(devices)])


def masked(values, mask):
    rows_b, cols_b = mask.shape
    tiles = values.reshape(rows_b, BLOCK, cols_b, BLOCK)
    return (tiles * mask.astype(values.dtype)[:, None, :, None]).reshape(values.shape)


def per_device(
    x0_rows, x1_rows, x0_cols, x1_cols, mask0_rows, mask1_rows, mask0_cols, mask1_cols, keep_mask
):
    n_row = lax.axis_size("row")
    n_col = lax.axis_size("col")
    group = n_row // n_col
    row_index = lax.axis_index("row")
    col_index = lax.axis_index("col")
    panel = x0_cols.shape[0]
    start = row_index % group * panel
    block_start = row_index % group * (panel // BLOCK)
    left_zero = masked(
        lax.dynamic_slice_in_dim(x0_rows, start, panel, 1),
        lax.dynamic_slice_in_dim(mask0_rows, block_start, panel // BLOCK, 1),
    )
    left_one = masked(
        lax.dynamic_slice_in_dim(x1_rows, start, panel, 1),
        lax.dynamic_slice_in_dim(mask1_rows, block_start, panel // BLOCK, 1),
    )
    right_zero = masked(x0_cols, mask0_cols)
    right_one = masked(x1_cols, mask1_cols)
    left = jnp.stack([left_zero, left_one])
    right = jnp.stack([right_zero, right_one])
    left_offset = row_index // group % n_col
    right_offset = col_index % n_col
    levels = n_col.bit_length() - 1
    for level in range(levels):
        moved_left = passed_along(left, "col", -(1 << level))
        moved_right = passed_along(right, "row", -group * (1 << level))
        left = jnp.where(left_offset // (1 << level) % 2 == 1, moved_left, left)
        right = jnp.where(right_offset // (1 << level) % 2 == 1, moved_right, right)

    def accumulate(left_now, right_now, square, tangent):
        square = square + jnp.dot(left_now[0], right_now[0], preferred_element_type=jnp.float32)
        tangent = tangent + jnp.dot(left_now[0], right_now[1], preferred_element_type=jnp.float32)
        tangent = tangent + jnp.dot(left_now[1], right_now[0], preferred_element_type=jnp.float32)
        return (square, tangent)

    def section_body(section, carry):
        left_now, right_now, square, tangent = carry
        square, tangent = accumulate(left_now, right_now, square, tangent)
        left_now = passed_along(left_now, "col", -1)
        right_now = passed_along(right_now, "row", -group)
        return (left_now, right_now, square, tangent)

    zeros = jnp.zeros((left_zero.shape[0], right_zero.shape[1]), jnp.float32)
    left, right, square, tangent = lax.fori_loop(
        0, n_col - 1, section_body, (left, right, zeros, zeros)
    )
    square, tangent = accumulate(left, right, square, tangent)
    x_square = masked(square, keep_mask).astype(jnp.bfloat16)
    x_tangent = masked(tangent, keep_mask).astype(jnp.bfloat16)
    return (x_square, x_tangent)


def solution(mesh):
    if mesh.shape["col"] == 2:
        body = functools.partial(per_device_pair, mesh.shape["row"])
    else:
        body = per_device
    return jax.shard_map(
        body,
        mesh=mesh,
        in_specs=(P("row", "col"),) * 9,
        out_specs=(P("row", "col"), P("row", "col")),
        check_vma=False,
    )
```

```python
import functools
import math

import jax
import jax.numpy as jnp
from jax import lax
from jax.experimental import pallas as pl
from jax.experimental.pallas import tpu as pltpu
from jax.sharding import PartitionSpec as P

BLOCK = 128
LEVELS = 32000.0
STEPS = 32.0
LN2 = math.log(2.0)
VMEM_BYTES = 48 * 1024 * 1024
ALL_VMEM_BYTES = 62 * 1024 * 1024

VM = functools.partial(pl.BlockSpec, memory_space=pltpu.VMEM)
SM = functools.partial(pl.BlockSpec, memory_space=pltpu.SMEM)
HB = functools.partial(pl.BlockSpec, memory_space=pl.ANY)


def params(limit=VMEM_BYTES):
    return pltpu.CompilerParams(vmem_limit_bytes=limit)


def cost(flops, moved):
    return pl.CostEstimate(flops=int(flops) // 64, bytes_accessed=int(moved) // 64, transcendentals=0)


def scaled(values, entry):
    return (values.astype(jnp.float32) * entry.astype(jnp.float32)).astype(values.dtype)


def row_pieces(start, rows):
    edges = sorted({start, start + rows} | {e for e in range(0, start + rows, BLOCK) if e > start})
    return [(lo // BLOCK, slice(lo - start, hi - start)) for lo, hi in zip(edges, edges[1:])]


def chunk_kernel(spans, stacked, panel, *refs):
    place, mask0_far, mask1_far, x0, x1 = refs[:5]
    outs = refs[-5 - 2 * len(spans) + stacked : -5]
    held, mask0, mask1, mask_sems, sems = refs[-5:]
    start, rows = spans[0][0], held.shape[1]
    blocks = panel // BLOCK
    first = place[0] * blocks
    at = pl.ds(pl.multiple_of(place[0] * panel, BLOCK), panel)
    copies = [
        pltpu.make_async_copy(mask0_far, mask0, mask_sems.at[0]),
        pltpu.make_async_copy(mask1_far, mask1, mask_sems.at[1]),
        pltpu.make_async_copy(x0.at[pl.ds(start, rows), at], held.at[0], sems.at[0]),
        pltpu.make_async_copy(x1.at[pl.ds(start, rows), at], held.at[1], sems.at[1]),
    ]
    for copy in copies:
        copy.start()
    for copy in copies:
        copy.wait()
    for n, (lo, hi) in enumerate(spans):
        for which, mask in enumerate((mask0, mask1)):
            joint = stacked and n == 0
            out = outs[0] if joint else outs[2 * n - stacked + which]
            down = which * (hi - lo) if joint else 0
            for row_block, part in row_pieces(lo, hi - lo):
                source = slice(part.start + lo - start, part.stop + lo - start)
                target = slice(part.start + down, part.stop + down)
                for j in range(blocks):
                    cut = slice(j * BLOCK, (j + 1) * BLOCK)
                    values = scaled(held[which, source, cut], mask[row_block, first + j])
                    out[target, cut] = values


def masked_chunks(place, mask0, mask1, x0, x1, spans, stacked, panel, limit, after=()):
    rows = spans[-1][1] - spans[0][0]
    outs = []
    for n, (lo, hi) in enumerate(spans):
        if stacked and n == 0:
            outs.append(jax.ShapeDtypeStruct((2 * (hi - lo), panel), x0.dtype))
        else:
            outs += [jax.ShapeDtypeStruct((hi - lo, panel), x0.dtype)] * 2
    return pl.pallas_call(
        functools.partial(chunk_kernel, spans, int(stacked), panel),
        in_specs=[SM()] + [HB() for _ in range(4 + len(after))],
        out_specs=[VM() for _ in outs],
        out_shape=outs,
        scratch_shapes=[
            pltpu.VMEM((2, rows, panel), x0.dtype),
            pltpu.SMEM(mask0.shape, mask0.dtype),
            pltpu.SMEM(mask1.shape, mask1.dtype),
            pltpu.SemaphoreType.DMA((2,)),
            pltpu.SemaphoreType.DMA((2,)),
        ],
        compiler_params=params(limit),
        cost_estimate=cost(0, 8 * rows * panel),
        name="left_chunks",
    )(place, mask0, mask1, x0, x1, *after)


def choose_kernel(gates, many, diag, *refs):
    one, other = refs[gates : gates + 2]
    held, outs, sems = refs[gates + 2 : gates + 2 + many], refs[-many - 2 : -1], refs[-1]
    others = [
        pltpu.make_async_copy(x, out, sems.at[1 + i])
        for i, (x, out) in enumerate(zip(held, outs[1:]))
    ]
    for copy in others:
        copy.start()

    @pl.when(diag[0] == 1)
    def _():
        copy = pltpu.make_async_copy(one, outs[0], sems.at[0])
        copy.start()
        copy.wait()

    @pl.when(diag[0] == 0)
    def _():
        copy = pltpu.make_async_copy(other, outs[0], sems.at[0])
        copy.start()
        copy.wait()

    for copy in others:
        copy.wait()


def chosen(diag, one, other, held=(), after=()):
    outs = [jax.ShapeDtypeStruct(x.shape, x.dtype) for x in (one, *held)]
    return pl.pallas_call(
        functools.partial(choose_kernel, len(after), len(held)),
        in_specs=[SM()] + [HB() for _ in (*after, one, other, *held)],
        out_specs=[HB() for _ in outs],
        out_shape=outs,
        scratch_shapes=[pltpu.SemaphoreType.DMA((len(outs),))],
        compiler_params=params(),
        cost_estimate=cost(0, 4 * one.size),
        name="to_send",
    )(diag, *after, one, other, *held)


def hand_kernel(many, *refs):
    sems = refs[-1]
    copies = [
        pltpu.make_async_copy(refs[i], refs[i - many - 1], sems.at[i]) for i in range(many)
    ]
    for copy in copies:
        copy.start()
    for copy in copies:
        copy.wait()


def handed_on(values, gates):
    outs = [jax.ShapeDtypeStruct(x.shape, x.dtype) for x in values]
    return pl.pallas_call(
        functools.partial(hand_kernel, len(values)),
        in_specs=[HB() for _ in (*values, *gates)],
        out_specs=[HB() for _ in outs],
        out_shape=outs,
        scratch_shapes=[pltpu.SemaphoreType.DMA((len(outs),))],
        compiler_params=params(),
        cost_estimate=cost(0, 4 * sum(x.size for x in values)),
        name="handed_on",
    )(*values, *gates)


def right_kernel(mask0, mask1, x0, x1, *rest):
    out0, out1 = rest[-2:]
    step = pl.program_id(0)
    many = x0.shape[0] // BLOCK
    for i in range(many):
        for j in range(x0.shape[1] // BLOCK):
            at = (slice(i * BLOCK, (i + 1) * BLOCK), slice(j * BLOCK, (j + 1) * BLOCK))
            out0[at] = scaled(x0[at], mask0[step * many + i, j])
            out1[at] = scaled(x1[at], mask1[step * many + i, j])


def masked_right(mask0, mask1, x0, x1, after=()):
    depth, columns = x0.shape
    tall = 2 * BLOCK
    out = jax.ShapeDtypeStruct(x0.shape, x0.dtype)
    tile = pl.BlockSpec((tall, columns), lambda g: (g, 0))
    return pl.pallas_call(
        right_kernel,
        grid=(depth // tall,),
        in_specs=[SM(), SM(), tile, tile] + [HB() for _ in after],
        out_specs=[tile, tile],
        out_shape=[out, out],
        compiler_params=params(),
        cost_estimate=cost(0, 8 * depth * columns),
        name="right_panels",
    )(mask0, mask1, x0, x1, *after)


def both_products(held, right0, right1):
    rows = held.shape[0] // 2
    first = jnp.dot(held[...], right0[...], preferred_element_type=jnp.float32)
    second = jnp.dot(held[:rows], right1[...], preferred_element_type=jnp.float32)
    return first[:rows], first[rows:] + second


def piece(array, lo=0, hi=None):
    return (array, lo, array.shape[0] if hi is None else hi)


def numbered(one, other):
    arrays = []
    for array, _, _ in (*one, *other):
        if all(array is not known for known in arrays):
            arrays.append(array)
    number = {id(array): i for i, array in enumerate(arrays)}
    return arrays, *(
        tuple((number[id(array)], lo, hi) for array, lo, hi in pieces) for pieces in (one, other)
    )


def fetched(pieces, refs, held, sems):
    copies = []
    top = 0
    for i, (which, lo, hi) in enumerate(pieces):
        source = refs[which].at[pl.ds(lo, hi - lo)]
        copies.append(pltpu.make_async_copy(source, held.at[pl.ds(top, hi - lo)], sems.at[i]))
        top += hi - lo
    for copy in copies:
        copy.start()
    for copy in copies:
        copy.wait()


def fetch_left(diag, one, other, refs, held, sems):
    first = pl.program_id(0) == 0

    @pl.when(first & (diag[0] == 1))
    def _():
        fetched(one, refs, held, sems)

    @pl.when(first & (diag[0] == 0))
    def _():
        fetched(other, refs, held, sems)


def local_kernel(one, other, diag, right0, right1, *refs):
    square, tangent, held, sems = refs[-4:]
    fetch_left(diag, one, other, refs, held, sems)
    square[...], tangent[...] = both_products(held, right0, right1)


def local_products(diag, one, other, right0, right1, wide):
    arrays, one, other = numbered(one, other)
    rows = sum(hi - lo for _, lo, hi in one) // 2
    depth, columns = right0.shape
    out = jax.ShapeDtypeStruct((rows, columns), jnp.float32)
    tile = pl.BlockSpec((rows, wide), lambda g: (0, g))
    return pl.pallas_call(
        functools.partial(local_kernel, one, other),
        grid=(columns // wide,),
        in_specs=[
            SM(),
            pl.BlockSpec((depth, wide), lambda g: (0, g)),
            pl.BlockSpec((depth, wide), lambda g: (0, g)),
        ]
        + [HB() for _ in arrays],
        out_specs=[tile, tile],
        out_shape=[out, out],
        scratch_shapes=[
            pltpu.VMEM((2 * rows, depth), right0.dtype),
            pltpu.SemaphoreType.DMA((max(len(one), len(other)),)),
        ],
        compiler_params=params(),
        cost_estimate=cost(6 * rows * depth * columns, 8 * rows * depth + 4 * depth * columns),
        name="own_products",
    )(diag, right0, right1, *arrays)


def partial_kernel(one, other, many, cuts, diag, right0, right1, *refs):
    given = len(cuts)
    out, passed = refs[-5 - given], refs[-4 - given : -4]
    held, steps, sems, hand_sems = refs[-4:]
    others = [
        pltpu.make_async_copy(x.at[pl.ds(lo, hi - lo)], y, hand_sems.at[i])
        for i, (x, y, (lo, hi)) in enumerate(zip(refs[many : many + given], passed, cuts))
    ]

    @pl.when(pl.program_id(0) == 0)
    def _():
        for copy in others:
            copy.start()

    rows, wide = held.shape[0] // 2, right0.shape[1]
    step = pl.program_id(0)
    tiles = wide // BLOCK
    across = pl.num_programs(0) * tiles
    fetch_left(diag, one, other, refs, held, sems)
    for which, values in enumerate(both_products(held, right0, right1)):
        top = jnp.maximum(jnp.max(jnp.abs(values), axis=0, keepdims=True), 1e-30)
        level = jnp.ceil(jnp.log(top) * (STEPS / LN2)) + 1.0
        coded = jnp.round(values * (LEVELS * jnp.exp(level * (-LN2 / STEPS))))
        coded = jnp.clip(coded, -32767.0, 32767.0).astype(jnp.int32).astype(jnp.int16)
        for t in range(tiles):
            at = which * across + step * tiles + t
            cut = slice(t * BLOCK, (t + 1) * BLOCK)
            out[pl.ds(pl.multiple_of(at * rows, rows), rows), :] = coded[:, cut]
            steps[pl.ds(at, 1), :] = level[:, cut]

    @pl.when(step == pl.num_programs(0) - 1)
    def _():
        tail = steps.shape[0]
        out[out.shape[0] - tail :, :] = steps[...].astype(jnp.int32).astype(jnp.int16)
        for copy in others:
            copy.wait()


def partial_products(diag, one, other, right0, right1, wide, given=(), gates=()):
    arrays, one, other = numbered(one, other)
    rows = sum(hi - lo for _, lo, hi in one) // 2
    depth, columns = right0.shape
    tiles = 2 * columns // BLOCK
    tail = -(-tiles // 16) * 16
    return pl.pallas_call(
        functools.partial(partial_kernel, one, other, len(arrays), [cut for _, *cut in given]),
        grid=(columns // wide,),
        in_specs=[
            SM(),
            pl.BlockSpec((depth, wide), lambda g: (0, g)),
            pl.BlockSpec((depth, wide), lambda g: (0, g)),
        ]
        + [HB() for _ in (*arrays, *given, *gates)],
        out_specs=[pl.BlockSpec((tiles * rows + tail, BLOCK), lambda g: (0, 0))]
        + [HB() for _ in given],
        out_shape=[jax.ShapeDtypeStruct((tiles * rows + tail, BLOCK), jnp.int16)]
        + [jax.ShapeDtypeStruct((hi - lo, x.shape[1]), x.dtype) for x, lo, hi in given],
        scratch_shapes=[
            pltpu.VMEM((2 * rows, depth), right0.dtype),
            pltpu.VMEM((tail, BLOCK), jnp.float32),
            pltpu.SemaphoreType.DMA((max(len(one), len(other)),)),
            pltpu.SemaphoreType.DMA((max(len(given), 1),)),
        ],
        compiler_params=params(),
        cost_estimate=cost(6 * rows * depth * columns, 4 * rows * depth + 4 * depth * columns),
        name="partial_products",
    )(diag, right0, right1, *arrays, *(x for x, _, _ in given), *gates)


def finish_kernel(start, cuts, keep, coded, square, tangent, *rest):
    many = len(cuts)
    given, outs, passed = rest[:many], rest[-5 - many : -3 - many], rest[-3 - many : -3]
    made, out_sems, sems = rest[-3:]
    rows, columns = square.shape
    across = columns // BLOCK
    others = [
        pltpu.make_async_copy(x.at[pl.ds(lo, hi - lo)], y, sems.at[i])
        for i, (x, y, (lo, hi)) in enumerate(zip(given, passed, cuts))
    ]
    results = [
        pltpu.make_async_copy(made.at[i], x.at[pl.ds(start, rows)], out_sems.at[i])
        for i, x in enumerate(outs)
    ]
    for copy in others:
        copy.start()
    tail = coded.shape[0] - 2 * across * rows
    levels = coded[coded.shape[0] - tail :, :].astype(jnp.int32).astype(jnp.float32)
    steps = jnp.exp(levels * (LN2 / STEPS)) * (1.0 / LEVELS)
    for which, mine in enumerate((square, tangent)):
        for j in range(across):
            tile = which * across + j
            cut = slice(j * BLOCK, (j + 1) * BLOCK)
            other = coded[tile * rows : (tile + 1) * rows, :].astype(jnp.int32).astype(jnp.float32)
            total = mine[:, cut] + other * steps[tile : tile + 1, :]
            for row_block, part in row_pieces(start, rows):
                kept = total[part] * keep[row_block, j].astype(jnp.float32)
                made[which, part, cut] = kept.astype(made.dtype)
        results[which].start()
    for copy in results + others:
        copy.wait()


def finished(keep, square, tangent, coded, before, start, all_rows, held=(), after=()):
    rows, columns = square.shape
    out = jax.ShapeDtypeStruct((all_rows, columns), jnp.bfloat16)
    held, before = list(held), list(before)
    passed = [jax.ShapeDtypeStruct((hi - lo, x.shape[1]), x.dtype) for x, lo, hi in held]
    many = len(held)
    return pl.pallas_call(
        functools.partial(finish_kernel, start, [cut for _, *cut in held]),
        in_specs=[SM(), VM(), VM(), VM()] + [HB() for _ in (*held, *before, *after)],
        out_specs=[HB() for _ in range(2 + many)],
        out_shape=[out, out] + passed,
        input_output_aliases={4 + many: 0, 5 + many: 1} if before else {},
        scratch_shapes=[
            pltpu.VMEM((2, rows, columns), jnp.bfloat16),
            pltpu.SemaphoreType.DMA((2,)),
            pltpu.SemaphoreType.DMA((max(many, 1),)),
        ],
        compiler_params=params(),
        cost_estimate=cost(0, 16 * rows * columns),
        name="finish",
    )(keep, coded, square, tangent, *(x for x, _, _ in held), *before, *after)


def per_device_pair(
    n_row, x0_rows, x1_rows, x0_cols, x1_cols, mask0_rows, mask1_rows, mask0_cols, mask1_cols, keep
):
    n_col = 2
    group = n_row // n_col
    panel = x0_cols.shape[0]
    all_rows = x0_rows.shape[0]
    row_index = lax.axis_index("row")
    half = row_index // group
    diag = (half == lax.axis_index("col")).astype(jnp.int32).reshape(1)
    place = (row_index % group).astype(jnp.int32).reshape(1)
    direct = all_rows // 16
    split = all_rows // 2
    wide = 256

    def device(h, q, c):
        return (h * group + q) * n_col + c

    spots = [(h, q, c) for h in range(2) for q in range(group) for c in range(2)]
    over_y = [(device(h, q, c), device(h, q, 1 - c)) for h, q, c in spots]
    over_z = [(device(h, q, c), device(1 - h, q, c)) for h, q, c in spots]
    ring = [
        (device(h, q, c), device(h, q, 1 - c) if h == c else device(1 - h, q, c))
        for h, q, c in spots
    ]
    in_chip = [(device(h, q, c), device(h, q ^ 1, c)) for h, q, c in spots]

    def move(values, pairs):
        return lax.ppermute(values, ("row", "col"), pairs)

    def chunks(spans, stacked, limit, after=()):
        inputs = (place, mask0_rows, mask1_rows, x0_rows, x1_rows)
        return masked_chunks(*inputs, spans, stacked, panel, limit, after)

    def partials(one, other, **more):
        return partial_products(diag, one, other, right0, right1, wide, **more)

    def own(one, other):
        return local_products(diag, one, other, right0, right1, wide)

    def parts(joint, a, b):
        top, low = piece(joint, 0, direct), piece(joint, direct)
        return (top, piece(a), low, piece(b))

    joint, a1, b1 = chunks(((0, direct), (direct, split)), True, ALL_VMEM_BYTES)
    passed1 = move(b1, over_y)
    near0 = move(joint, ring)
    a2, b2 = chunks(((split, all_rows),), False, VMEM_BYTES, (a1,))
    right0, right1 = masked_right(mask0_cols, mask1_cols, x0_cols, x1_cols, (a2,))
    send, b2 = chosen(diag, passed1, a1, (b2,), (near0, right0))
    near1 = move(send, over_z)
    passed2 = move(b2, over_y)
    far0 = move(near0, over_y)
    send, a1 = chosen(diag, passed2, a2, (a1,), (far0,))
    near2 = move(send, over_z)
    got1 = move(a1, over_y)
    far1 = move(near1, over_y)
    (coded,) = partials(parts(near0, near1, far1), parts(far0, far1, near1))
    coded, near2 = handed_on((coded, near2), (got1,))
    back = move(coded, over_z)
    far2 = move(near2, over_y)
    sums = own(parts(joint, a1, b1), parts(near0, got1, passed1))
    coded, rest, mark = partials(
        (piece(near2), piece(far2)),
        (piece(far2), piece(near2)),
        given=(piece(a2), piece(near1, 0, all_rows // 4)),
        gates=sums[:1],
    )
    (mark,) = handed_on((mark,), (back,))
    mark = move(mark, in_chip)
    outs = finished(keep, *sums, back, (), 0, all_rows)
    back = move(coded, over_z)
    got2 = move(rest, over_y)
    sums = own((piece(a2), piece(b2)), (piece(got2), piece(passed2)))
    return tuple(finished(keep, *sums, back, outs, split, all_rows, after=(mark,)))


def passed_along(shard, axis, by):
    devices = lax.axis_size(axis)
    return lax.ppermute(shard, axis, [(i, (i + by) % devices) for i in range(devices)])


def masked(values, mask):
    rows_b, cols_b = mask.shape
    tiles = values.reshape(rows_b, BLOCK, cols_b, BLOCK)
    return (tiles * mask.astype(values.dtype)[:, None, :, None]).reshape(values.shape)


def per_device(
    x0_rows, x1_rows, x0_cols, x1_cols, mask0_rows, mask1_rows, mask0_cols, mask1_cols, keep_mask
):
    n_row = lax.axis_size("row")
    n_col = lax.axis_size("col")
    group = n_row // n_col
    row_index = lax.axis_index("row")
    col_index = lax.axis_index("col")
    panel = x0_cols.shape[0]
    start = row_index % group * panel
    block_start = row_index % group * (panel // BLOCK)
    left_zero = masked(
        lax.dynamic_slice_in_dim(x0_rows, start, panel, 1),
        lax.dynamic_slice_in_dim(mask0_rows, block_start, panel // BLOCK, 1),
    )
    left_one = masked(
        lax.dynamic_slice_in_dim(x1_rows, start, panel, 1),
        lax.dynamic_slice_in_dim(mask1_rows, block_start, panel // BLOCK, 1),
    )
    right_zero = masked(x0_cols, mask0_cols)
    right_one = masked(x1_cols, mask1_cols)
    left = jnp.stack([left_zero, left_one])
    right = jnp.stack([right_zero, right_one])
    left_offset = row_index // group % n_col
    right_offset = col_index % n_col
    levels = n_col.bit_length() - 1
    for level in range(levels):
        moved_left = passed_along(left, "col", -(1 << level))
        moved_right = passed_along(right, "row", -group * (1 << level))
        left = jnp.where(left_offset // (1 << level) % 2 == 1, moved_left, left)
        right = jnp.where(right_offset // (1 << level) % 2 == 1, moved_right, right)

    def accumulate(left_now, right_now, square, tangent):
        square = square + jnp.dot(left_now[0], right_now[0], preferred_element_type=jnp.float32)
        tangent = tangent + jnp.dot(left_now[0], right_now[1], preferred_element_type=jnp.float32)
        tangent = tangent + jnp.dot(left_now[1], right_now[0], preferred_element_type=jnp.float32)
        return (square, tangent)

    def section_body(section, carry):
        left_now, right_now, square, tangent = carry
        square, tangent = accumulate(left_now, right_now, square, tangent)
        left_now = passed_along(left_now, "col", -1)
        right_now = passed_along(right_now, "row", -group)
        return (left_now, right_now, square, tangent)

    zeros = jnp.zeros((left_zero.shape[0], right_zero.shape[1]), jnp.float32)
    left, right, square, tangent = lax.fori_loop(
        0, n_col - 1, section_body, (left, right, zeros, zeros)
    )
    square, tangent = accumulate(left, right, square, tangent)
    x_square = masked(square, keep_mask).astype(jnp.bfloat16)
    x_tangent = masked(tangent, keep_mask).astype(jnp.bfloat16)
    return (x_square, x_tangent)


def solution(mesh):
    if mesh.shape["col"] == 2:
        body = functools.partial(per_device_pair, mesh.shape["row"])
    else:
        body = per_device
    return jax.shard_map(
        body,
        mesh=mesh,
        in_specs=(P("row", "col"),) * 9,
        out_specs=(P("row", "col"), P("row", "col")),
        check_vma=False,
    )
```

```python
import functools
import math

import jax
import jax.numpy as jnp
from jax import lax
from jax.experimental import pallas as pl
from jax.experimental.pallas import tpu as pltpu
from jax.sharding import PartitionSpec as P

BLOCK = 128
LEVELS = 32000.0
STEPS = 32.0
LN2 = math.log(2.0)
VMEM_BYTES = 48 * 1024 * 1024
ALL_VMEM_BYTES = 62 * 1024 * 1024

VM = functools.partial(pl.BlockSpec, memory_space=pltpu.VMEM)
SM = functools.partial(pl.BlockSpec, memory_space=pltpu.SMEM)
HB = functools.partial(pl.BlockSpec, memory_space=pl.ANY)


def params(limit=VMEM_BYTES):
    return pltpu.CompilerParams(vmem_limit_bytes=limit)


def cost(flops, moved):
    return pl.CostEstimate(flops=int(flops) // 64, bytes_accessed=int(moved) // 64, transcendentals=0)


def scaled(values, entry):
    return (values.astype(jnp.float32) * entry.astype(jnp.float32)).astype(values.dtype)


def row_pieces(start, rows):
    edges = sorted({start, start + rows} | {e for e in range(0, start + rows, BLOCK) if e > start})
    return [(lo // BLOCK, slice(lo - start, hi - start)) for lo, hi in zip(edges, edges[1:])]


def chunk_kernel(spans, stacked, panel, *refs):
    place, mask0_far, mask1_far, x0, x1 = refs[:5]
    outs = refs[-5 - 2 * len(spans) + stacked : -5]
    held, mask0, mask1, mask_sems, sems = refs[-5:]
    start, rows = spans[0][0], held.shape[1]
    blocks = panel // BLOCK
    first = place[0] * blocks
    at = pl.ds(pl.multiple_of(place[0] * panel, BLOCK), panel)
    copies = [
        pltpu.make_async_copy(mask0_far, mask0, mask_sems.at[0]),
        pltpu.make_async_copy(mask1_far, mask1, mask_sems.at[1]),
        pltpu.make_async_copy(x0.at[pl.ds(start, rows), at], held.at[0], sems.at[0]),
        pltpu.make_async_copy(x1.at[pl.ds(start, rows), at], held.at[1], sems.at[1]),
    ]
    for copy in copies:
        copy.start()
    for copy in copies:
        copy.wait()
    for n, (lo, hi) in enumerate(spans):
        for which, mask in enumerate((mask0, mask1)):
            joint = stacked and n == 0
            out = outs[0] if joint else outs[2 * n - stacked + which]
            down = which * (hi - lo) if joint else 0
            for row_block, part in row_pieces(lo, hi - lo):
                source = slice(part.start + lo - start, part.stop + lo - start)
                target = slice(part.start + down, part.stop + down)
                for j in range(blocks):
                    cut = slice(j * BLOCK, (j + 1) * BLOCK)
                    values = scaled(held[which, source, cut], mask[row_block, first + j])
                    out[target, cut] = values


def masked_chunks(place, mask0, mask1, x0, x1, spans, stacked, panel, limit, after=()):
    rows = spans[-1][1] - spans[0][0]
    outs = []
    for n, (lo, hi) in enumerate(spans):
        if stacked and n == 0:
            outs.append(jax.ShapeDtypeStruct((2 * (hi - lo), panel), x0.dtype))
        else:
            outs += [jax.ShapeDtypeStruct((hi - lo, panel), x0.dtype)] * 2
    return pl.pallas_call(
        functools.partial(chunk_kernel, spans, int(stacked), panel),
        in_specs=[SM()] + [HB() for _ in range(4 + len(after))],
        out_specs=[VM() for _ in outs],
        out_shape=outs,
        scratch_shapes=[
            pltpu.VMEM((2, rows, panel), x0.dtype),
            pltpu.SMEM(mask0.shape, mask0.dtype),
            pltpu.SMEM(mask1.shape, mask1.dtype),
            pltpu.SemaphoreType.DMA((2,)),
            pltpu.SemaphoreType.DMA((2,)),
        ],
        compiler_params=params(limit),
        cost_estimate=cost(0, 8 * rows * panel),
        name="left_chunks",
    )(place, mask0, mask1, x0, x1, *after)


def choose_kernel(gates, many, diag, *refs):
    one, other = refs[gates : gates + 2]
    held, outs, sems = refs[gates + 2 : gates + 2 + many], refs[-many - 2 : -1], refs[-1]
    others = [
        pltpu.make_async_copy(x, out, sems.at[1 + i])
        for i, (x, out) in enumerate(zip(held, outs[1:]))
    ]
    for copy in others:
        copy.start()

    @pl.when(diag[0] == 1)
    def _():
        copy = pltpu.make_async_copy(one, outs[0], sems.at[0])
        copy.start()
        copy.wait()

    @pl.when(diag[0] == 0)
    def _():
        copy = pltpu.make_async_copy(other, outs[0], sems.at[0])
        copy.start()
        copy.wait()

    for copy in others:
        copy.wait()


def chosen(diag, one, other, held=(), after=()):
    outs = [jax.ShapeDtypeStruct(x.shape, x.dtype) for x in (one, *held)]
    return pl.pallas_call(
        functools.partial(choose_kernel, len(after), len(held)),
        in_specs=[SM()] + [HB() for _ in (*after, one, other, *held)],
        out_specs=[HB() for _ in outs],
        out_shape=outs,
        scratch_shapes=[pltpu.SemaphoreType.DMA((len(outs),))],
        compiler_params=params(),
        cost_estimate=cost(0, 4 * one.size),
        name="to_send",
    )(diag, *after, one, other, *held)


def hand_kernel(many, *refs):
    sems = refs[-1]
    copies = [
        pltpu.make_async_copy(refs[i], refs[i - many - 1], sems.at[i]) for i in range(many)
    ]
    for copy in copies:
        copy.start()
    for copy in copies:
        copy.wait()


def handed_on(values, gates):
    outs = [jax.ShapeDtypeStruct(x.shape, x.dtype) for x in values]
    return pl.pallas_call(
        functools.partial(hand_kernel, len(values)),
        in_specs=[HB() for _ in (*values, *gates)],
        out_specs=[HB() for _ in outs],
        out_shape=outs,
        scratch_shapes=[pltpu.SemaphoreType.DMA((len(outs),))],
        compiler_params=params(),
        cost_estimate=cost(0, 4 * sum(x.size for x in values)),
        name="handed_on",
    )(*values, *gates)


def right_kernel(mask0, mask1, x0, x1, *rest):
    out0, out1 = rest[-2:]
    step = pl.program_id(0)
    many = x0.shape[0] // BLOCK
    for i in range(many):
        for j in range(x0.shape[1] // BLOCK):
            at = (slice(i * BLOCK, (i + 1) * BLOCK), slice(j * BLOCK, (j + 1) * BLOCK))
            out0[at] = scaled(x0[at], mask0[step * many + i, j])
            out1[at] = scaled(x1[at], mask1[step * many + i, j])


def masked_right(mask0, mask1, x0, x1, after=()):
    depth, columns = x0.shape
    tall = 2 * BLOCK
    out = jax.ShapeDtypeStruct(x0.shape, x0.dtype)
    tile = pl.BlockSpec((tall, columns), lambda g: (g, 0))
    return pl.pallas_call(
        right_kernel,
        grid=(depth // tall,),
        in_specs=[SM(), SM(), tile, tile] + [HB() for _ in after],
        out_specs=[tile, tile],
        out_shape=[out, out],
        compiler_params=params(),
        cost_estimate=cost(0, 8 * depth * columns),
        name="right_panels",
    )(mask0, mask1, x0, x1, *after)


def both_products(held, right0, right1):
    rows = held.shape[0] // 2
    first = jnp.dot(held[...], right0[...], preferred_element_type=jnp.float32)
    second = jnp.dot(held[:rows], right1[...], preferred_element_type=jnp.float32)
    return first[:rows], first[rows:] + second


def piece(array, lo=0, hi=None):
    return (array, lo, array.shape[0] if hi is None else hi)


def numbered(one, other):
    arrays = []
    for array, _, _ in (*one, *other):
        if all(array is not known for known in arrays):
            arrays.append(array)
    number = {id(array): i for i, array in enumerate(arrays)}
    return arrays, *(
        tuple((number[id(array)], lo, hi) for array, lo, hi in pieces) for pieces in (one, other)
    )


def fetched(pieces, refs, held, sems):
    copies = []
    top = 0
    for i, (which, lo, hi) in enumerate(pieces):
        source = refs[which].at[pl.ds(lo, hi - lo)]
        copies.append(pltpu.make_async_copy(source, held.at[pl.ds(top, hi - lo)], sems.at[i]))
        top += hi - lo
    for copy in copies:
        copy.start()
    for copy in copies:
        copy.wait()


def fetch_left(diag, one, other, refs, held, sems):
    first = pl.program_id(0) == 0

    @pl.when(first & (diag[0] == 1))
    def _():
        fetched(one, refs, held, sems)

    @pl.when(first & (diag[0] == 0))
    def _():
        fetched(other, refs, held, sems)


def local_kernel(one, other, diag, right0, right1, *refs):
    square, tangent, held, sems = refs[-4:]
    fetch_left(diag, one, other, refs, held, sems)
    square[...], tangent[...] = both_products(held, right0, right1)


def local_products(diag, one, other, right0, right1, wide):
    arrays, one, other = numbered(one, other)
    rows = sum(hi - lo for _, lo, hi in one) // 2
    depth, columns = right0.shape
    out = jax.ShapeDtypeStruct((rows, columns), jnp.float32)
    tile = pl.BlockSpec((rows, wide), lambda g: (0, g))
    return pl.pallas_call(
        functools.partial(local_kernel, one, other),
        grid=(columns // wide,),
        in_specs=[
            SM(),
            pl.BlockSpec((depth, wide), lambda g: (0, g)),
            pl.BlockSpec((depth, wide), lambda g: (0, g)),
        ]
        + [HB() for _ in arrays],
        out_specs=[tile, tile],
        out_shape=[out, out],
        scratch_shapes=[
            pltpu.VMEM((2 * rows, depth), right0.dtype),
            pltpu.SemaphoreType.DMA((max(len(one), len(other)),)),
        ],
        compiler_params=params(),
        cost_estimate=cost(6 * rows * depth * columns, 8 * rows * depth + 4 * depth * columns),
        name="own_products",
    )(diag, right0, right1, *arrays)


def partial_kernel(one, other, many, cuts, diag, right0, right1, *refs):
    given = len(cuts)
    out, passed = refs[-5 - given], refs[-4 - given : -4]
    held, steps, sems, hand_sems = refs[-4:]
    others = [
        pltpu.make_async_copy(x.at[pl.ds(lo, hi - lo)], y, hand_sems.at[i])
        for i, (x, y, (lo, hi)) in enumerate(zip(refs[many : many + given], passed, cuts))
    ]

    @pl.when(pl.program_id(0) == 0)
    def _():
        for copy in others:
            copy.start()

    rows, wide = held.shape[0] // 2, right0.shape[1]
    step = pl.program_id(0)
    tiles = wide // BLOCK
    across = pl.num_programs(0) * tiles
    fetch_left(diag, one, other, refs, held, sems)
    for which, values in enumerate(both_products(held, right0, right1)):
        top = jnp.maximum(jnp.max(jnp.abs(values), axis=0, keepdims=True), 1e-30)
        level = jnp.ceil(jnp.log(top) * (STEPS / LN2)) + 1.0
        coded = jnp.round(values * (LEVELS * jnp.exp(level * (-LN2 / STEPS))))
        coded = jnp.clip(coded, -32767.0, 32767.0).astype(jnp.int32).astype(jnp.int16)
        for t in range(tiles):
            at = which * across + step * tiles + t
            cut = slice(t * BLOCK, (t + 1) * BLOCK)
            out[pl.ds(pl.multiple_of(at * rows, rows), rows), :] = coded[:, cut]
            steps[pl.ds(at, 1), :] = level[:, cut]

    @pl.when(step == pl.num_programs(0) - 1)
    def _():
        tail = steps.shape[0]
        out[out.shape[0] - tail :, :] = steps[...].astype(jnp.int32).astype(jnp.int16)
        for copy in others:
            copy.wait()


def partial_products(diag, one, other, right0, right1, wide, given=(), gates=()):
    arrays, one, other = numbered(one, other)
    rows = sum(hi - lo for _, lo, hi in one) // 2
    depth, columns = right0.shape
    tiles = 2 * columns // BLOCK
    tail = -(-tiles // 16) * 16
    return pl.pallas_call(
        functools.partial(partial_kernel, one, other, len(arrays), [cut for _, *cut in given]),
        grid=(columns // wide,),
        in_specs=[
            SM(),
            pl.BlockSpec((depth, wide), lambda g: (0, g)),
            pl.BlockSpec((depth, wide), lambda g: (0, g)),
        ]
        + [HB() for _ in (*arrays, *given, *gates)],
        out_specs=[pl.BlockSpec((tiles * rows + tail, BLOCK), lambda g: (0, 0))]
        + [HB() for _ in given],
        out_shape=[jax.ShapeDtypeStruct((tiles * rows + tail, BLOCK), jnp.int16)]
        + [jax.ShapeDtypeStruct((hi - lo, x.shape[1]), x.dtype) for x, lo, hi in given],
        scratch_shapes=[
            pltpu.VMEM((2 * rows, depth), right0.dtype),
            pltpu.VMEM((tail, BLOCK), jnp.float32),
            pltpu.SemaphoreType.DMA((max(len(one), len(other)),)),
            pltpu.SemaphoreType.DMA((max(len(given), 1),)),
        ],
        compiler_params=params(),
        cost_estimate=cost(6 * rows * depth * columns, 4 * rows * depth + 4 * depth * columns),
        name="partial_products",
    )(diag, right0, right1, *arrays, *(x for x, _, _ in given), *gates)


def finish_kernel(start, cuts, keep, coded, square, tangent, *rest):
    many = len(cuts)
    given, outs, passed = rest[:many], rest[-5 - many : -3 - many], rest[-3 - many : -3]
    made, out_sems, sems = rest[-3:]
    rows, columns = square.shape
    across = columns // BLOCK
    others = [
        pltpu.make_async_copy(x.at[pl.ds(lo, hi - lo)], y, sems.at[i])
        for i, (x, y, (lo, hi)) in enumerate(zip(given, passed, cuts))
    ]
    results = [
        pltpu.make_async_copy(made.at[i], x.at[pl.ds(start, rows)], out_sems.at[i])
        for i, x in enumerate(outs)
    ]
    for copy in others:
        copy.start()
    tail = coded.shape[0] - 2 * across * rows
    levels = coded[coded.shape[0] - tail :, :].astype(jnp.int32).astype(jnp.float32)
    steps = jnp.exp(levels * (LN2 / STEPS)) * (1.0 / LEVELS)
    for which, mine in enumerate((square, tangent)):
        for j in range(across):
            tile = which * across + j
            cut = slice(j * BLOCK, (j + 1) * BLOCK)
            other = coded[tile * rows : (tile + 1) * rows, :].astype(jnp.int32).astype(jnp.float32)
            total = mine[:, cut] + other * steps[tile : tile + 1, :]
            for row_block, part in row_pieces(start, rows):
                kept = total[part] * keep[row_block, j].astype(jnp.float32)
                made[which, part, cut] = kept.astype(made.dtype)
        results[which].start()
    for copy in results + others:
        copy.wait()


def finished(keep, square, tangent, coded, before, start, all_rows, held=(), after=()):
    rows, columns = square.shape
    out = jax.ShapeDtypeStruct((all_rows, columns), jnp.bfloat16)
    held, before = list(held), list(before)
    passed = [jax.ShapeDtypeStruct((hi - lo, x.shape[1]), x.dtype) for x, lo, hi in held]
    many = len(held)
    return pl.pallas_call(
        functools.partial(finish_kernel, start, [cut for _, *cut in held]),
        in_specs=[SM(), VM(), VM(), VM()] + [HB() for _ in (*held, *before, *after)],
        out_specs=[HB() for _ in range(2 + many)],
        out_shape=[out, out] + passed,
        input_output_aliases={4 + many: 0, 5 + many: 1} if before else {},
        scratch_shapes=[
            pltpu.VMEM((2, rows, columns), jnp.bfloat16),
            pltpu.SemaphoreType.DMA((2,)),
            pltpu.SemaphoreType.DMA((max(many, 1),)),
        ],
        compiler_params=params(),
        cost_estimate=cost(0, 16 * rows * columns),
        name="finish",
    )(keep, coded, square, tangent, *(x for x, _, _ in held), *before, *after)


def per_device_pair(
    n_row, x0_rows, x1_rows, x0_cols, x1_cols, mask0_rows, mask1_rows, mask0_cols, mask1_cols, keep
):
    n_col = 2
    group = n_row // n_col
    panel = x0_cols.shape[0]
    all_rows = x0_rows.shape[0]
    row_index = lax.axis_index("row")
    half = row_index // group
    diag = (half == lax.axis_index("col")).astype(jnp.int32).reshape(1)
    place = (row_index % group).astype(jnp.int32).reshape(1)
    direct = all_rows // 8
    split = all_rows // 2
    wide = 256

    def device(h, q, c):
        return (h * group + q) * n_col + c

    spots = [(h, q, c) for h in range(2) for q in range(group) for c in range(2)]
    over_y = [(device(h, q, c), device(h, q, 1 - c)) for h, q, c in spots]
    over_z = [(device(h, q, c), device(1 - h, q, c)) for h, q, c in spots]
    ring = [
        (device(h, q, c), device(h, q, 1 - c) if h == c else device(1 - h, q, c))
        for h, q, c in spots
    ]
    in_chip = [(device(h, q, c), device(h, q ^ 1, c)) for h, q, c in spots]

    def move(values, pairs):
        return lax.ppermute(values, ("row", "col"), pairs)

    def chunks(spans, stacked, limit, after=()):
        inputs = (place, mask0_rows, mask1_rows, x0_rows, x1_rows)
        return masked_chunks(*inputs, spans, stacked, panel, limit, after)

    def partials(one, other, **more):
        return partial_products(diag, one, other, right0, right1, wide, **more)

    def own(one, other):
        return local_products(diag, one, other, right0, right1, wide)

    def parts(joint, a, b):
        top, low = piece(joint, 0, direct), piece(joint, direct)
        return (top, piece(a), low, piece(b))

    joint, a1, b1 = chunks(((0, direct), (direct, split)), True, ALL_VMEM_BYTES)
    passed1 = move(b1, over_y)
    near0 = move(joint, ring)
    a2, b2 = chunks(((split, all_rows),), False, VMEM_BYTES, (a1,))
    right0, right1 = masked_right(mask0_cols, mask1_cols, x0_cols, x1_cols, (a2,))
    send, b2 = chosen(diag, passed1, a1, (b2,), (near0, right0))
    near1 = move(send, over_z)
    passed2 = move(b2, over_y)
    far0 = move(near0, over_y)
    send, a1 = chosen(diag, passed2, a2, (a1,), (far0, near1))
    near2 = move(send, over_z)
    got1 = move(a1, over_y)
    far1 = move(near1, over_y)
    (coded,) = partials(parts(near0, near1, far1), parts(far0, far1, near1))
    coded, near2 = handed_on((coded, near2), (got1,))
    back = move(coded, over_z)
    far2 = move(near2, over_y)
    sums = own(parts(joint, a1, b1), parts(near0, got1, passed1))
    coded, rest, mark = partials(
        (piece(near2), piece(far2)),
        (piece(far2), piece(near2)),
        given=(piece(a2), piece(near1, 0, all_rows // 4)),
        gates=sums[:1],
    )
    (mark,) = handed_on((mark,), (back,))
    mark = move(mark, in_chip)
    outs = finished(keep, *sums, back, (), 0, all_rows)
    back = move(coded, over_z)
    got2 = move(rest, over_y)
    sums = own((piece(a2), piece(b2)), (piece(got2), piece(passed2)))
    return tuple(finished(keep, *sums, back, outs, split, all_rows, after=(mark,)))


def passed_along(shard, axis, by):
    devices = lax.axis_size(axis)
    return lax.ppermute(shard, axis, [(i, (i + by) % devices) for i in range(devices)])


def masked(values, mask):
    rows_b, cols_b = mask.shape
    tiles = values.reshape(rows_b, BLOCK, cols_b, BLOCK)
    return (tiles * mask.astype(values.dtype)[:, None, :, None]).reshape(values.shape)


def per_device(
    x0_rows, x1_rows, x0_cols, x1_cols, mask0_rows, mask1_rows, mask0_cols, mask1_cols, keep_mask
):
    n_row = lax.axis_size("row")
    n_col = lax.axis_size("col")
    group = n_row // n_col
    row_index = lax.axis_index("row")
    col_index = lax.axis_index("col")
    panel = x0_cols.shape[0]
    start = row_index % group * panel
    block_start = row_index % group * (panel // BLOCK)
    left_zero = masked(
        lax.dynamic_slice_in_dim(x0_rows, start, panel, 1),
        lax.dynamic_slice_in_dim(mask0_rows, block_start, panel // BLOCK, 1),
    )
    left_one = masked(
        lax.dynamic_slice_in_dim(x1_rows, start, panel, 1),
        lax.dynamic_slice_in_dim(mask1_rows, block_start, panel // BLOCK, 1),
    )
    right_zero = masked(x0_cols, mask0_cols)
    right_one = masked(x1_cols, mask1_cols)
    left = jnp.stack([left_zero, left_one])
    right = jnp.stack([right_zero, right_one])
    left_offset = row_index // group % n_col
    right_offset = col_index % n_col
    levels = n_col.bit_length() - 1
    for level in range(levels):
        moved_left = passed_along(left, "col", -(1 << level))
        moved_right = passed_along(right, "row", -group * (1 << level))
        left = jnp.where(left_offset // (1 << level) % 2 == 1, moved_left, left)
        right = jnp.where(right_offset // (1 << level) % 2 == 1, moved_right, right)

    def accumulate(left_now, right_now, square, tangent):
        square = square + jnp.dot(left_now[0], right_now[0], preferred_element_type=jnp.float32)
        tangent = tangent + jnp.dot(left_now[0], right_now[1], preferred_element_type=jnp.float32)
        tangent = tangent + jnp.dot(left_now[1], right_now[0], preferred_element_type=jnp.float32)
        return (square, tangent)

    def section_body(section, carry):
        left_now, right_now, square, tangent = carry
        square, tangent = accumulate(left_now, right_now, square, tangent)
        left_now = passed_along(left_now, "col", -1)
        right_now = passed_along(right_now, "row", -group)
        return (left_now, right_now, square, tangent)

    zeros = jnp.zeros((left_zero.shape[0], right_zero.shape[1]), jnp.float32)
    left, right, square, tangent = lax.fori_loop(
        0, n_col - 1, section_body, (left, right, zeros, zeros)
    )
    square, tangent = accumulate(left, right, square, tangent)
    x_square = masked(square, keep_mask).astype(jnp.bfloat16)
    x_tangent = masked(tangent, keep_mask).astype(jnp.bfloat16)
    return (x_square, x_tangent)


def solution(mesh):
    if mesh.shape["col"] == 2:
        body = functools.partial(per_device_pair, mesh.shape["row"])
    else:
        body = per_device
    return jax.shard_map(
        body,
        mesh=mesh,
        in_specs=(P("row", "col"),) * 9,
        out_specs=(P("row", "col"), P("row", "col")),
        check_vma=False,
    )
```

```python
import functools
import math

import jax
import jax.numpy as jnp
from jax import lax
from jax.experimental import pallas as pl
from jax.experimental.pallas import tpu as pltpu
from jax.sharding import PartitionSpec as P

BLOCK = 128
LEVELS = 32000.0
STEPS = 32.0
LN2 = math.log(2.0)
VMEM_BYTES = 48 * 1024 * 1024
ALL_VMEM_BYTES = 62 * 1024 * 1024

VM = functools.partial(pl.BlockSpec, memory_space=pltpu.VMEM)
SM = functools.partial(pl.BlockSpec, memory_space=pltpu.SMEM)
HB = functools.partial(pl.BlockSpec, memory_space=pl.ANY)


def params(limit=VMEM_BYTES):
    return pltpu.CompilerParams(vmem_limit_bytes=limit)


def cost(flops, moved):
    return pl.CostEstimate(flops=int(flops) // 64, bytes_accessed=int(moved) // 64, transcendentals=0)


def scaled(values, entry):
    return (values.astype(jnp.float32) * entry.astype(jnp.float32)).astype(values.dtype)


def row_pieces(start, rows):
    edges = sorted({start, start + rows} | {e for e in range(0, start + rows, BLOCK) if e > start})
    return [(lo // BLOCK, slice(lo - start, hi - start)) for lo, hi in zip(edges, edges[1:])]


def chunk_kernel(spans, stacked, panel, *refs):
    place, mask0_far, mask1_far, x0, x1 = refs[:5]
    outs = refs[-5 - 2 * len(spans) + stacked : -5]
    held, mask0, mask1, mask_sems, sems = refs[-5:]
    start, rows = spans[0][0], held.shape[1]
    blocks = panel // BLOCK
    first = place[0] * blocks
    at = pl.ds(pl.multiple_of(place[0] * panel, BLOCK), panel)
    copies = [
        pltpu.make_async_copy(mask0_far, mask0, mask_sems.at[0]),
        pltpu.make_async_copy(mask1_far, mask1, mask_sems.at[1]),
        pltpu.make_async_copy(x0.at[pl.ds(start, rows), at], held.at[0], sems.at[0]),
        pltpu.make_async_copy(x1.at[pl.ds(start, rows), at], held.at[1], sems.at[1]),
    ]
    for copy in copies:
        copy.start()
    for copy in copies:
        copy.wait()
    for n, (lo, hi) in enumerate(spans):
        for which, mask in enumerate((mask0, mask1)):
            joint = stacked and n == 0
            out = outs[0] if joint else outs[2 * n - stacked + which]
            down = which * (hi - lo) if joint else 0
            for row_block, part in row_pieces(lo, hi - lo):
                source = slice(part.start + lo - start, part.stop + lo - start)
                target = slice(part.start + down, part.stop + down)
                for j in range(blocks):
                    cut = slice(j * BLOCK, (j + 1) * BLOCK)
                    values = scaled(held[which, source, cut], mask[row_block, first + j])
                    out[target, cut] = values


def masked_chunks(place, mask0, mask1, x0, x1, spans, stacked, panel, limit, after=()):
    rows = spans[-1][1] - spans[0][0]
    outs = []
    for n, (lo, hi) in enumerate(spans):
        if stacked and n == 0:
            outs.append(jax.ShapeDtypeStruct((2 * (hi - lo), panel), x0.dtype))
        else:
            outs += [jax.ShapeDtypeStruct((hi - lo, panel), x0.dtype)] * 2
    return pl.pallas_call(
        functools.partial(chunk_kernel, spans, int(stacked), panel),
        in_specs=[SM()] + [HB() for _ in range(4 + len(after))],
        out_specs=[VM() for _ in outs],
        out_shape=outs,
        scratch_shapes=[
            pltpu.VMEM((2, rows, panel), x0.dtype),
            pltpu.SMEM(mask0.shape, mask0.dtype),
            pltpu.SMEM(mask1.shape, mask1.dtype),
            pltpu.SemaphoreType.DMA((2,)),
            pltpu.SemaphoreType.DMA((2,)),
        ],
        compiler_params=params(limit),
        cost_estimate=cost(0, 8 * rows * panel),
        name="left_chunks",
    )(place, mask0, mask1, x0, x1, *after)


def choose_kernel(gates, many, cuts, diag, *refs):
    one, other = refs[gates : gates + many], refs[gates + many]
    held = refs[gates + many + 1 : gates + many + 1 + len(cuts)]
    outs, sems = refs[-len(cuts) - 2 : -1], refs[-1]
    send = outs[0]
    others = [
        pltpu.make_async_copy(x.at[pl.ds(lo, hi - lo)], out, sems.at[many + i])
        for i, (x, out, (lo, hi)) in enumerate(zip(held, outs[1:], cuts))
    ]
    for copy in others:
        copy.start()

    @pl.when(diag[0] == 1)
    def _():
        fetched([(i, 0, x.shape[0]) for i, x in enumerate(one)], one, send, sems)

    @pl.when(diag[0] == 0)
    def _():
        fetched([(0, 0, other.shape[0])], [other], send, sems)

    for copy in others:
        copy.wait()


def chosen(diag, one, other, held=(), after=()):
    outs = [jax.ShapeDtypeStruct(other.shape, other.dtype)]
    outs += [jax.ShapeDtypeStruct((hi - lo, x.shape[1]), x.dtype) for x, lo, hi in held]
    return pl.pallas_call(
        functools.partial(choose_kernel, len(after), len(one), [cut for _, *cut in held]),
        in_specs=[SM()] + [HB() for _ in (*after, *one, other, *held)],
        out_specs=[HB() for _ in outs],
        out_shape=outs,
        scratch_shapes=[pltpu.SemaphoreType.DMA((len(one) + len(held),))],
        compiler_params=params(),
        cost_estimate=cost(0, 4 * other.size),
        name="to_send",
    )(diag, *after, *one, other, *(x for x, _, _ in held))


def hand_kernel(many, *refs):
    sems = refs[-1]
    copies = [
        pltpu.make_async_copy(refs[i], refs[i - many - 1], sems.at[i]) for i in range(many)
    ]
    for copy in copies:
        copy.start()
    for copy in copies:
        copy.wait()


def handed_on(values, gates):
    outs = [jax.ShapeDtypeStruct(x.shape, x.dtype) for x in values]
    return pl.pallas_call(
        functools.partial(hand_kernel, len(values)),
        in_specs=[HB() for _ in (*values, *gates)],
        out_specs=[HB() for _ in outs],
        out_shape=outs,
        scratch_shapes=[pltpu.SemaphoreType.DMA((len(outs),))],
        compiler_params=params(),
        cost_estimate=cost(0, 4 * sum(x.size for x in values)),
        name="handed_on",
    )(*values, *gates)


def right_kernel(mask0, mask1, x0, x1, *rest):
    out0, out1 = rest[-2:]
    step = pl.program_id(0)
    many = x0.shape[0] // BLOCK
    for i in range(many):
        for j in range(x0.shape[1] // BLOCK):
            at = (slice(i * BLOCK, (i + 1) * BLOCK), slice(j * BLOCK, (j + 1) * BLOCK))
            out0[at] = scaled(x0[at], mask0[step * many + i, j])
            out1[at] = scaled(x1[at], mask1[step * many + i, j])


def masked_right(mask0, mask1, x0, x1, after=()):
    depth, columns = x0.shape
    tall = 2 * BLOCK
    out = jax.ShapeDtypeStruct(x0.shape, x0.dtype)
    tile = pl.BlockSpec((tall, columns), lambda g: (g, 0))
    return pl.pallas_call(
        right_kernel,
        grid=(depth // tall,),
        in_specs=[SM(), SM(), tile, tile] + [HB() for _ in after],
        out_specs=[tile, tile],
        out_shape=[out, out],
        compiler_params=params(),
        cost_estimate=cost(0, 8 * depth * columns),
        name="right_panels",
    )(mask0, mask1, x0, x1, *after)


def both_products(held, right0, right1):
    rows = held.shape[0] // 2
    first = jnp.dot(held[...], right0[...], preferred_element_type=jnp.float32)
    second = jnp.dot(held[:rows], right1[...], preferred_element_type=jnp.float32)
    return first[:rows], first[rows:] + second


def piece(array, lo=0, hi=None):
    return (array, lo, array.shape[0] if hi is None else hi)


def numbered(one, other):
    arrays = []
    for array, _, _ in (*one, *other):
        if all(array is not known for known in arrays):
            arrays.append(array)
    number = {id(array): i for i, array in enumerate(arrays)}
    return arrays, *(
        tuple((number[id(array)], lo, hi) for array, lo, hi in pieces) for pieces in (one, other)
    )


def fetched(pieces, refs, held, sems):
    copies = []
    top = 0
    for i, (which, lo, hi) in enumerate(pieces):
        source = refs[which].at[pl.ds(lo, hi - lo)]
        copies.append(pltpu.make_async_copy(source, held.at[pl.ds(top, hi - lo)], sems.at[i]))
        top += hi - lo
    for copy in copies:
        copy.start()
    for copy in copies:
        copy.wait()


def fetch_left(diag, one, other, refs, held, sems):
    first = pl.program_id(0) == 0

    @pl.when(first & (diag[0] == 1))
    def _():
        fetched(one, refs, held, sems)

    @pl.when(first & (diag[0] == 0))
    def _():
        fetched(other, refs, held, sems)


def local_kernel(one, other, diag, right0, right1, *refs):
    square, tangent, held, sems = refs[-4:]
    fetch_left(diag, one, other, refs, held, sems)
    square[...], tangent[...] = both_products(held, right0, right1)


def local_products(diag, one, other, right0, right1, wide):
    arrays, one, other = numbered(one, other)
    rows = sum(hi - lo for _, lo, hi in one) // 2
    depth, columns = right0.shape
    out = jax.ShapeDtypeStruct((rows, columns), jnp.float32)
    tile = pl.BlockSpec((rows, wide), lambda g: (0, g))
    return pl.pallas_call(
        functools.partial(local_kernel, one, other),
        grid=(columns // wide,),
        in_specs=[
            SM(),
            pl.BlockSpec((depth, wide), lambda g: (0, g)),
            pl.BlockSpec((depth, wide), lambda g: (0, g)),
        ]
        + [HB() for _ in arrays],
        out_specs=[tile, tile],
        out_shape=[out, out],
        scratch_shapes=[
            pltpu.VMEM((2 * rows, depth), right0.dtype),
            pltpu.SemaphoreType.DMA((max(len(one), len(other)),)),
        ],
        compiler_params=params(),
        cost_estimate=cost(6 * rows * depth * columns, 8 * rows * depth + 4 * depth * columns),
        name="own_products",
    )(diag, right0, right1, *arrays)


def partial_kernel(one, other, many, cuts, diag, right0, right1, *refs):
    given = len(cuts)
    out, passed = refs[-5 - given], refs[-4 - given : -4]
    held, steps, sems, hand_sems = refs[-4:]
    others = [
        pltpu.make_async_copy(x.at[pl.ds(lo, hi - lo)], y, hand_sems.at[i])
        for i, (x, y, (lo, hi)) in enumerate(zip(refs[many : many + given], passed, cuts))
    ]

    @pl.when(pl.program_id(0) == 0)
    def _():
        for copy in others:
            copy.start()

    rows, wide = held.shape[0] // 2, right0.shape[1]
    step = pl.program_id(0)
    tiles = wide // BLOCK
    across = pl.num_programs(0) * tiles
    fetch_left(diag, one, other, refs, held, sems)
    for which, values in enumerate(both_products(held, right0, right1)):
        top = jnp.maximum(jnp.max(jnp.abs(values), axis=0, keepdims=True), 1e-30)
        level = jnp.ceil(jnp.log(top) * (STEPS / LN2)) + 1.0
        coded = jnp.round(values * (LEVELS * jnp.exp(level * (-LN2 / STEPS))))
        coded = jnp.clip(coded, -32767.0, 32767.0).astype(jnp.int32).astype(jnp.int16)
        for t in range(tiles):
            at = which * across + step * tiles + t
            cut = slice(t * BLOCK, (t + 1) * BLOCK)
            out[pl.ds(pl.multiple_of(at * rows, rows), rows), :] = coded[:, cut]
            steps[pl.ds(at, 1), :] = level[:, cut]

    @pl.when(step == pl.num_programs(0) - 1)
    def _():
        tail = steps.shape[0]
        out[out.shape[0] - tail :, :] = steps[...].astype(jnp.int32).astype(jnp.int16)
        for copy in others:
            copy.wait()


def partial_products(diag, one, other, right0, right1, wide, given=(), gates=()):
    arrays, one, other = numbered(one, other)
    rows = sum(hi - lo for _, lo, hi in one) // 2
    depth, columns = right0.shape
    tiles = 2 * columns // BLOCK
    tail = -(-tiles // 16) * 16
    return pl.pallas_call(
        functools.partial(partial_kernel, one, other, len(arrays), [cut for _, *cut in given]),
        grid=(columns // wide,),
        in_specs=[
            SM(),
            pl.BlockSpec((depth, wide), lambda g: (0, g)),
            pl.BlockSpec((depth, wide), lambda g: (0, g)),
        ]
        + [HB() for _ in (*arrays, *given, *gates)],
        out_specs=[pl.BlockSpec((tiles * rows + tail, BLOCK), lambda g: (0, 0))]
        + [HB() for _ in given],
        out_shape=[jax.ShapeDtypeStruct((tiles * rows + tail, BLOCK), jnp.int16)]
        + [jax.ShapeDtypeStruct((hi - lo, x.shape[1]), x.dtype) for x, lo, hi in given],
        scratch_shapes=[
            pltpu.VMEM((2 * rows, depth), right0.dtype),
            pltpu.VMEM((tail, BLOCK), jnp.float32),
            pltpu.SemaphoreType.DMA((max(len(one), len(other)),)),
            pltpu.SemaphoreType.DMA((max(len(given), 1),)),
        ],
        compiler_params=params(),
        cost_estimate=cost(6 * rows * depth * columns, 4 * rows * depth + 4 * depth * columns),
        name="partial_products",
    )(diag, right0, right1, *arrays, *(x for x, _, _ in given), *gates)


def finish_kernel(start, cuts, keep, coded, square, tangent, *rest):
    many = len(cuts)
    given, outs, passed = rest[:many], rest[-5 - many : -3 - many], rest[-3 - many : -3]
    made, out_sems, sems = rest[-3:]
    rows, columns = square.shape
    across = columns // BLOCK
    others = [
        pltpu.make_async_copy(x.at[pl.ds(lo, hi - lo)], y, sems.at[i])
        for i, (x, y, (lo, hi)) in enumerate(zip(given, passed, cuts))
    ]
    results = [
        pltpu.make_async_copy(made.at[i], x.at[pl.ds(start, rows)], out_sems.at[i])
        for i, x in enumerate(outs)
    ]
    for copy in others:
        copy.start()
    tail = coded.shape[0] - 2 * across * rows
    levels = coded[coded.shape[0] - tail :, :].astype(jnp.int32).astype(jnp.float32)
    steps = jnp.exp(levels * (LN2 / STEPS)) * (1.0 / LEVELS)
    for which, mine in enumerate((square, tangent)):
        for j in range(across):
            tile = which * across + j
            cut = slice(j * BLOCK, (j + 1) * BLOCK)
            other = coded[tile * rows : (tile + 1) * rows, :].astype(jnp.int32).astype(jnp.float32)
            total = mine[:, cut] + other * steps[tile : tile + 1, :]
            for row_block, part in row_pieces(start, rows):
                kept = total[part] * keep[row_block, j].astype(jnp.float32)
                made[which, part, cut] = kept.astype(made.dtype)
        results[which].start()
    for copy in results + others:
        copy.wait()


def finished(keep, square, tangent, coded, before, start, all_rows, held=(), after=()):
    rows, columns = square.shape
    out = jax.ShapeDtypeStruct((all_rows, columns), jnp.bfloat16)
    held, before = list(held), list(before)
    passed = [jax.ShapeDtypeStruct((hi - lo, x.shape[1]), x.dtype) for x, lo, hi in held]
    many = len(held)
    return pl.pallas_call(
        functools.partial(finish_kernel, start, [cut for _, *cut in held]),
        in_specs=[SM(), VM(), VM(), VM()] + [HB() for _ in (*held, *before, *after)],
        out_specs=[HB() for _ in range(2 + many)],
        out_shape=[out, out] + passed,
        input_output_aliases={4 + many: 0, 5 + many: 1} if before else {},
        scratch_shapes=[
            pltpu.VMEM((2, rows, columns), jnp.bfloat16),
            pltpu.SemaphoreType.DMA((2,)),
            pltpu.SemaphoreType.DMA((max(many, 1),)),
        ],
        compiler_params=params(),
        cost_estimate=cost(0, 16 * rows * columns),
        name="finish",
    )(keep, coded, square, tangent, *(x for x, _, _ in held), *before, *after)


def per_device_pair(
    n_row, x0_rows, x1_rows, x0_cols, x1_cols, mask0_rows, mask1_rows, mask0_cols, mask1_cols, keep
):
    n_col = 2
    group = n_row // n_col
    panel = x0_cols.shape[0]
    all_rows = x0_rows.shape[0]
    row_index = lax.axis_index("row")
    half = row_index // group
    diag = (half == lax.axis_index("col")).astype(jnp.int32).reshape(1)
    place = (row_index % group).astype(jnp.int32).reshape(1)
    direct = all_rows // 8
    split = all_rows // 2
    wide = 256

    def device(h, q, c):
        return (h * group + q) * n_col + c

    spots = [(h, q, c) for h in range(2) for q in range(group) for c in range(2)]
    over_y = [(device(h, q, c), device(h, q, 1 - c)) for h, q, c in spots]
    over_z = [(device(h, q, c), device(1 - h, q, c)) for h, q, c in spots]
    ring = [
        (device(h, q, c), device(h, q, 1 - c) if h == c else device(1 - h, q, c))
        for h, q, c in spots
    ]
    in_chip = [(device(h, q, c), device(h, q ^ 1, c)) for h, q, c in spots]

    def move(values, pairs):
        return lax.ppermute(values, ("row", "col"), pairs)

    def chunks(spans, stacked, limit, after=()):
        inputs = (place, mask0_rows, mask1_rows, x0_rows, x1_rows)
        return masked_chunks(*inputs, spans, stacked, panel, limit, after)

    def partials(one, other, **more):
        return partial_products(diag, one, other, right0, right1, wide, **more)

    def own(one, other):
        return local_products(diag, one, other, right0, right1, wide)

    def parts(joint, a, b):
        top, low = piece(joint, 0, direct), piece(joint, direct)
        return (top, piece(a), low, piece(b))

    joint, a1, b1 = chunks(((0, direct), (direct, split)), True, ALL_VMEM_BYTES)
    passed1 = move(b1, over_y)
    near0 = move(joint, ring)
    a2, b2 = chunks(((split, all_rows),), False, VMEM_BYTES, (a1,))
    right0, right1 = masked_right(mask0_cols, mask1_cols, x0_cols, x1_cols, (a2,))
    middle = b2.shape[0] // 2
    send, top2, low2 = chosen(
        diag, (passed1,), a1, (piece(b2, 0, middle), piece(b2, middle)), (near0, right0)
    )
    near1 = move(send, over_z)
    passed2 = (move(top2, over_y), move(low2, over_y))
    far0 = move(near0, over_y)
    send, a1 = chosen(diag, passed2, a2, (piece(a1),), (far0, near1))
    near2 = move(send, over_z)
    got1 = move(a1, over_y)
    far1 = move(near1, over_y)
    (coded,) = partials(parts(near0, near1, far1), parts(far0, far1, near1))
    coded, near2 = handed_on((coded, near2), (got1,))
    back = move(coded, over_z)
    far2 = move(near2, over_y)
    sums = own(parts(joint, a1, b1), parts(near0, got1, passed1))
    coded, *rest, mark = partials(
        (piece(near2), piece(far2)),
        (piece(far2), piece(near2)),
        given=(piece(a2, 0, middle), piece(a2, middle), piece(near1, 0, all_rows // 4)),
        gates=sums[:1],
    )
    (mark,) = handed_on((mark,), (back,))
    mark = move(mark, in_chip)
    outs = finished(keep, *sums, back, (), 0, all_rows)
    back = move(coded, over_z)
    got2 = [move(part, over_y) for part in rest]
    sums = own((piece(a2), piece(b2)), (*map(piece, got2), *map(piece, passed2)))
    return tuple(finished(keep, *sums, back, outs, split, all_rows, after=(mark,)))


def passed_along(shard, axis, by):
    devices = lax.axis_size(axis)
    return lax.ppermute(shard, axis, [(i, (i + by) % devices) for i in range(devices)])


def masked(values, mask):
    rows_b, cols_b = mask.shape
    tiles = values.reshape(rows_b, BLOCK, cols_b, BLOCK)
    return (tiles * mask.astype(values.dtype)[:, None, :, None]).reshape(values.shape)


def per_device(
    x0_rows, x1_rows, x0_cols, x1_cols, mask0_rows, mask1_rows, mask0_cols, mask1_cols, keep_mask
):
    n_row = lax.axis_size("row")
    n_col = lax.axis_size("col")
    group = n_row // n_col
    row_index = lax.axis_index("row")
    col_index = lax.axis_index("col")
    panel = x0_cols.shape[0]
    start = row_index % group * panel
    block_start = row_index % group * (panel // BLOCK)
    left_zero = masked(
        lax.dynamic_slice_in_dim(x0_rows, start, panel, 1),
        lax.dynamic_slice_in_dim(mask0_rows, block_start, panel // BLOCK, 1),
    )
    left_one = masked(
        lax.dynamic_slice_in_dim(x1_rows, start, panel, 1),
        lax.dynamic_slice_in_dim(mask1_rows, block_start, panel // BLOCK, 1),
    )
    right_zero = masked(x0_cols, mask0_cols)
    right_one = masked(x1_cols, mask1_cols)
    left = jnp.stack([left_zero, left_one])
    right = jnp.stack([right_zero, right_one])
    left_offset = row_index // group % n_col
    right_offset = col_index % n_col
    levels = n_col.bit_length() - 1
    for level in range(levels):
        moved_left = passed_along(left, "col", -(1 << level))
        moved_right = passed_along(right, "row", -group * (1 << level))
        left = jnp.where(left_offset // (1 << level) % 2 == 1, moved_left, left)
        right = jnp.where(right_offset // (1 << level) % 2 == 1, moved_right, right)

    def accumulate(left_now, right_now, square, tangent):
        square = square + jnp.dot(left_now[0], right_now[0], preferred_element_type=jnp.float32)
        tangent = tangent + jnp.dot(left_now[0], right_now[1], preferred_element_type=jnp.float32)
        tangent = tangent + jnp.dot(left_now[1], right_now[0], preferred_element_type=jnp.float32)
        return (square, tangent)

    def section_body(section, carry):
        left_now, right_now, square, tangent = carry
        square, tangent = accumulate(left_now, right_now, square, tangent)
        left_now = passed_along(left_now, "col", -1)
        right_now = passed_along(right_now, "row", -group)
        return (left_now, right_now, square, tangent)

    zeros = jnp.zeros((left_zero.shape[0], right_zero.shape[1]), jnp.float32)
    left, right, square, tangent = lax.fori_loop(
        0, n_col - 1, section_body, (left, right, zeros, zeros)
    )
    square, tangent = accumulate(left, right, square, tangent)
    x_square = masked(square, keep_mask).astype(jnp.bfloat16)
    x_tangent = masked(tangent, keep_mask).astype(jnp.bfloat16)
    return (x_square, x_tangent)


def solution(mesh):
    if mesh.shape["col"] == 2:
        body = functools.partial(per_device_pair, mesh.shape["row"])
    else:
        body = per_device
    return jax.shard_map(
        body,
        mesh=mesh,
        in_specs=(P("row", "col"),) * 9,
        out_specs=(P("row", "col"), P("row", "col")),
        check_vma=False,
    )
```

```python
import functools
import math

import jax
import jax.numpy as jnp
from jax import lax
from jax.experimental import pallas as pl
from jax.experimental.pallas import tpu as pltpu
from jax.sharding import PartitionSpec as P

BLOCK = 128
LEVELS = 32000.0
STEPS = 32.0
LN2 = math.log(2.0)
VMEM_BYTES = 48 * 1024 * 1024
ALL_VMEM_BYTES = 62 * 1024 * 1024

VM = functools.partial(pl.BlockSpec, memory_space=pltpu.VMEM)
SM = functools.partial(pl.BlockSpec, memory_space=pltpu.SMEM)
HB = functools.partial(pl.BlockSpec, memory_space=pl.ANY)


def params(limit=VMEM_BYTES):
    return pltpu.CompilerParams(vmem_limit_bytes=limit)


def cost(flops, moved):
    return pl.CostEstimate(flops=int(flops) // 64, bytes_accessed=int(moved) // 64, transcendentals=0)


def scaled(values, entry):
    return (values.astype(jnp.float32) * entry.astype(jnp.float32)).astype(values.dtype)


def row_pieces(start, rows):
    edges = sorted({start, start + rows} | {e for e in range(0, start + rows, BLOCK) if e > start})
    return [(lo // BLOCK, slice(lo - start, hi - start)) for lo, hi in zip(edges, edges[1:])]


def chunk_kernel(spans, stacked, panel, *refs):
    place, mask0_far, mask1_far, x0, x1 = refs[:5]
    outs = refs[-5 - 2 * len(spans) + stacked : -5]
    held, mask0, mask1, mask_sems, sems = refs[-5:]
    start, rows = spans[0][0], held.shape[1]
    blocks = panel // BLOCK
    first = place[0] * blocks
    at = pl.ds(pl.multiple_of(place[0] * panel, BLOCK), panel)
    copies = [
        pltpu.make_async_copy(mask0_far, mask0, mask_sems.at[0]),
        pltpu.make_async_copy(mask1_far, mask1, mask_sems.at[1]),
        pltpu.make_async_copy(x0.at[pl.ds(start, rows), at], held.at[0], sems.at[0]),
        pltpu.make_async_copy(x1.at[pl.ds(start, rows), at], held.at[1], sems.at[1]),
    ]
    for copy in copies:
        copy.start()
    for copy in copies:
        copy.wait()
    for n, (lo, hi) in enumerate(spans):
        for which, mask in enumerate((mask0, mask1)):
            joint = stacked and n == 0
            out = outs[0] if joint else outs[2 * n - stacked + which]
            down = which * (hi - lo) if joint else 0
            for row_block, part in row_pieces(lo, hi - lo):
                source = slice(part.start + lo - start, part.stop + lo - start)
                target = slice(part.start + down, part.stop + down)
                for j in range(blocks):
                    cut = slice(j * BLOCK, (j + 1) * BLOCK)
                    values = scaled(held[which, source, cut], mask[row_block, first + j])
                    out[target, cut] = values


def masked_chunks(place, mask0, mask1, x0, x1, spans, stacked, panel, limit, after=()):
    rows = spans[-1][1] - spans[0][0]
    outs = []
    for n, (lo, hi) in enumerate(spans):
        if stacked and n == 0:
            outs.append(jax.ShapeDtypeStruct((2 * (hi - lo), panel), x0.dtype))
        else:
            outs += [jax.ShapeDtypeStruct((hi - lo, panel), x0.dtype)] * 2
    return pl.pallas_call(
        functools.partial(chunk_kernel, spans, int(stacked), panel),
        in_specs=[SM()] + [HB() for _ in range(4 + len(after))],
        out_specs=[VM() for _ in outs],
        out_shape=outs,
        scratch_shapes=[
            pltpu.VMEM((2, rows, panel), x0.dtype),
            pltpu.SMEM(mask0.shape, mask0.dtype),
            pltpu.SMEM(mask1.shape, mask1.dtype),
            pltpu.SemaphoreType.DMA((2,)),
            pltpu.SemaphoreType.DMA((2,)),
        ],
        compiler_params=params(limit),
        cost_estimate=cost(0, 8 * rows * panel),
        name="left_chunks",
    )(place, mask0, mask1, x0, x1, *after)


def choose_kernel(gates, many, cuts, diag, *refs):
    one, other = refs[gates : gates + many], refs[gates + many]
    held = refs[gates + many + 1 : gates + many + 1 + len(cuts)]
    outs, sems = refs[-len(cuts) - 2 : -1], refs[-1]
    send = outs[0]
    others = [
        pltpu.make_async_copy(x.at[pl.ds(lo, hi - lo)], out, sems.at[many + i])
        for i, (x, out, (lo, hi)) in enumerate(zip(held, outs[1:], cuts))
    ]
    for copy in others:
        copy.start()

    @pl.when(diag[0] == 1)
    def _():
        fetched([(i, 0, x.shape[0]) for i, x in enumerate(one)], one, send, sems)

    @pl.when(diag[0] == 0)
    def _():
        fetched([(0, 0, other.shape[0])], [other], send, sems)

    for copy in others:
        copy.wait()


def chosen(diag, one, other, held=(), after=()):
    outs = [jax.ShapeDtypeStruct(other.shape, other.dtype)]
    outs += [jax.ShapeDtypeStruct((hi - lo, x.shape[1]), x.dtype) for x, lo, hi in held]
    return pl.pallas_call(
        functools.partial(choose_kernel, len(after), len(one), [cut for _, *cut in held]),
        in_specs=[SM()] + [HB() for _ in (*after, *one, other, *held)],
        out_specs=[HB() for _ in outs],
        out_shape=outs,
        scratch_shapes=[pltpu.SemaphoreType.DMA((len(one) + len(held),))],
        compiler_params=params(),
        cost_estimate=cost(0, 4 * other.size),
        name="to_send",
    )(diag, *after, *one, other, *(x for x, _, _ in held))


def hand_kernel(many, *refs):
    sems = refs[-1]
    copies = [
        pltpu.make_async_copy(refs[i], refs[i - many - 1], sems.at[i]) for i in range(many)
    ]
    for copy in copies:
        copy.start()
    for copy in copies:
        copy.wait()


def handed_on(values, gates):
    outs = [jax.ShapeDtypeStruct(x.shape, x.dtype) for x in values]
    return pl.pallas_call(
        functools.partial(hand_kernel, len(values)),
        in_specs=[HB() for _ in (*values, *gates)],
        out_specs=[HB() for _ in outs],
        out_shape=outs,
        scratch_shapes=[pltpu.SemaphoreType.DMA((len(outs),))],
        compiler_params=params(),
        cost_estimate=cost(0, 4 * sum(x.size for x in values)),
        name="handed_on",
    )(*values, *gates)


def right_kernel(mask0, mask1, x0, x1, *rest):
    out0, out1 = rest[-2:]
    step = pl.program_id(0)
    many = x0.shape[0] // BLOCK
    for i in range(many):
        for j in range(x0.shape[1] // BLOCK):
            at = (slice(i * BLOCK, (i + 1) * BLOCK), slice(j * BLOCK, (j + 1) * BLOCK))
            out0[at] = scaled(x0[at], mask0[step * many + i, j])
            out1[at] = scaled(x1[at], mask1[step * many + i, j])


def masked_right(mask0, mask1, x0, x1, after=()):
    depth, columns = x0.shape
    tall = 2 * BLOCK
    out = jax.ShapeDtypeStruct(x0.shape, x0.dtype)
    tile = pl.BlockSpec((tall, columns), lambda g: (g, 0))
    return pl.pallas_call(
        right_kernel,
        grid=(depth // tall,),
        in_specs=[SM(), SM(), tile, tile] + [HB() for _ in after],
        out_specs=[tile, tile],
        out_shape=[out, out],
        compiler_params=params(),
        cost_estimate=cost(0, 8 * depth * columns),
        name="right_panels",
    )(mask0, mask1, x0, x1, *after)


def both_products(held, right0, right1):
    rows = held.shape[0] // 2
    first = jnp.dot(held[...], right0[...], preferred_element_type=jnp.float32)
    second = jnp.dot(held[:rows], right1[...], preferred_element_type=jnp.float32)
    return first[:rows], first[rows:] + second


def piece(array, lo=0, hi=None):
    return (array, lo, array.shape[0] if hi is None else hi)


def numbered(one, other):
    arrays = []
    for array, _, _ in (*one, *other):
        if all(array is not known for known in arrays):
            arrays.append(array)
    number = {id(array): i for i, array in enumerate(arrays)}
    return arrays, *(
        tuple((number[id(array)], lo, hi) for array, lo, hi in pieces) for pieces in (one, other)
    )


def fetched(pieces, refs, held, sems):
    copies = []
    top = 0
    for i, (which, lo, hi) in enumerate(pieces):
        source = refs[which].at[pl.ds(lo, hi - lo)]
        copies.append(pltpu.make_async_copy(source, held.at[pl.ds(top, hi - lo)], sems.at[i]))
        top += hi - lo
    for copy in copies:
        copy.start()
    for copy in copies:
        copy.wait()


def fetch_left(diag, one, other, refs, held, sems):
    first = pl.program_id(0) == 0

    @pl.when(first & (diag[0] == 1))
    def _():
        fetched(one, refs, held, sems)

    @pl.when(first & (diag[0] == 0))
    def _():
        fetched(other, refs, held, sems)


def local_kernel(one, other, diag, right0, right1, *refs):
    square, tangent, held, sems = refs[-4:]
    fetch_left(diag, one, other, refs, held, sems)
    square[...], tangent[...] = both_products(held, right0, right1)


def local_products(diag, one, other, right0, right1, wide):
    arrays, one, other = numbered(one, other)
    rows = sum(hi - lo for _, lo, hi in one) // 2
    depth, columns = right0.shape
    out = jax.ShapeDtypeStruct((rows, columns), jnp.float32)
    tile = pl.BlockSpec((rows, wide), lambda g: (0, g))
    return pl.pallas_call(
        functools.partial(local_kernel, one, other),
        grid=(columns // wide,),
        in_specs=[
            SM(),
            pl.BlockSpec((depth, wide), lambda g: (0, g)),
            pl.BlockSpec((depth, wide), lambda g: (0, g)),
        ]
        + [HB() for _ in arrays],
        out_specs=[tile, tile],
        out_shape=[out, out],
        scratch_shapes=[
            pltpu.VMEM((2 * rows, depth), right0.dtype),
            pltpu.SemaphoreType.DMA((max(len(one), len(other)),)),
        ],
        compiler_params=params(),
        cost_estimate=cost(6 * rows * depth * columns, 8 * rows * depth + 4 * depth * columns),
        name="own_products",
    )(diag, right0, right1, *arrays)


def partial_kernel(one, other, many, cuts, diag, right0, right1, *refs):
    given = len(cuts)
    out, passed = refs[-5 - given], refs[-4 - given : -4]
    held, steps, sems, hand_sems = refs[-4:]
    others = [
        pltpu.make_async_copy(x.at[pl.ds(lo, hi - lo)], y, hand_sems.at[i])
        for i, (x, y, (lo, hi)) in enumerate(zip(refs[many : many + given], passed, cuts))
    ]

    @pl.when(pl.program_id(0) == 0)
    def _():
        for copy in others:
            copy.start()

    rows, wide = held.shape[0] // 2, right0.shape[1]
    step = pl.program_id(0)
    tiles = wide // BLOCK
    across = pl.num_programs(0) * tiles
    fetch_left(diag, one, other, refs, held, sems)
    for which, values in enumerate(both_products(held, right0, right1)):
        top = jnp.maximum(jnp.max(jnp.abs(values), axis=0, keepdims=True), 1e-30)
        level = jnp.ceil(jnp.log(top) * (STEPS / LN2)) + 1.0
        coded = jnp.round(values * (LEVELS * jnp.exp(level * (-LN2 / STEPS))))
        coded = jnp.clip(coded, -32767.0, 32767.0).astype(jnp.int32).astype(jnp.int16)
        for t in range(tiles):
            at = which * across + step * tiles + t
            cut = slice(t * BLOCK, (t + 1) * BLOCK)
            out[pl.ds(pl.multiple_of(at * rows, rows), rows), :] = coded[:, cut]
            steps[pl.ds(at, 1), :] = level[:, cut]

    @pl.when(step == pl.num_programs(0) - 1)
    def _():
        tail = steps.shape[0]
        out[out.shape[0] - tail :, :] = steps[...].astype(jnp.int32).astype(jnp.int16)
        for copy in others:
            copy.wait()


def partial_products(diag, one, other, right0, right1, wide, given=(), gates=()):
    arrays, one, other = numbered(one, other)
    rows = sum(hi - lo for _, lo, hi in one) // 2
    depth, columns = right0.shape
    tiles = 2 * columns // BLOCK
    tail = -(-tiles // 16) * 16
    return pl.pallas_call(
        functools.partial(partial_kernel, one, other, len(arrays), [cut for _, *cut in given]),
        grid=(columns // wide,),
        in_specs=[
            SM(),
            pl.BlockSpec((depth, wide), lambda g: (0, g)),
            pl.BlockSpec((depth, wide), lambda g: (0, g)),
        ]
        + [HB() for _ in (*arrays, *given, *gates)],
        out_specs=[pl.BlockSpec((tiles * rows + tail, BLOCK), lambda g: (0, 0))]
        + [HB() for _ in given],
        out_shape=[jax.ShapeDtypeStruct((tiles * rows + tail, BLOCK), jnp.int16)]
        + [jax.ShapeDtypeStruct((hi - lo, x.shape[1]), x.dtype) for x, lo, hi in given],
        scratch_shapes=[
            pltpu.VMEM((2 * rows, depth), right0.dtype),
            pltpu.VMEM((tail, BLOCK), jnp.float32),
            pltpu.SemaphoreType.DMA((max(len(one), len(other)),)),
            pltpu.SemaphoreType.DMA((max(len(given), 1),)),
        ],
        compiler_params=params(),
        cost_estimate=cost(6 * rows * depth * columns, 4 * rows * depth + 4 * depth * columns),
        name="partial_products",
    )(diag, right0, right1, *arrays, *(x for x, _, _ in given), *gates)


def finish_kernel(start, cuts, keep, coded, square, tangent, *rest):
    many = len(cuts)
    given, outs, passed = rest[:many], rest[-5 - many : -3 - many], rest[-3 - many : -3]
    made, out_sems, sems = rest[-3:]
    rows, columns = square.shape
    across = columns // BLOCK
    others = [
        pltpu.make_async_copy(x.at[pl.ds(lo, hi - lo)], y, sems.at[i])
        for i, (x, y, (lo, hi)) in enumerate(zip(given, passed, cuts))
    ]
    results = [
        pltpu.make_async_copy(made.at[i], x.at[pl.ds(start, rows)], out_sems.at[i])
        for i, x in enumerate(outs)
    ]
    for copy in others:
        copy.start()
    tail = coded.shape[0] - 2 * across * rows
    levels = coded[coded.shape[0] - tail :, :].astype(jnp.int32).astype(jnp.float32)
    steps = jnp.exp(levels * (LN2 / STEPS)) * (1.0 / LEVELS)
    for which, mine in enumerate((square, tangent)):
        for j in range(across):
            tile = which * across + j
            cut = slice(j * BLOCK, (j + 1) * BLOCK)
            other = coded[tile * rows : (tile + 1) * rows, :].astype(jnp.int32).astype(jnp.float32)
            total = mine[:, cut] + other * steps[tile : tile + 1, :]
            for row_block, part in row_pieces(start, rows):
                kept = total[part] * keep[row_block, j].astype(jnp.float32)
                made[which, part, cut] = kept.astype(made.dtype)
        results[which].start()
    for copy in results + others:
        copy.wait()


def finished(keep, square, tangent, coded, before, start, all_rows, held=(), after=()):
    rows, columns = square.shape
    out = jax.ShapeDtypeStruct((all_rows, columns), jnp.bfloat16)
    held, before = list(held), list(before)
    passed = [jax.ShapeDtypeStruct((hi - lo, x.shape[1]), x.dtype) for x, lo, hi in held]
    many = len(held)
    return pl.pallas_call(
        functools.partial(finish_kernel, start, [cut for _, *cut in held]),
        in_specs=[SM(), VM(), VM(), VM()] + [HB() for _ in (*held, *before, *after)],
        out_specs=[HB() for _ in range(2 + many)],
        out_shape=[out, out] + passed,
        input_output_aliases={4 + many: 0, 5 + many: 1} if before else {},
        scratch_shapes=[
            pltpu.VMEM((2, rows, columns), jnp.bfloat16),
            pltpu.SemaphoreType.DMA((2,)),
            pltpu.SemaphoreType.DMA((max(many, 1),)),
        ],
        compiler_params=params(),
        cost_estimate=cost(0, 16 * rows * columns),
        name="finish",
    )(keep, coded, square, tangent, *(x for x, _, _ in held), *before, *after)


def per_device_pair(
    n_row, x0_rows, x1_rows, x0_cols, x1_cols, mask0_rows, mask1_rows, mask0_cols, mask1_cols, keep
):
    n_col = 2
    group = n_row // n_col
    panel = x0_cols.shape[0]
    all_rows = x0_rows.shape[0]
    row_index = lax.axis_index("row")
    half = row_index // group
    diag = (half == lax.axis_index("col")).astype(jnp.int32).reshape(1)
    place = (row_index % group).astype(jnp.int32).reshape(1)
    direct = all_rows // 16
    split = all_rows * 7 // 16
    wide = 256

    def device(h, q, c):
        return (h * group + q) * n_col + c

    spots = [(h, q, c) for h in range(2) for q in range(group) for c in range(2)]
    over_y = [(device(h, q, c), device(h, q, 1 - c)) for h, q, c in spots]
    over_z = [(device(h, q, c), device(1 - h, q, c)) for h, q, c in spots]
    ring = [
        (device(h, q, c), device(h, q, 1 - c) if h == c else device(1 - h, q, c))
        for h, q, c in spots
    ]
    in_chip = [(device(h, q, c), device(h, q ^ 1, c)) for h, q, c in spots]

    def move(values, pairs):
        return lax.ppermute(values, ("row", "col"), pairs)

    def chunks(spans, stacked, limit, after=()):
        inputs = (place, mask0_rows, mask1_rows, x0_rows, x1_rows)
        return masked_chunks(*inputs, spans, stacked, panel, limit, after)

    def partials(one, other, **more):
        return partial_products(diag, one, other, right0, right1, wide, **more)

    def own(one, other):
        return local_products(diag, one, other, right0, right1, wide)

    def parts(joint, a, b):
        top, low = piece(joint, 0, direct), piece(joint, direct)
        return (top, piece(a), low, piece(b))

    joint, a1, b1 = chunks(((0, direct), (direct, split)), True, ALL_VMEM_BYTES)
    passed1 = move(b1, over_y)
    near0 = move(joint, ring)
    a2, b2 = chunks(((split, all_rows),), False, VMEM_BYTES, (a1,))
    right0, right1 = masked_right(mask0_cols, mask1_cols, x0_cols, x1_cols, (a2,))
    middle = b2.shape[0] // 32 * 16
    send, top2, low2 = chosen(
        diag, (passed1,), a1, (piece(b2, 0, middle), piece(b2, middle)), (near0, right0)
    )
    near1 = move(send, over_z)
    passed2 = (move(top2, over_y), move(low2, over_y))
    far0 = move(near0, over_y)
    send, a1 = chosen(diag, passed2, a2, (piece(a1),), (far0, near1))
    near2 = move(send, over_z)
    got1 = move(a1, over_y)
    far1 = move(near1, over_y)
    (coded,) = partials(parts(near0, near1, far1), parts(far0, far1, near1))
    coded, near2 = handed_on((coded, near2), (got1,))
    back = move(coded, over_z)
    far2 = move(near2, over_y)
    sums = own(parts(joint, a1, b1), parts(near0, got1, passed1))
    coded, *rest, mark = partials(
        (piece(near2), piece(far2)),
        (piece(far2), piece(near2)),
        given=(piece(a2, 0, middle), piece(a2, middle), piece(near1, 0, all_rows // 4)),
        gates=sums[:1],
    )
    (mark,) = handed_on((mark,), (back,))
    mark = move(mark, in_chip)
    outs = finished(keep, *sums, back, (), 0, all_rows)
    back = move(coded, over_z)
    got2 = [move(part, over_y) for part in rest]
    sums = own((piece(a2), piece(b2)), (*map(piece, got2), *map(piece, passed2)))
    return tuple(finished(keep, *sums, back, outs, split, all_rows, after=(mark,)))


def passed_along(shard, axis, by):
    devices = lax.axis_size(axis)
    return lax.ppermute(shard, axis, [(i, (i + by) % devices) for i in range(devices)])


def masked(values, mask):
    rows_b, cols_b = mask.shape
    tiles = values.reshape(rows_b, BLOCK, cols_b, BLOCK)
    return (tiles * mask.astype(values.dtype)[:, None, :, None]).reshape(values.shape)


def per_device(
    x0_rows, x1_rows, x0_cols, x1_cols, mask0_rows, mask1_rows, mask0_cols, mask1_cols, keep_mask
):
    n_row = lax.axis_size("row")
    n_col = lax.axis_size("col")
    group = n_row // n_col
    row_index = lax.axis_index("row")
    col_index = lax.axis_index("col")
    panel = x0_cols.shape[0]
    start = row_index % group * panel
    block_start = row_index % group * (panel // BLOCK)
    left_zero = masked(
        lax.dynamic_slice_in_dim(x0_rows, start, panel, 1),
        lax.dynamic_slice_in_dim(mask0_rows, block_start, panel // BLOCK, 1),
    )
    left_one = masked(
        lax.dynamic_slice_in_dim(x1_rows, start, panel, 1),
        lax.dynamic_slice_in_dim(mask1_rows, block_start, panel // BLOCK, 1),
    )
    right_zero = masked(x0_cols, mask0_cols)
    right_one = masked(x1_cols, mask1_cols)
    left = jnp.stack([left_zero, left_one])
    right = jnp.stack([right_zero, right_one])
    left_offset = row_index // group % n_col
    right_offset = col_index % n_col
    levels = n_col.bit_length() - 1
    for level in range(levels):
        moved_left = passed_along(left, "col", -(1 << level))
        moved_right = passed_along(right, "row", -group * (1 << level))
        left = jnp.where(left_offset // (1 << level) % 2 == 1, moved_left, left)
        right = jnp.where(right_offset // (1 << level) % 2 == 1, moved_right, right)

    def accumulate(left_now, right_now, square, tangent):
        square = square + jnp.dot(left_now[0], right_now[0], preferred_element_type=jnp.float32)
        tangent = tangent + jnp.dot(left_now[0], right_now[1], preferred_element_type=jnp.float32)
        tangent = tangent + jnp.dot(left_now[1], right_now[0], preferred_element_type=jnp.float32)
        return (square, tangent)

    def section_body(section, carry):
        left_now, right_now, square, tangent = carry
        square, tangent = accumulate(left_now, right_now, square, tangent)
        left_now = passed_along(left_now, "col", -1)
        right_now = passed_along(right_now, "row", -group)
        return (left_now, right_now, square, tangent)

    zeros = jnp.zeros((left_zero.shape[0], right_zero.shape[1]), jnp.float32)
    left, right, square, tangent = lax.fori_loop(
        0, n_col - 1, section_body, (left, right, zeros, zeros)
    )
    square, tangent = accumulate(left, right, square, tangent)
    x_square = masked(square, keep_mask).astype(jnp.bfloat16)
    x_tangent = masked(tangent, keep_mask).astype(jnp.bfloat16)
    return (x_square, x_tangent)


def solution(mesh):
    if mesh.shape["col"] == 2:
        body = functools.partial(per_device_pair, mesh.shape["row"])
    else:
        body = per_device
    return jax.shard_map(
        body,
        mesh=mesh,
        in_specs=(P("row", "col"),) * 9,
        out_specs=(P("row", "col"), P("row", "col")),
        check_vma=False,
    )
```

```python
import functools
import math

import jax
import jax.numpy as jnp
from jax import lax
from jax.experimental import pallas as pl
from jax.experimental.pallas import tpu as pltpu
from jax.sharding import PartitionSpec as P

BLOCK = 128
LEVELS = 32000.0
STEPS = 32.0
LN2 = math.log(2.0)
VMEM_BYTES = 48 * 1024 * 1024
ALL_VMEM_BYTES = 62 * 1024 * 1024

VM = functools.partial(pl.BlockSpec, memory_space=pltpu.VMEM)
SM = functools.partial(pl.BlockSpec, memory_space=pltpu.SMEM)
HB = functools.partial(pl.BlockSpec, memory_space=pl.ANY)


def params(limit=VMEM_BYTES):
    return pltpu.CompilerParams(vmem_limit_bytes=limit)


def cost(flops, moved):
    return pl.CostEstimate(flops=int(flops) // 64, bytes_accessed=int(moved) // 64, transcendentals=0)


def scaled(values, entry):
    return (values.astype(jnp.float32) * entry.astype(jnp.float32)).astype(values.dtype)


def row_pieces(start, rows):
    edges = sorted({start, start + rows} | {e for e in range(0, start + rows, BLOCK) if e > start})
    return [(lo // BLOCK, slice(lo - start, hi - start)) for lo, hi in zip(edges, edges[1:])]


def chunk_kernel(spans, stacked, panel, *refs):
    place, mask0_far, mask1_far, x0, x1 = refs[:5]
    outs = refs[-5 - 2 * len(spans) + stacked : -5]
    held, mask0, mask1, mask_sems, sems = refs[-5:]
    start, rows = spans[0][0], held.shape[1]
    blocks = panel // BLOCK
    first = place[0] * blocks
    at = pl.ds(pl.multiple_of(place[0] * panel, BLOCK), panel)
    copies = [
        pltpu.make_async_copy(mask0_far, mask0, mask_sems.at[0]),
        pltpu.make_async_copy(mask1_far, mask1, mask_sems.at[1]),
        pltpu.make_async_copy(x0.at[pl.ds(start, rows), at], held.at[0], sems.at[0]),
        pltpu.make_async_copy(x1.at[pl.ds(start, rows), at], held.at[1], sems.at[1]),
    ]
    for copy in copies:
        copy.start()
    for copy in copies:
        copy.wait()
    for n, (lo, hi) in enumerate(spans):
        for which, mask in enumerate((mask0, mask1)):
            joint = stacked and n == 0
            out = outs[0] if joint else outs[2 * n - stacked + which]
            down = which * (hi - lo) if joint else 0
            for row_block, part in row_pieces(lo, hi - lo):
                source = slice(part.start + lo - start, part.stop + lo - start)
                target = slice(part.start + down, part.stop + down)
                for j in range(blocks):
                    cut = slice(j * BLOCK, (j + 1) * BLOCK)
                    values = scaled(held[which, source, cut], mask[row_block, first + j])
                    out[target, cut] = values


def masked_chunks(place, mask0, mask1, x0, x1, spans, stacked, panel, limit, after=()):
    rows = spans[-1][1] - spans[0][0]
    outs = []
    for n, (lo, hi) in enumerate(spans):
        if stacked and n == 0:
            outs.append(jax.ShapeDtypeStruct((2 * (hi - lo), panel), x0.dtype))
        else:
            outs += [jax.ShapeDtypeStruct((hi - lo, panel), x0.dtype)] * 2
    return pl.pallas_call(
        functools.partial(chunk_kernel, spans, int(stacked), panel),
        in_specs=[SM()] + [HB() for _ in range(4 + len(after))],
        out_specs=[VM() for _ in outs],
        out_shape=outs,
        scratch_shapes=[
            pltpu.VMEM((2, rows, panel), x0.dtype),
            pltpu.SMEM(mask0.shape, mask0.dtype),
            pltpu.SMEM(mask1.shape, mask1.dtype),
            pltpu.SemaphoreType.DMA((2,)),
            pltpu.SemaphoreType.DMA((2,)),
        ],
        compiler_params=params(limit),
        cost_estimate=cost(0, 8 * rows * panel),
        name="left_chunks",
    )(place, mask0, mask1, x0, x1, *after)


def choose_kernel(gates, many, cuts, diag, *refs):
    one, other = refs[gates : gates + many], refs[gates + many]
    held = refs[gates + many + 1 : gates + many + 1 + len(cuts)]
    outs, sems = refs[-len(cuts) - 2 : -1], refs[-1]
    send = outs[0]
    others = [
        pltpu.make_async_copy(x.at[pl.ds(lo, hi - lo)], out, sems.at[many + i])
        for i, (x, out, (lo, hi)) in enumerate(zip(held, outs[1:], cuts))
    ]
    for copy in others:
        copy.start()

    @pl.when(diag[0] == 1)
    def _():
        fetched([(i, 0, x.shape[0]) for i, x in enumerate(one)], one, send, sems)

    @pl.when(diag[0] == 0)
    def _():
        fetched([(0, 0, other.shape[0])], [other], send, sems)

    for copy in others:
        copy.wait()


def chosen(diag, one, other, held=(), after=()):
    outs = [jax.ShapeDtypeStruct(other.shape, other.dtype)]
    outs += [jax.ShapeDtypeStruct((hi - lo, x.shape[1]), x.dtype) for x, lo, hi in held]
    return pl.pallas_call(
        functools.partial(choose_kernel, len(after), len(one), [cut for _, *cut in held]),
        in_specs=[SM()] + [HB() for _ in (*after, *one, other, *held)],
        out_specs=[HB() for _ in outs],
        out_shape=outs,
        scratch_shapes=[pltpu.SemaphoreType.DMA((len(one) + len(held),))],
        compiler_params=params(),
        cost_estimate=cost(0, 4 * other.size),
        name="to_send",
    )(diag, *after, *one, other, *(x for x, _, _ in held))


def hand_kernel(many, *refs):
    sems = refs[-1]
    copies = [
        pltpu.make_async_copy(refs[i], refs[i - many - 1], sems.at[i]) for i in range(many)
    ]
    for copy in copies:
        copy.start()
    for copy in copies:
        copy.wait()


def handed_on(values, gates):
    outs = [jax.ShapeDtypeStruct(x.shape, x.dtype) for x in values]
    return pl.pallas_call(
        functools.partial(hand_kernel, len(values)),
        in_specs=[HB() for _ in (*values, *gates)],
        out_specs=[HB() for _ in outs],
        out_shape=outs,
        scratch_shapes=[pltpu.SemaphoreType.DMA((len(outs),))],
        compiler_params=params(),
        cost_estimate=cost(0, 4 * sum(x.size for x in values)),
        name="handed_on",
    )(*values, *gates)


def right_kernel(mask0, mask1, x0, x1, *rest):
    out0, out1 = rest[-2:]
    step = pl.program_id(0)
    many = x0.shape[0] // BLOCK
    for i in range(many):
        for j in range(x0.shape[1] // BLOCK):
            at = (slice(i * BLOCK, (i + 1) * BLOCK), slice(j * BLOCK, (j + 1) * BLOCK))
            out0[at] = scaled(x0[at], mask0[step * many + i, j])
            out1[at] = scaled(x1[at], mask1[step * many + i, j])


def masked_right(mask0, mask1, x0, x1, after=()):
    depth, columns = x0.shape
    tall = 2 * BLOCK
    out = jax.ShapeDtypeStruct(x0.shape, x0.dtype)
    tile = pl.BlockSpec((tall, columns), lambda g: (g, 0))
    return pl.pallas_call(
        right_kernel,
        grid=(depth // tall,),
        in_specs=[SM(), SM(), tile, tile] + [HB() for _ in after],
        out_specs=[tile, tile],
        out_shape=[out, out],
        compiler_params=params(),
        cost_estimate=cost(0, 8 * depth * columns),
        name="right_panels",
    )(mask0, mask1, x0, x1, *after)


def both_products(held, right0, right1):
    rows = held.shape[0] // 2
    first = jnp.dot(held[...], right0[...], preferred_element_type=jnp.float32)
    second = jnp.dot(held[:rows], right1[...], preferred_element_type=jnp.float32)
    return first[:rows], first[rows:] + second


def piece(array, lo=0, hi=None):
    return (array, lo, array.shape[0] if hi is None else hi)


def numbered(one, other):
    arrays = []
    for array, _, _ in (*one, *other):
        if all(array is not known for known in arrays):
            arrays.append(array)
    number = {id(array): i for i, array in enumerate(arrays)}
    return arrays, *(
        tuple((number[id(array)], lo, hi) for array, lo, hi in pieces) for pieces in (one, other)
    )


def fetched(pieces, refs, held, sems):
    copies = []
    top = 0
    for i, (which, lo, hi) in enumerate(pieces):
        source = refs[which].at[pl.ds(lo, hi - lo)]
        copies.append(pltpu.make_async_copy(source, held.at[pl.ds(top, hi - lo)], sems.at[i]))
        top += hi - lo
    for copy in copies:
        copy.start()
    for copy in copies:
        copy.wait()


def fetch_left(diag, one, other, refs, held, sems):
    first = pl.program_id(0) == 0

    @pl.when(first & (diag[0] == 1))
    def _():
        fetched(one, refs, held, sems)

    @pl.when(first & (diag[0] == 0))
    def _():
        fetched(other, refs, held, sems)


def local_kernel(one, other, diag, right0, right1, *refs):
    square, tangent, held, sems = refs[-4:]
    fetch_left(diag, one, other, refs, held, sems)
    square[...], tangent[...] = both_products(held, right0, right1)


def local_products(diag, one, other, right0, right1, wide):
    arrays, one, other = numbered(one, other)
    rows = sum(hi - lo for _, lo, hi in one) // 2
    depth, columns = right0.shape
    out = jax.ShapeDtypeStruct((rows, columns), jnp.float32)
    tile = pl.BlockSpec((rows, wide), lambda g: (0, g))
    return pl.pallas_call(
        functools.partial(local_kernel, one, other),
        grid=(columns // wide,),
        in_specs=[
            SM(),
            pl.BlockSpec((depth, wide), lambda g: (0, g)),
            pl.BlockSpec((depth, wide), lambda g: (0, g)),
        ]
        + [HB() for _ in arrays],
        out_specs=[tile, tile],
        out_shape=[out, out],
        scratch_shapes=[
            pltpu.VMEM((2 * rows, depth), right0.dtype),
            pltpu.SemaphoreType.DMA((max(len(one), len(other)),)),
        ],
        compiler_params=params(),
        cost_estimate=cost(6 * rows * depth * columns, 8 * rows * depth + 4 * depth * columns),
        name="own_products",
    )(diag, right0, right1, *arrays)


def partial_kernel(one, other, many, cuts, diag, right0, right1, *refs):
    given = len(cuts)
    out, passed = refs[-5 - given], refs[-4 - given : -4]
    held, steps, sems, hand_sems = refs[-4:]
    others = [
        pltpu.make_async_copy(x.at[pl.ds(lo, hi - lo)], y, hand_sems.at[i])
        for i, (x, y, (lo, hi)) in enumerate(zip(refs[many : many + given], passed, cuts))
    ]

    @pl.when(pl.program_id(0) == 0)
    def _():
        for copy in others:
            copy.start()

    rows, wide = held.shape[0] // 2, right0.shape[1]
    step = pl.program_id(0)
    tiles = wide // BLOCK
    across = pl.num_programs(0) * tiles
    fetch_left(diag, one, other, refs, held, sems)
    for which, values in enumerate(both_products(held, right0, right1)):
        top = jnp.maximum(jnp.max(jnp.abs(values), axis=0, keepdims=True), 1e-30)
        level = jnp.ceil(jnp.log(top) * (STEPS / LN2)) + 1.0
        coded = jnp.round(values * (LEVELS * jnp.exp(level * (-LN2 / STEPS))))
        coded = jnp.clip(coded, -32767.0, 32767.0).astype(jnp.int32).astype(jnp.int16)
        for t in range(tiles):
            at = which * across + step * tiles + t
            cut = slice(t * BLOCK, (t + 1) * BLOCK)
            out[pl.ds(pl.multiple_of(at * rows, rows), rows), :] = coded[:, cut]
            steps[pl.ds(at, 1), :] = level[:, cut]

    @pl.when(step == pl.num_programs(0) - 1)
    def _():
        tail = steps.shape[0]
        out[out.shape[0] - tail :, :] = steps[...].astype(jnp.int32).astype(jnp.int16)
        for copy in others:
            copy.wait()


def partial_products(diag, one, other, right0, right1, wide, given=(), gates=()):
    arrays, one, other = numbered(one, other)
    rows = sum(hi - lo for _, lo, hi in one) // 2
    depth, columns = right0.shape
    tiles = 2 * columns // BLOCK
    tail = -(-tiles // 16) * 16
    return pl.pallas_call(
        functools.partial(partial_kernel, one, other, len(arrays), [cut for _, *cut in given]),
        grid=(columns // wide,),
        in_specs=[
            SM(),
            pl.BlockSpec((depth, wide), lambda g: (0, g)),
            pl.BlockSpec((depth, wide), lambda g: (0, g)),
        ]
        + [HB() for _ in (*arrays, *given, *gates)],
        out_specs=[pl.BlockSpec((tiles * rows + tail, BLOCK), lambda g: (0, 0))]
        + [HB() for _ in given],
        out_shape=[jax.ShapeDtypeStruct((tiles * rows + tail, BLOCK), jnp.int16)]
        + [jax.ShapeDtypeStruct((hi - lo, x.shape[1]), x.dtype) for x, lo, hi in given],
        scratch_shapes=[
            pltpu.VMEM((2 * rows, depth), right0.dtype),
            pltpu.VMEM((tail, BLOCK), jnp.float32),
            pltpu.SemaphoreType.DMA((max(len(one), len(other)),)),
            pltpu.SemaphoreType.DMA((max(len(given), 1),)),
        ],
        compiler_params=params(),
        cost_estimate=cost(6 * rows * depth * columns, 4 * rows * depth + 4 * depth * columns),
        name="partial_products",
    )(diag, right0, right1, *arrays, *(x for x, _, _ in given), *gates)


def finish_kernel(start, cuts, keep, coded, square, tangent, *rest):
    many = len(cuts)
    given, outs, passed = rest[:many], rest[-5 - many : -3 - many], rest[-3 - many : -3]
    made, out_sems, sems = rest[-3:]
    rows, columns = square.shape
    across = columns // BLOCK
    others = [
        pltpu.make_async_copy(x.at[pl.ds(lo, hi - lo)], y, sems.at[i])
        for i, (x, y, (lo, hi)) in enumerate(zip(given, passed, cuts))
    ]
    results = [
        pltpu.make_async_copy(made.at[i], x.at[pl.ds(start, rows)], out_sems.at[i])
        for i, x in enumerate(outs)
    ]
    for copy in others:
        copy.start()
    tail = coded.shape[0] - 2 * across * rows
    levels = coded[coded.shape[0] - tail :, :].astype(jnp.int32).astype(jnp.float32)
    steps = jnp.exp(levels * (LN2 / STEPS)) * (1.0 / LEVELS)
    for which, mine in enumerate((square, tangent)):
        for j in range(across):
            tile = which * across + j
            cut = slice(j * BLOCK, (j + 1) * BLOCK)
            other = coded[tile * rows : (tile + 1) * rows, :].astype(jnp.int32).astype(jnp.float32)
            total = mine[:, cut] + other * steps[tile : tile + 1, :]
            for row_block, part in row_pieces(start, rows):
                kept = total[part] * keep[row_block, j].astype(jnp.float32)
                made[which, part, cut] = kept.astype(made.dtype)
        results[which].start()
    for copy in results + others:
        copy.wait()


def finished(keep, square, tangent, coded, before, start, all_rows, held=(), after=()):
    rows, columns = square.shape
    out = jax.ShapeDtypeStruct((all_rows, columns), jnp.bfloat16)
    held, before = list(held), list(before)
    passed = [jax.ShapeDtypeStruct((hi - lo, x.shape[1]), x.dtype) for x, lo, hi in held]
    many = len(held)
    return pl.pallas_call(
        functools.partial(finish_kernel, start, [cut for _, *cut in held]),
        in_specs=[SM(), VM(), VM(), VM()] + [HB() for _ in (*held, *before, *after)],
        out_specs=[HB() for _ in range(2 + many)],
        out_shape=[out, out] + passed,
        input_output_aliases={4 + many: 0, 5 + many: 1} if before else {},
        scratch_shapes=[
            pltpu.VMEM((2, rows, columns), jnp.bfloat16),
            pltpu.SemaphoreType.DMA((2,)),
            pltpu.SemaphoreType.DMA((max(many, 1),)),
        ],
        compiler_params=params(),
        cost_estimate=cost(0, 16 * rows * columns),
        name="finish",
    )(keep, coded, square, tangent, *(x for x, _, _ in held), *before, *after)


def per_device_pair(
    n_row, x0_rows, x1_rows, x0_cols, x1_cols, mask0_rows, mask1_rows, mask0_cols, mask1_cols, keep
):
    n_col = 2
    group = n_row // n_col
    panel = x0_cols.shape[0]
    all_rows = x0_rows.shape[0]
    row_index = lax.axis_index("row")
    half = row_index // group
    diag = (half == lax.axis_index("col")).astype(jnp.int32).reshape(1)
    place = (row_index % group).astype(jnp.int32).reshape(1)
    direct = all_rows // 16
    split = all_rows // 2
    wide = 256

    def device(h, q, c):
        return (h * group + q) * n_col + c

    spots = [(h, q, c) for h in range(2) for q in range(group) for c in range(2)]
    over_y = [(device(h, q, c), device(h, q, 1 - c)) for h, q, c in spots]
    over_z = [(device(h, q, c), device(1 - h, q, c)) for h, q, c in spots]
    ring = [
        (device(h, q, c), device(h, q, 1 - c) if h == c else device(1 - h, q, c))
        for h, q, c in spots
    ]
    in_chip = [(device(h, q, c), device(h, q ^ 1, c)) for h, q, c in spots]

    def move(values, pairs):
        return lax.ppermute(values, ("row", "col"), pairs)

    def chunks(spans, stacked, limit, after=()):
        inputs = (place, mask0_rows, mask1_rows, x0_rows, x1_rows)
        return masked_chunks(*inputs, spans, stacked, panel, limit, after)

    def partials(one, other, **more):
        return partial_products(diag, one, other, right0, right1, wide, **more)

    def own(one, other):
        return local_products(diag, one, other, right0, right1, wide)

    def parts(joint, a, b):
        top, low = piece(joint, 0, direct), piece(joint, direct)
        return (top, piece(a), low, piece(b))

    joint, a1, b1 = chunks(((0, direct), (direct, split)), True, ALL_VMEM_BYTES)
    passed1 = move(b1, over_y)
    near0 = move(joint, ring)
    a2, b2 = chunks(((split, all_rows),), False, VMEM_BYTES, (a1,))
    right0, right1 = masked_right(mask0_cols, mask1_cols, x0_cols, x1_cols, (a2,))
    middle = b2.shape[0] // 32 * 16
    send, top2, low2 = chosen(
        diag, (passed1,), a1, (piece(b2, 0, middle), piece(b2, middle)), (near0, right0)
    )
    near1 = move(send, over_z)
    passed2 = (move(top2, over_y), move(low2, over_y))
    far0 = move(near0, over_y)
    send, a1 = chosen(diag, passed2, a2, (piece(a1),), (far0, near1))
    near2 = move(send, over_z)
    got1 = move(a1, over_y)
    far1 = move(near1, over_y)
    (coded,) = partials(parts(near0, near1, far1), parts(far0, far1, near1))
    coded, near2 = handed_on((coded, near2), (got1,))
    back = move(coded, over_z)
    far2 = move(near2, over_y)
    sums = own(parts(joint, a1, b1), parts(near0, got1, passed1))
    coded, *rest, mark = partials(
        (piece(near2), piece(far2)),
        (piece(far2), piece(near2)),
        given=(piece(a2, 0, middle), piece(a2, middle), piece(near1, 0, all_rows // 4)),
        gates=sums[:1],
    )
    (mark,) = handed_on((mark,), (back,))
    mark = move(mark, in_chip)
    outs = finished(keep, *sums, back, (), 0, all_rows)
    back = move(coded, over_z)
    got2 = [move(part, over_y) for part in rest]
    sums = own((piece(a2), piece(b2)), (*map(piece, got2), *map(piece, passed2)))
    return tuple(finished(keep, *sums, back, outs, split, all_rows, after=(mark,)))


def passed_along(shard, axis, by):
    devices = lax.axis_size(axis)
    return lax.ppermute(shard, axis, [(i, (i + by) % devices) for i in range(devices)])


def masked(values, mask):
    rows_b, cols_b = mask.shape
    tiles = values.reshape(rows_b, BLOCK, cols_b, BLOCK)
    return (tiles * mask.astype(values.dtype)[:, None, :, None]).reshape(values.shape)


def per_device(
    x0_rows, x1_rows, x0_cols, x1_cols, mask0_rows, mask1_rows, mask0_cols, mask1_cols, keep_mask
):
    n_row = lax.axis_size("row")
    n_col = lax.axis_size("col")
    group = n_row // n_col
    row_index = lax.axis_index("row")
    col_index = lax.axis_index("col")
    panel = x0_cols.shape[0]
    start = row_index % group * panel
    block_start = row_index % group * (panel // BLOCK)
    left_zero = masked(
        lax.dynamic_slice_in_dim(x0_rows, start, panel, 1),
        lax.dynamic_slice_in_dim(mask0_rows, block_start, panel // BLOCK, 1),
    )
    left_one = masked(
        lax.dynamic_slice_in_dim(x1_rows, start, panel, 1),
        lax.dynamic_slice_in_dim(mask1_rows, block_start, panel // BLOCK, 1),
    )
    right_zero = masked(x0_cols, mask0_cols)
    right_one = masked(x1_cols, mask1_cols)
    left = jnp.stack([left_zero, left_one])
    right = jnp.stack([right_zero, right_one])
    left_offset = row_index // group % n_col
    right_offset = col_index % n_col
    levels = n_col.bit_length() - 1
    for level in range(levels):
        moved_left = passed_along(left, "col", -(1 << level))
        moved_right = passed_along(right, "row", -group * (1 << level))
        left = jnp.where(left_offset // (1 << level) % 2 == 1, moved_left, left)
        right = jnp.where(right_offset // (1 << level) % 2 == 1, moved_right, right)

    def accumulate(left_now, right_now, square, tangent):
        square = square + jnp.dot(left_now[0], right_now[0], preferred_element_type=jnp.float32)
        tangent = tangent + jnp.dot(left_now[0], right_now[1], preferred_element_type=jnp.float32)
        tangent = tangent + jnp.dot(left_now[1], right_now[0], preferred_element_type=jnp.float32)
        return (square, tangent)

    def section_body(section, carry):
        left_now, right_now, square, tangent = carry
        square, tangent = accumulate(left_now, right_now, square, tangent)
        left_now = passed_along(left_now, "col", -1)
        right_now = passed_along(right_now, "row", -group)
        return (left_now, right_now, square, tangent)

    zeros = jnp.zeros((left_zero.shape[0], right_zero.shape[1]), jnp.float32)
    left, right, square, tangent = lax.fori_loop(
        0, n_col - 1, section_body, (left, right, zeros, zeros)
    )
    square, tangent = accumulate(left, right, square, tangent)
    x_square = masked(square, keep_mask).astype(jnp.bfloat16)
    x_tangent = masked(tangent, keep_mask).astype(jnp.bfloat16)
    return (x_square, x_tangent)


def solution(mesh):
    if mesh.shape["col"] == 2:
        body = functools.partial(per_device_pair, mesh.shape["row"])
    else:
        body = per_device
    return jax.shard_map(
        body,
        mesh=mesh,
        in_specs=(P("row", "col"),) * 9,
        out_specs=(P("row", "col"), P("row", "col")),
        check_vma=False,
    )
```

```python
import functools
import math

import jax
import jax.numpy as jnp
from jax import lax
from jax.experimental import pallas as pl
from jax.experimental.pallas import tpu as pltpu
from jax.sharding import PartitionSpec as P

BLOCK = 128
LEVELS = 32000.0
STEPS = 32.0
LN2 = math.log(2.0)
VMEM_BYTES = 48 * 1024 * 1024
ALL_VMEM_BYTES = 62 * 1024 * 1024

VM = functools.partial(pl.BlockSpec, memory_space=pltpu.VMEM)
SM = functools.partial(pl.BlockSpec, memory_space=pltpu.SMEM)
HB = functools.partial(pl.BlockSpec, memory_space=pl.ANY)


def params(limit=VMEM_BYTES):
    return pltpu.CompilerParams(vmem_limit_bytes=limit)


def cost(flops, moved):
    return pl.CostEstimate(flops=int(flops) // 64, bytes_accessed=int(moved) // 64, transcendentals=0)


def scaled(values, entry):
    return (values.astype(jnp.float32) * entry.astype(jnp.float32)).astype(values.dtype)


def row_pieces(start, rows):
    edges = sorted({start, start + rows} | {e for e in range(0, start + rows, BLOCK) if e > start})
    return [(lo // BLOCK, slice(lo - start, hi - start)) for lo, hi in zip(edges, edges[1:])]


def chunk_kernel(spans, stacked, panel, *refs):
    place, mask0_far, mask1_far, x0, x1 = refs[:5]
    outs = refs[-5 - 2 * len(spans) + stacked : -5]
    held, mask0, mask1, mask_sems, sems = refs[-5:]
    start, rows = spans[0][0], held.shape[1]
    blocks = panel // BLOCK
    first = place[0] * blocks
    at = pl.ds(pl.multiple_of(place[0] * panel, BLOCK), panel)
    copies = [
        pltpu.make_async_copy(mask0_far, mask0, mask_sems.at[0]),
        pltpu.make_async_copy(mask1_far, mask1, mask_sems.at[1]),
        pltpu.make_async_copy(x0.at[pl.ds(start, rows), at], held.at[0], sems.at[0]),
        pltpu.make_async_copy(x1.at[pl.ds(start, rows), at], held.at[1], sems.at[1]),
    ]
    for copy in copies:
        copy.start()
    for copy in copies:
        copy.wait()
    for n, (lo, hi) in enumerate(spans):
        for which, mask in enumerate((mask0, mask1)):
            joint = stacked and n == 0
            out = outs[0] if joint else outs[2 * n - stacked + which]
            down = which * (hi - lo) if joint else 0
            for row_block, part in row_pieces(lo, hi - lo):
                source = slice(part.start + lo - start, part.stop + lo - start)
                target = slice(part.start + down, part.stop + down)
                for j in range(blocks):
                    cut = slice(j * BLOCK, (j + 1) * BLOCK)
                    values = scaled(held[which, source, cut], mask[row_block, first + j])
                    out[target, cut] = values


def masked_chunks(place, mask0, mask1, x0, x1, spans, stacked, panel, limit, after=()):
    rows = spans[-1][1] - spans[0][0]
    outs = []
    for n, (lo, hi) in enumerate(spans):
        if stacked and n == 0:
            outs.append(jax.ShapeDtypeStruct((2 * (hi - lo), panel), x0.dtype))
        else:
            outs += [jax.ShapeDtypeStruct((hi - lo, panel), x0.dtype)] * 2
    return pl.pallas_call(
        functools.partial(chunk_kernel, spans, int(stacked), panel),
        in_specs=[SM()] + [HB() for _ in range(4 + len(after))],
        out_specs=[VM() for _ in outs],
        out_shape=outs,
        scratch_shapes=[
            pltpu.VMEM((2, rows, panel), x0.dtype),
            pltpu.SMEM(mask0.shape, mask0.dtype),
            pltpu.SMEM(mask1.shape, mask1.dtype),
            pltpu.SemaphoreType.DMA((2,)),
            pltpu.SemaphoreType.DMA((2,)),
        ],
        compiler_params=params(limit),
        cost_estimate=cost(0, 8 * rows * panel),
        name="left_chunks",
    )(place, mask0, mask1, x0, x1, *after)


def choose_kernel(gates, many, diag, *refs):
    one, other = refs[gates : gates + 2]
    held, outs, sems = refs[gates + 2 : gates + 2 + many], refs[-many - 2 : -1], refs[-1]
    others = [
        pltpu.make_async_copy(x, out, sems.at[1 + i])
        for i, (x, out) in enumerate(zip(held, outs[1:]))
    ]
    for copy in others:
        copy.start()

    @pl.when(diag[0] == 1)
    def _():
        copy = pltpu.make_async_copy(one, outs[0], sems.at[0])
        copy.start()
        copy.wait()

    @pl.when(diag[0] == 0)
    def _():
        copy = pltpu.make_async_copy(other, outs[0], sems.at[0])
        copy.start()
        copy.wait()

    for copy in others:
        copy.wait()


def chosen(diag, one, other, held=(), after=()):
    outs = [jax.ShapeDtypeStruct(x.shape, x.dtype) for x in (one, *held)]
    return pl.pallas_call(
        functools.partial(choose_kernel, len(after), len(held)),
        in_specs=[SM()] + [HB() for _ in (*after, one, other, *held)],
        out_specs=[HB() for _ in outs],
        out_shape=outs,
        scratch_shapes=[pltpu.SemaphoreType.DMA((len(outs),))],
        compiler_params=params(),
        cost_estimate=cost(0, 4 * one.size),
        name="to_send",
    )(diag, *after, one, other, *held)


def hand_kernel(many, *refs):
    sems = refs[-1]
    copies = [
        pltpu.make_async_copy(refs[i], refs[i - many - 1], sems.at[i]) for i in range(many)
    ]
    for copy in copies:
        copy.start()
    for copy in copies:
        copy.wait()


def handed_on(values, gates):
    outs = [jax.ShapeDtypeStruct(x.shape, x.dtype) for x in values]
    return pl.pallas_call(
        functools.partial(hand_kernel, len(values)),
        in_specs=[HB() for _ in (*values, *gates)],
        out_specs=[HB() for _ in outs],
        out_shape=outs,
        scratch_shapes=[pltpu.SemaphoreType.DMA((len(outs),))],
        compiler_params=params(),
        cost_estimate=cost(0, 4 * sum(x.size for x in values)),
        name="handed_on",
    )(*values, *gates)


def right_kernel(mask0, mask1, x0, x1, *rest):
    out0, out1 = rest[-2:]
    step = pl.program_id(0)
    many = x0.shape[0] // BLOCK
    for i in range(many):
        for j in range(x0.shape[1] // BLOCK):
            at = (slice(i * BLOCK, (i + 1) * BLOCK), slice(j * BLOCK, (j + 1) * BLOCK))
            out0[at] = scaled(x0[at], mask0[step * many + i, j])
            out1[at] = scaled(x1[at], mask1[step * many + i, j])


def masked_right(mask0, mask1, x0, x1, after=()):
    depth, columns = x0.shape
    tall = 2 * BLOCK
    out = jax.ShapeDtypeStruct(x0.shape, x0.dtype)
    tile = pl.BlockSpec((tall, columns), lambda g: (g, 0))
    return pl.pallas_call(
        right_kernel,
        grid=(depth // tall,),
        in_specs=[SM(), SM(), tile, tile] + [HB() for _ in after],
        out_specs=[tile, tile],
        out_shape=[out, out],
        compiler_params=params(),
        cost_estimate=cost(0, 8 * depth * columns),
        name="right_panels",
    )(mask0, mask1, x0, x1, *after)


def both_products(held, right0, right1):
    rows = held.shape[0] // 2
    first = jnp.dot(held[...], right0[...], preferred_element_type=jnp.float32)
    second = jnp.dot(held[:rows], right1[...], preferred_element_type=jnp.float32)
    return first[:rows], first[rows:] + second


def piece(array, lo=0, hi=None):
    return (array, lo, array.shape[0] if hi is None else hi)


def numbered(one, other):
    arrays = []
    for array, _, _ in (*one, *other):
        if all(array is not known for known in arrays):
            arrays.append(array)
    number = {id(array): i for i, array in enumerate(arrays)}
    return arrays, *(
        tuple((number[id(array)], lo, hi) for array, lo, hi in pieces) for pieces in (one, other)
    )


def fetched(pieces, refs, held, sems):
    copies = []
    top = 0
    for i, (which, lo, hi) in enumerate(pieces):
        source = refs[which].at[pl.ds(lo, hi - lo)]
        copies.append(pltpu.make_async_copy(source, held.at[pl.ds(top, hi - lo)], sems.at[i]))
        top += hi - lo
    for copy in copies:
        copy.start()
    for copy in copies:
        copy.wait()


def fetch_left(diag, one, other, refs, held, sems):
    first = pl.program_id(0) == 0

    @pl.when(first & (diag[0] == 1))
    def _():
        fetched(one, refs, held, sems)

    @pl.when(first & (diag[0] == 0))
    def _():
        fetched(other, refs, held, sems)


def local_kernel(one, other, diag, right0, right1, *refs):
    square, tangent, held, sems = refs[-4:]
    fetch_left(diag, one, other, refs, held, sems)
    square[...], tangent[...] = both_products(held, right0, right1)


def local_products(diag, one, other, right0, right1, wide):
    arrays, one, other = numbered(one, other)
    rows = sum(hi - lo for _, lo, hi in one) // 2
    depth, columns = right0.shape
    out = jax.ShapeDtypeStruct((rows, columns), jnp.float32)
    tile = pl.BlockSpec((rows, wide), lambda g: (0, g))
    return pl.pallas_call(
        functools.partial(local_kernel, one, other),
        grid=(columns // wide,),
        in_specs=[
            SM(),
            pl.BlockSpec((depth, wide), lambda g: (0, g)),
            pl.BlockSpec((depth, wide), lambda g: (0, g)),
        ]
        + [HB() for _ in arrays],
        out_specs=[tile, tile],
        out_shape=[out, out],
        scratch_shapes=[
            pltpu.VMEM((2 * rows, depth), right0.dtype),
            pltpu.SemaphoreType.DMA((len(one),)),
        ],
        compiler_params=params(),
        cost_estimate=cost(6 * rows * depth * columns, 8 * rows * depth + 4 * depth * columns),
        name="own_products",
    )(diag, right0, right1, *arrays)


def partial_kernel(one, other, many, given, diag, right0, right1, *refs):
    out, passed = refs[-5 - given], refs[-4 - given : -4]
    held, steps, sems, hand_sems = refs[-4:]
    others = [
        pltpu.make_async_copy(x, y, hand_sems.at[i])
        for i, (x, y) in enumerate(zip(refs[many : many + given], passed))
    ]

    @pl.when(pl.program_id(0) == 0)
    def _():
        for copy in others:
            copy.start()

    rows, wide = held.shape[0] // 2, right0.shape[1]
    step = pl.program_id(0)
    tiles = wide // BLOCK
    across = pl.num_programs(0) * tiles
    fetch_left(diag, one, other, refs, held, sems)
    for which, values in enumerate(both_products(held, right0, right1)):
        top = jnp.maximum(jnp.max(jnp.abs(values), axis=0, keepdims=True), 1e-30)
        level = jnp.ceil(jnp.log(top) * (STEPS / LN2)) + 1.0
        coded = jnp.round(values * (LEVELS * jnp.exp(level * (-LN2 / STEPS))))
        coded = jnp.clip(coded, -32767.0, 32767.0).astype(jnp.int32).astype(jnp.int16)
        for t in range(tiles):
            at = which * across + step * tiles + t
            cut = slice(t * BLOCK, (t + 1) * BLOCK)
            out[pl.ds(pl.multiple_of(at * rows, rows), rows), :] = coded[:, cut]
            steps[pl.ds(at, 1), :] = level[:, cut]

    @pl.when(step == pl.num_programs(0) - 1)
    def _():
        tail = steps.shape[0]
        out[out.shape[0] - tail :, :] = steps[...].astype(jnp.int32).astype(jnp.int16)
        for copy in others:
            copy.wait()


def partial_products(diag, one, other, right0, right1, wide, given=(), gates=()):
    arrays, one, other = numbered(one, other)
    rows = sum(hi - lo for _, lo, hi in one) // 2
    depth, columns = right0.shape
    tiles = 2 * columns // BLOCK
    tail = -(-tiles // 16) * 16
    return pl.pallas_call(
        functools.partial(partial_kernel, one, other, len(arrays), len(given)),
        grid=(columns // wide,),
        in_specs=[
            SM(),
            pl.BlockSpec((depth, wide), lambda g: (0, g)),
            pl.BlockSpec((depth, wide), lambda g: (0, g)),
        ]
        + [HB() for _ in (*arrays, *given, *gates)],
        out_specs=[pl.BlockSpec((tiles * rows + tail, BLOCK), lambda g: (0, 0))]
        + [HB() for _ in given],
        out_shape=[jax.ShapeDtypeStruct((tiles * rows + tail, BLOCK), jnp.int16)]
        + [jax.ShapeDtypeStruct(x.shape, x.dtype) for x in given],
        scratch_shapes=[
            pltpu.VMEM((2 * rows, depth), right0.dtype),
            pltpu.VMEM((tail, BLOCK), jnp.float32),
            pltpu.SemaphoreType.DMA((len(one),)),
            pltpu.SemaphoreType.DMA((max(len(given), 1),)),
        ],
        compiler_params=params(),
        cost_estimate=cost(6 * rows * depth * columns, 4 * rows * depth + 4 * depth * columns),
        name="partial_products",
    )(diag, right0, right1, *arrays, *given, *gates)


def finish_kernel(start, many, keep, coded, square, tangent, *rest):
    given, outs, passed = rest[:many], rest[-5 - many : -3 - many], rest[-3 - many : -3]
    made, out_sems, sems = rest[-3:]
    rows, columns = square.shape
    across = columns // BLOCK
    others = [
        pltpu.make_async_copy(x, y, sems.at[i]) for i, (x, y) in enumerate(zip(given, passed))
    ]
    results = [
        pltpu.make_async_copy(made.at[i], x.at[pl.ds(start, rows)], out_sems.at[i])
        for i, x in enumerate(outs)
    ]
    for copy in others:
        copy.start()
    tail = coded.shape[0] - 2 * across * rows
    levels = coded[coded.shape[0] - tail :, :].astype(jnp.int32).astype(jnp.float32)
    steps = jnp.exp(levels * (LN2 / STEPS)) * (1.0 / LEVELS)
    for which, mine in enumerate((square, tangent)):
        for j in range(across):
            tile = which * across + j
            cut = slice(j * BLOCK, (j + 1) * BLOCK)
            other = coded[tile * rows : (tile + 1) * rows, :].astype(jnp.int32).astype(jnp.float32)
            total = mine[:, cut] + other * steps[tile : tile + 1, :]
            for row_block, part in row_pieces(start, rows):
                kept = total[part] * keep[row_block, j].astype(jnp.float32)
                made[which, part, cut] = kept.astype(made.dtype)
        results[which].start()
    for copy in results + others:
        copy.wait()


def finished(keep, square, tangent, coded, before, start, all_rows, held=(), after=()):
    rows, columns = square.shape
    out = jax.ShapeDtypeStruct((all_rows, columns), jnp.bfloat16)
    held, before = list(held), list(before)
    passed = [jax.ShapeDtypeStruct(x.shape, x.dtype) for x in held]
    many = len(held)
    return pl.pallas_call(
        functools.partial(finish_kernel, start, many),
        in_specs=[SM(), VM(), VM(), VM()] + [HB() for _ in (*held, *before, *after)],
        out_specs=[HB() for _ in range(2 + many)],
        out_shape=[out, out] + passed,
        input_output_aliases={4 + many: 0, 5 + many: 1} if before else {},
        scratch_shapes=[
            pltpu.VMEM((2, rows, columns), jnp.bfloat16),
            pltpu.SemaphoreType.DMA((2,)),
            pltpu.SemaphoreType.DMA((max(many, 1),)),
        ],
        compiler_params=params(),
        cost_estimate=cost(0, 16 * rows * columns),
        name="finish",
    )(keep, coded, square, tangent, *held, *before, *after)


def per_device_pair(
    n_row, x0_rows, x1_rows, x0_cols, x1_cols, mask0_rows, mask1_rows, mask0_cols, mask1_cols, keep
):
    n_col = 2
    group = n_row // n_col
    panel = x0_cols.shape[0]
    all_rows = x0_rows.shape[0]
    row_index = lax.axis_index("row")
    half = row_index // group
    diag = (half == lax.axis_index("col")).astype(jnp.int32).reshape(1)
    place = (row_index % group).astype(jnp.int32).reshape(1)
    direct = all_rows // 8
    split = all_rows // 2
    wide = 256

    def device(h, q, c):
        return (h * group + q) * n_col + c

    spots = [(h, q, c) for h in range(2) for q in range(group) for c in range(2)]
    over_y = [(device(h, q, c), device(h, q, 1 - c)) for h, q, c in spots]
    over_z = [(device(h, q, c), device(1 - h, q, c)) for h, q, c in spots]
    ring = [
        (device(h, q, c), device(h, q, 1 - c) if h == c else device(1 - h, q, c))
        for h, q, c in spots
    ]
    def move(values, pairs):
        return lax.ppermute(values, ("row", "col"), pairs)

    def chunks(spans, stacked, limit, after=()):
        inputs = (place, mask0_rows, mask1_rows, x0_rows, x1_rows)
        return masked_chunks(*inputs, spans, stacked, panel, limit, after)

    def partials(one, other, **more):
        return partial_products(diag, one, other, right0, right1, wide, **more)

    def own(one, other):
        return local_products(diag, one, other, right0, right1, wide)

    def parts(joint, a, b):
        top, low = piece(joint, 0, direct), piece(joint, direct)
        return (top, piece(a), low, piece(b))

    joint, a1, b1 = chunks(((0, direct), (direct, split)), True, ALL_VMEM_BYTES)
    passed1 = move(b1, over_y)
    near0 = move(joint, ring)
    a2, b2 = chunks(((split, all_rows),), False, VMEM_BYTES, (a1,))
    right0, right1 = masked_right(mask0_cols, mask1_cols, x0_cols, x1_cols, (a2,))
    send, b2 = chosen(diag, passed1, a1, (b2,), (near0, right0))
    near1 = move(send, over_z)
    passed2 = move(b2, over_y)
    far0 = move(near0, over_y)
    send, a1 = chosen(diag, passed2, a2, (a1,), (far0, near1))
    near2 = move(send, over_z)
    got1 = move(a1, over_y)
    far1 = move(near1, over_y)
    (coded,) = partials(parts(near0, near1, far1), parts(far0, far1, near1))
    coded, near2 = handed_on((coded, near2), (got1,))
    back = move(coded, over_z)
    far2 = move(near2, over_y)
    sums = own(parts(joint, a1, b1), parts(near0, got1, passed1))
    coded, a2 = partials(
        (piece(near2), piece(far2)), (piece(far2), piece(near2)), given=(a2,), gates=sums[:1]
    )
    (coded,) = handed_on((coded,), (back,))
    outs = finished(keep, *sums, back, (), 0, all_rows)
    back = move(coded, over_z)
    got2 = move(a2, over_y)
    sums = own((piece(a2), piece(b2)), (piece(got2), piece(passed2)))
    return tuple(finished(keep, *sums, back, outs, split, all_rows))


def passed_along(shard, axis, by):
    devices = lax.axis_size(axis)
    return lax.ppermute(shard, axis, [(i, (i + by) % devices) for i in range(devices)])


def masked(values, mask):
    rows_b, cols_b = mask.shape
    tiles = values.reshape(rows_b, BLOCK, cols_b, BLOCK)
    return (tiles * mask.astype(values.dtype)[:, None, :, None]).reshape(values.shape)


def per_device(
    x0_rows, x1_rows, x0_cols, x1_cols, mask0_rows, mask1_rows, mask0_cols, mask1_cols, keep_mask
):
    n_row = lax.axis_size("row")
    n_col = lax.axis_size("col")
    group = n_row // n_col
    row_index = lax.axis_index("row")
    col_index = lax.axis_index("col")
    panel = x0_cols.shape[0]
    start = row_index % group * panel
    block_start = row_index % group * (panel // BLOCK)
    left_zero = masked(
        lax.dynamic_slice_in_dim(x0_rows, start, panel, 1),
        lax.dynamic_slice_in_dim(mask0_rows, block_start, panel // BLOCK, 1),
    )
    left_one = masked(
        lax.dynamic_slice_in_dim(x1_rows, start, panel, 1),
        lax.dynamic_slice_in_dim(mask1_rows, block_start, panel // BLOCK, 1),
    )
    right_zero = masked(x0_cols, mask0_cols)
    right_one = masked(x1_cols, mask1_cols)
    left = jnp.stack([left_zero, left_one])
    right = jnp.stack([right_zero, right_one])
    left_offset = row_index // group % n_col
    right_offset = col_index % n_col
    levels = n_col.bit_length() - 1
    for level in range(levels):
        moved_left = passed_along(left, "col", -(1 << level))
        moved_right = passed_along(right, "row", -group * (1 << level))
        left = jnp.where(left_offset // (1 << level) % 2 == 1, moved_left, left)
        right = jnp.where(right_offset // (1 << level) % 2 == 1, moved_right, right)

    def accumulate(left_now, right_now, square, tangent):
        square = square + jnp.dot(left_now[0], right_now[0], preferred_element_type=jnp.float32)
        tangent = tangent + jnp.dot(left_now[0], right_now[1], preferred_element_type=jnp.float32)
        tangent = tangent + jnp.dot(left_now[1], right_now[0], preferred_element_type=jnp.float32)
        return (square, tangent)

    def section_body(section, carry):
        left_now, right_now, square, tangent = carry
        square, tangent = accumulate(left_now, right_now, square, tangent)
        left_now = passed_along(left_now, "col", -1)
        right_now = passed_along(right_now, "row", -group)
        return (left_now, right_now, square, tangent)

    zeros = jnp.zeros((left_zero.shape[0], right_zero.shape[1]), jnp.float32)
    left, right, square, tangent = lax.fori_loop(
        0, n_col - 1, section_body, (left, right, zeros, zeros)
    )
    square, tangent = accumulate(left, right, square, tangent)
    x_square = masked(square, keep_mask).astype(jnp.bfloat16)
    x_tangent = masked(tangent, keep_mask).astype(jnp.bfloat16)
    return (x_square, x_tangent)


def solution(mesh):
    if mesh.shape["col"] == 2:
        body = functools.partial(per_device_pair, mesh.shape["row"])
    else:
        body = per_device
    return jax.shard_map(
        body,
        mesh=mesh,
        in_specs=(P("row", "col"),) * 9,
        out_specs=(P("row", "col"), P("row", "col")),
        check_vma=False,
    )
```
